128 devices in a mesh: gx: 8 (over z, x_lo), yt: 16 (over x_hi, y, core).
Axes of the slice: x: 4 (x_hi: 2, x_lo: 2; x = x_hi * 2 + x_lo), y: 4, z: 4, core: 2. Of those that a mesh axis runs over, the one named last changes fastest.
Arguments:
- voltage_old: float32 [4, 4096, 2048], P(None, 'gx', 'yt'), may hold values from -6 to 6
- storage: float32 [4, 4096, 2048], P(None, 'gx', 'yt'), may hold values from 0.5 to 4
- cond_x: float32 [4, 4096, 2048], P(None, 'gx', 'yt'), may hold values from 0.5 to 2
- cond_y: float32 [4, 4096, 2048], P(None, 'gx', 'yt'), may hold values from 0.5 to 2
- cond_via: float32 [3, 4096, 2048], P(None, 'gx', 'yt'), may hold values from 0.5 to 2
- bond_mask: int32 [4096, 2048], P('gx', 'yt'), may hold values from 0 to 1, as said below
- current_blocks: float32 [16384, 8, 128], P(('gx', 'yt')), may hold values from -6 to 6
- block_owner: int32 [16384, 1], P(('gx', 'yt')), may hold values from 0 to 127; in each aligned block of 128 rows (0 to 127, 128 to 255, ...) at most 2 rows name the same one
- block_slot: int32 [16384], P(('gx', 'yt')), may hold values from 0 to 63
Outputs:
- voltage_new: float32 [4, 4096, 2048], P(None, 'gx', 'yt')
- block_voltage: float32 [16384, 8, 128], P(('gx', 'yt'))
The draws below stay inside these ranges and needn't reach their ends.
Inputs may be any that keep to these rules, and one draw needn't show every extreme that they name: `block_owner`: among the 128 blocks of one device no owner is named more than 2 times; owner o is the tile at x index o // 16 and tier-y index o % 16. bond_mask(i, j) equals bond_mask(i, (j + 1024) mod 2048).
All inputs are finite; a program needn't handle non-finite values.
Results may differ from the reference program's by a relative error of at most 0.00011.
Values sent between devices are 32-bit elements; how exact they have to be, the bound alone decides.
No kernel may reach another device: no remote copies, remote signals or barrier semaphores. Data moves between devices by JAX's collectives and lax.ppermute only.
A program may use at most 128 MiB of HBM per device.

```python
import math
import jax
import jax.numpy as jnp
import numpy as np

L = 4
CY = 128
BX = 8
SWEEPS = 3
CAP = 2
SLOTS = 64
NB = 128
BLOCKS = 16384
NX = 4096
NYU = 2048
N_GX = 8
N_YT = 16
DEVICES = 128


def draw_bond_mask(key, part):
    halves = jax.random.randint(key, (NX, NYU // 2), 0, 4)
    tier_half = (halves == 0).astype(jnp.int32)
    return jnp.concatenate([tier_half, tier_half], 1)


def place_ends(array, stream_key, least, largest):
    place = [jax.random.randint(jax.random.fold_in(stream_key, axis), (), 0, length) for axis, length in enumerate(array.shape)]
    longest = array.shape.index(max(array.shape))
    next_to = place[:longest] + [(place[longest] + 1) % array.shape[longest]] + place[longest + 1:]
    return array.at[tuple(place)].set(least).at[tuple(next_to)].set(largest)


def level_of(stream_key, shape, split, low, largest):
    def one(dim, shards_of):
        steps = jax.random.uniform(jax.random.fold_in(jax.random.fold_in(stream_key, 6), dim), (shards_of,), jnp.float32, low / len(split), largest / len(split))
        return jnp.repeat(jnp.exp(steps), shape[dim] // shards_of).reshape((-1,) + (1,) * (len(shape) - dim - 1))

    factor_of = one(*split[0])
    for cut in split[1:]:
        factor_of = factor_of * one(*cut)
    return factor_of


def assign_block(key, own, number, rows, number_of, top, reach, slope):
    ranking = jax.random.permutation(key, number_of)
    crowded, usual = shares(number_of, rows * top, reach, slope, True), shares(number_of, rows * top, reach, slope, False)
    places = jnp.arange(number_of)

    def named(lengths, turn):
        used = int((lengths > 0).sum())
        fixed = max(1, used // 4)
        moved = fixed + (places - fixed + turn * (used - fixed)) % max(1, number_of - fixed)
        return jnp.zeros((number_of,), jnp.int32).at[ranking[jnp.where(places < fixed, places, moved)]].set(jnp.asarray(lengths, jnp.int32))

    lengths = jnp.where(number % 4 == 0, named(crowded, number // 4), named(usual, number - number // 4 - 1))
    mixed = jax.random.permutation(jax.random.fold_in(own, 3), number_of)
    source_of, receiver = mixed[0:number_of // 2 * 2:2], mixed[1:number_of // 2 * 2:2]
    room = jnp.minimum(lengths[source_of] - 1, reach - lengths[receiver]) // 2
    room = jnp.where((source_of == ranking[0]) | (receiver == ranking[0]) | (lengths[receiver] == 0), 0, jnp.maximum(room, 0))
    moved = jax.random.randint(jax.random.fold_in(own, 4), (number_of // 2,), 0, 1 << 20) % (room + 1)
    lengths = lengths.at[source_of].add(-moved).at[receiver].add(moved)
    members = jnp.searchsorted(jnp.cumsum(lengths), jnp.arange(rows * top), side="right").astype(jnp.int32)
    grid = members.reshape(top, rows).T
    grid = grid[jax.random.permutation(jax.random.fold_in(own, 1), rows)]
    turn = jax.random.randint(jax.random.fold_in(own, 2), (rows, 1), 0, top)
    return jnp.take_along_axis(grid, (jnp.arange(top)[None, :] + turn) % top, axis=1)


def shares(number_of, total, bound, skew, full):
    weights = [(1 << 20) // math.isqrt(rank ** skew) + 1 for rank in range(1, number_of + 1)]
    largest = bound if full else min(bound, max(-(-total // number_of), total * weights[0] // sum(weights)))
    least = 1 if total - largest >= number_of - 1 else 0
    counts, surplus = [largest] + [least] * (number_of - 1), total - largest - least * (number_of - 1)
    while surplus > 0:
        candidates = [i for i in range(1, number_of) if counts[i] < largest] or [i for i in range(1, number_of) if counts[i] < bound]
        mass, budget = sum([weights[i] for i in candidates]), surplus
        for i in candidates:
            addition = min(bound - counts[i], max(1, budget * weights[i] // mass), surplus)
            counts[i] = counts[i] + addition
            surplus = surplus - addition
    return np.array(counts)


def noise(rng, dims, spread, most, pieces=(), held_as=jnp.bfloat16):
    result = spread * jax.random.normal(rng, dims, jnp.float32)
    if pieces:
        result = result * level_of(rng, dims, pieces, -0.22, 0.18)
    return jnp.clip(result, -most, most).astype(held_as)


def setup_inputs(seed: int = 0) -> dict:
    streams_of = jax.random.split(jax.random.key(seed), 10)
    voltage_old = noise(streams_of[0], (L, NX, NYU), 1.0, 6.0, ((1, 8), (2, 16)), jnp.float32)
    storage = jnp.clip(jnp.exp(math.log(4.0) - 2.0794415 * jax.random.uniform(streams_of[1], (L, NX, NYU), jnp.float32) ** level_of(streams_of[1], (L, NX, NYU), ((1, 8), (2, 16)), -0.2, 0.2)), 0.5, 4.0)
    cond_x = jnp.clip(jnp.exp(math.log(2.0) - 1.3862944 * jax.random.uniform(streams_of[2], (L, NX, NYU), jnp.float32) ** level_of(streams_of[2], (L, NX, NYU), ((1, 8), (2, 16)), -0.2, 0.2)), 0.5, 2.0)
    cond_y = jnp.clip(jnp.exp(math.log(2.0) - 1.3862944 * jax.random.uniform(streams_of[3], (L, NX, NYU), jnp.float32) ** level_of(streams_of[3], (L, NX, NYU), ((1, 8), (2, 16)), -0.2, 0.2)), 0.5, 2.0)
    cond_via = jnp.clip(jnp.exp(math.log(2.0) - 1.3862944 * jax.random.uniform(streams_of[4], (L - 1, NX, NYU), jnp.float32) ** level_of(streams_of[4], (L - 1, NX, NYU), ((1, 8), (2, 16)), -0.2, 0.2)), 0.5, 2.0)
    bond_mask = draw_bond_mask(jax.random.fold_in(streams_of[9], 71), 0)
    current_blocks = noise(streams_of[6], (BLOCKS, BX, CY), 1.0, 6.0, ((0, 128),), jnp.float32)
    block_owner_keys = jax.random.split(jax.random.fold_in(streams_of[7], 1), BLOCKS // NB)
    block_owner_turns = jax.random.permutation(jax.random.fold_in(streams_of[7], 3), BLOCKS // NB)
    block_owner = jax.vmap(lambda own, number: assign_block(jax.random.fold_in(streams_of[7], 2), own, number, NB, DEVICES, 1, CAP, 2))(block_owner_keys, block_owner_turns).reshape((BLOCKS, 1))
    block_slot = place_ends(jax.random.randint(streams_of[8], (BLOCKS,), 0, SLOTS), jax.random.fold_in(streams_of[8], 1), 0, SLOTS - 1).astype(jnp.int32)
    return {"voltage_old": voltage_old, "storage": storage, "cond_x": cond_x, "cond_y": cond_y, "cond_via": cond_via, "bond_mask": bond_mask, "current_blocks": current_blocks, "block_owner": block_owner, "block_slot": block_slot}


bond_conductance = 2.0
cheb_center = 1.0
cheb_halfwidth = 0.97


def link_values(cond_x, cond_y):
    columns = cond_y.shape[2]
    links_x = 0.5 * (cond_x[:, :-1, :] + cond_x[:, 1:, :])
    links_y = 0.5 * (cond_y + jnp.roll(cond_y, -1, axis=2))
    shifted = (jnp.arange(columns) + 1) % columns
    seam = CY // 2
    tier_cut = ((shifted != seam) & (shifted != seam + columns // 2)).astype(jnp.float32)
    return links_x, links_y * tier_cut


def neighbours(field_in, links_x, links_y, cond_via, bond_weight):
    zero_row = jnp.zeros_like(field_in[:, :1, :])
    zero_layer = jnp.zeros_like(field_in[:1])
    summed = jnp.concatenate([links_x * field_in[:, 1:, :], zero_row], 1) + jnp.concatenate([zero_row, links_x * field_in[:, :-1, :]], 1)
    summed = summed + links_y * jnp.roll(field_in, -1, axis=2) + jnp.roll(links_y * field_in, 1, axis=2)
    summed = summed + jnp.concatenate([cond_via * field_in[1:], zero_layer], 0) + jnp.concatenate([zero_layer, cond_via * field_in[:-1]], 0)
    top_layer = field_in[-1]
    half_cols = top_layer.shape[1] // 2
    partner = jnp.concatenate([top_layer[:, half_cols:], top_layer[:, :half_cols]], 1)
    return summed.at[-1].add(bond_weight * partner)


def reference(voltage_old, storage, cond_x, cond_y, cond_via, bond_mask, current_blocks, block_owner, block_slot):
    bond_weight = bond_conductance * bond_mask.astype(jnp.float32)
    links_x, links_y = link_values(cond_x, cond_y)

    def off_part(field_in):
        return neighbours(field_in, links_x, links_y, cond_via, bond_weight)

    diagonal = storage + off_part(jnp.ones_like(voltage_old))
    strip_id = (block_owner[:, 0] * SLOTS + block_slot).astype(jnp.int32)
    strips = jax.ops.segment_sum(current_blocks, strip_id, num_segments=N_GX * N_YT * SLOTS)
    current_map = strips.reshape(N_GX, N_YT, SLOTS, BX, CY).transpose(0, 2, 3, 1, 4).reshape(NX, NYU)
    right_side = (storage * voltage_old).at[0].add(current_map)
    field_now = voltage_old
    residual = right_side - (diagonal * field_now - off_part(field_now))
    sigma_ratio = cheb_center / cheb_halfwidth
    rho_now = 1.0 / sigma_ratio
    direction = residual / (cheb_center * diagonal)
    for sweep_index in range(SWEEPS):
        field_now = field_now + direction
        residual = residual - (diagonal * direction - off_part(direction))
        rho_next = 1.0 / (2.0 * sigma_ratio - rho_now)
        direction = rho_next * rho_now * direction + (2.0 * rho_next / cheb_halfwidth) * residual / diagonal
        rho_now = rho_next
    field_now = field_now + direction
    volt_strips = field_now[0].reshape(N_GX, SLOTS, BX, N_YT, CY).transpose(0, 3, 1, 2, 4).reshape(N_GX * N_YT * SLOTS, BX, CY)
    block_voltage = volt_strips[strip_id]
    return field_now, block_voltage
```

```python
import functools

import jax
import jax.numpy as jnp
from jax import lax
from jax.experimental import pallas as pl
from jax.experimental.pallas import tpu as pltpu
from jax.sharding import PartitionSpec as P

CAP = 2
BOND = 2.0
CENTER = 1.0
HALFWIDTH = 0.97
SIGMA = CENTER / HALFWIDTH
RHO0 = 1.0 / SIGMA
RHO1 = 1.0 / (2.0 * SIGMA - RHO0)
RHO2 = 1.0 / (2.0 * SIGMA - RHO1)
RHO3 = 1.0 / (2.0 * SIGMA - RHO2)
A1, B1 = RHO1 * RHO0, 2.0 * RHO1 / HALFWIDTH
A2, B2 = RHO2 * RHO1, 2.0 * RHO2 / HALFWIDTH
A3, B3 = RHO3 * RHO2, 2.0 * RHO3 / HALFWIDTH

ALL = ("gx", "yt")
F32 = jnp.float32
W = 128
H = 8
PAD = 16
Q = 4
STEP = 16
ROWS_MSG = CAP * 8 + 1


def full(ndim):
    return lambda *_: (0,) * ndim


def call(kernel, out, args, scratch=(), specs=None, out_specs=None, vmem=40, cost=1_000_000):
    specs = specs or {}
    in_specs = [
        specs.get(i, pl.BlockSpec(memory_space=pltpu.VMEM)) for i in range(len(args))
    ]
    many = isinstance(out, (list, tuple))
    outs = list(out) if many else [out]
    o_specs = out_specs or [pl.BlockSpec(memory_space=pltpu.VMEM)] * len(outs)
    return pl.pallas_call(
        kernel,
        out_shape=outs if many else outs[0],
        in_specs=in_specs,
        out_specs=o_specs if many else o_specs[0],
        scratch_shapes=list(scratch),
        compiler_params=pltpu.CompilerParams(vmem_limit_bytes=vmem << 20),
        cost_estimate=pl.CostEstimate(flops=cost, bytes_accessed=cost, transcendentals=0),
    )(*args)


def shape(*dims):
    return jax.ShapeDtypeStruct(dims, F32)


SMEM = pl.BlockSpec(memory_space=pltpu.SMEM)


def from_right(x):
    return pltpu.roll(x, x.shape[-1] - 1, axis=1)


def from_left(x):
    return pltpu.roll(x, 1, axis=1)


def lanes(rows, width=W):
    return lax.broadcasted_iota(jnp.int32, (rows, width), 1)


def each_chunk(first, count, body, step=STEP):
    @pl.loop(0, count)
    def _(k):
        body(pl.multiple_of(first + k * step, 8))


def send_kernel(owner_ref, slot_ref, blocks_ref, out_ref, dest_ref, count_ref, buf, slots):
    devices = count_ref.shape[0]

    @pl.loop(0, devices, unroll=8)
    def _(o):
        count_ref[o] = 0

    buf[...] = jnp.zeros_like(buf)
    slots[...] = jnp.full(slots.shape, 64, jnp.int32)
    lane = lanes(1)

    @pl.loop(0, blocks_ref.shape[0], unroll=4)
    def _(k):
        owner = owner_ref[k]
        rank = count_ref[owner]
        count_ref[owner] = rank + 1
        dest = owner * CAP + rank
        dest_ref[k] = dest
        buf[pl.ds(pl.multiple_of(dest * 8, 8), 8), :] = blocks_ref[k]
        row = slots[pl.ds(owner, 1), :]
        slots[pl.ds(owner, 1), :] = jnp.where(lane == rank, slot_ref[k], row)

    @pl.loop(0, devices // 8)
    def _(g):
        data = buf[pl.ds(pl.multiple_of(g * CAP * 64, 8), CAP * 64), :]
        label = slots[pl.ds(pl.multiple_of(g * 8, 8), 8), :].astype(F32)
        pieces = []
        for j in range(8):
            pieces += [data[CAP * 8 * j : CAP * 8 * (j + 1)], label[j : j + 1]]
        out_ref[pl.ds(pl.multiple_of(g * ROWS_MSG * 8, 8), ROWS_MSG * 8), :] = (
            jnp.concatenate(pieces, axis=0)
        )


def pack_x_kernel(*refs):
    firsts, lasts, v3, mid = refs[:6], refs[6:12], refs[12], refs[13:]
    first_out, last_out, v3_out = mid
    for group, out in ((firsts, first_out), (lasts, last_out)):
        p = 0
        for ref in group[:5]:
            n = ref.shape[0]
            out[p : p + n] = ref[...]
            p += n
        out[p] = BOND * group[5][...].astype(F32)
    v3_out[...] = v3[0]


def pack_y_kernel(v, cx, cy, st, via, mask, vp, lo, hi, vph, to_left, to_right):
    rows = v.shape[1]

    def pack(planes, at, n):
        lane = lanes(n)
        left = jnp.zeros((n, W), F32)
        right = jnp.zeros((n, W), F32)
        for p, x in enumerate(planes):
            here = (lane >= Q * p) & (lane < Q * p + Q)
            left = jnp.where(here, x if p == 0 else pltpu.roll(x, Q * p, axis=1), left)
            right = jnp.where(here, pltpu.roll(x, (Q * p + Q) % W, axis=1), right)
        to_left[pl.ds(at, n), :] = left
        to_right[pl.ds(at, n), :] = right

    def tile(i):
        at = pl.ds(i, STEP)
        planes = [ref[l, at, :] for ref in (v, cx, cy, st, via) for l in range(ref.shape[0])]
        planes += [BOND * mask[at, :].astype(F32), vp[at, :]]
        pack(planes, pl.multiple_of(i + H, 8), STEP)

    each_chunk(0, rows // STEP, tile)
    count = lo.shape[0]
    pack([lo[p] for p in range(count)] + [vph[0:H, :]], 0, H)
    pack([hi[p] for p in range(count)] + [vph[H : 2 * H, :]], H + rows, H)


def transpose_side(u_ref, out, at, rows):
    for j in range(u_ref.shape[1] // W):
        n = min(W, rows - W * j)
        block = u_ref[:, W * j : W * j + W].T
        out(at + W * j, n, block[:n])


def weighted(x, s, n, gx, gy, l_g):
    low = pl.multiple_of(s - 8, 8)
    near = x(low, n + 16)
    gnear = gx(l_g, low, n + 8)
    c = near[8 : 8 + n]
    g = gy(l_g, s, n)
    up = gnear[8 : 8 + n] * near[9 : 9 + n]
    down = (gnear * near[0 : n + 8])[7 : 7 + n]
    return up + down + g * from_right(c) + from_left(g * c)


def at(ref, l=None):
    if l is None:
        return lambda s, n: ref[pl.ds(s, n), :]
    return lambda s, n: ref[l, pl.ds(s, n), :]


def planes(ref):
    return lambda l, s, n: ref[l, pl.ds(s, n), :]


def base_kernel(
    place, v, cx, cy, st, via, mask, vp, lo, hi, vph, f_left, f_right,
    gx, gy, inv, viae, bond, d0, d1, z1, d2, z2, sb0, vd0, msg,
    ev, ecx, ecy, est, evp, side,
):
    rows = v.shape[1]
    total = rows + 2 * H
    layers = v.shape[0]
    dests = (
        [(ev, l) for l in range(layers)]
        + [(ecx, l) for l in range(layers)]
        + [(ecy, l) for l in range(layers)]
        + [(est, l) for l in range(layers)]
        + [(viae, l) for l in range(layers - 1)]
        + [(bond, None), (evp, None)]
    )

    def put(dest, s, n, cols, x):
        ref, l = dest
        if l is None:
            ref[pl.ds(s, n), cols] = x
        else:
            ref[l, pl.ds(s, n), cols] = x

    main, edge = slice(0, W), slice(W, 2 * W)

    def sides(s, n):
        r = pl.multiple_of(s - H, 8)
        a = f_right[pl.ds(r, n), :]
        b = f_left[pl.ds(r, n), :]
        low = lanes(n) < W // 2
        for p, dest in enumerate(dests):
            x = a if p == 0 else pltpu.roll(a, W - Q * p, axis=1)
            y = pltpu.roll(b, W - Q - Q * p, axis=1)
            put(dest, s, n, edge, jnp.where(low, x, y))

    each_chunk(H, total // STEP, lambda s: sides(s, STEP))

    def tile(i):
        a = pl.ds(i, STEP)
        xs = [ref[l, a, :] for ref in (v, cx, cy, st, via) for l in range(ref.shape[0])]
        xs += [BOND * mask[a, :].astype(F32), vp[a, :]]
        for x, dest in zip(xs, dests):
            put(dest, pl.multiple_of(i + PAD, 8), STEP, main, x)

    each_chunk(0, rows // STEP, tile)
    for p, dest in enumerate(dests):
        is_vp = p == len(dests) - 1
        put(dest, H, H, main, vph[0:H, :] if is_vp else lo[p])
        put(dest, PAD + rows, H, main, vph[H : 2 * H, :] if is_vp else hi[p])

    x_first, x_total, y_first, y_total = place[0], place[1], place[2], place[3]
    col = lanes(1, 2 * W)
    col = y_first + jnp.where(col < W + W // 2, col, col - 2 * W)
    nxt = lax.rem(col + 1 + y_total, y_total)
    seam = W // 2
    keep_y = jnp.where((nxt != seam) & (nxt != seam + y_total // 2), 0.5, 0.0).astype(F32)

    def conductances(s):
        row = x_first + s - PAD + lax.broadcasted_iota(jnp.int32, (STEP, 1), 0)
        keep_x = jnp.where((row != -1) & (row != x_total - 1), 0.5, 0.0).astype(F32)
        for l in range(layers):
            c = ecx[l, pl.ds(s, STEP + 8), :]
            gx[l, pl.ds(s, STEP), :] = keep_x * (c[0:STEP] + c[1 : STEP + 1])
            c = ecy[l, pl.ds(s, STEP), :]
            gy[l, pl.ds(s, STEP), :] = keep_y * (c + from_right(c))

    each_chunk(H, total // STEP, conductances)

    pgx, pgy = planes(gx), planes(gy)

    def start(s):
        n = STEP
        a = pl.ds(s, n)
        for l in range(layers):
            near = gx[l, pl.ds(pl.multiple_of(s - 8, 8), n + 8), :]
            up, down, right = near[8 : 8 + n], near[7 : 7 + n], gy[l, a, :]
            off = up + down + right + from_left(right)
            nb = weighted(at(ev, l), s, n, pgx, pgy, l)
            if l < layers - 1:
                off = off + viae[l, a, :]
                nb = nb + viae[l, a, :] * ev[l + 1, a, :]
            else:
                off = off + bond[a, :]
                nb = nb + bond[a, :] * evp[a, :]
            if l > 0:
                off = off + viae[l - 1, a, :]
                nb = nb + viae[l - 1, a, :] * ev[l - 1, a, :]
            c = ev[l, a, :]
            inverse = 1.0 / (est[l, a, :] + off)
            inv[l, a, :] = inverse
            d0[l, a, :] = (nb - off * c) * inverse

    each_chunk(H, total // STEP, start)

    def links(d, l, s, n, top=layers):
        nb = weighted(at(d, l), s, n, pgx, pgy, l)
        if l < layers - 1:
            nb = nb + viae[l, pl.ds(s, n), :] * d[l + 1, pl.ds(s, n), :]
        if l > 0:
            nb = nb + viae[l - 1, pl.ds(s, n), :] * d[l - 1, pl.ds(s, n), :]
        return inv[l, pl.ds(s, n), :] * nb

    def first(s):
        a = pl.ds(s, STEP)
        side[pl.ds(s - H, STEP), :] = d0[layers - 1, a, edge]
        msg[pl.ds(s - H, STEP), :] = d0[layers - 1, a, main]
        for l in range(layers - 1):
            z = links(d0, l, s, STEP)
            z1[l, a, :] = z
            d1[l, a, :] = A1 * d0[l, a, :] + B1 * z

    each_chunk(H, total // STEP, first)
    pack_side(side, msg, total)

    def second(s):
        a = pl.ds(s, STEP)
        for l in range(2):
            z = z1[l, a, :] - d1[l, a, :] + links(d1, l, s, STEP)
            z2[l, a, :] = z
            d2[l, a, :] = A2 * d1[l, a, :] + B2 * z

    each_chunk(H, total // STEP, second)

    def third(s):
        a = pl.ds(s, STEP)
        o = pl.ds(pl.multiple_of(s - PAD, 8), STEP)
        nb = weighted(at(d2, 0), s, STEP, pgx, pgy, 0)[:, main]
        nb = inv[0, a, main] * (nb + viae[0, a, main] * d2[1, a, main])
        d = d2[0, a, main]
        z = z2[0, a, main] - d + nb
        sb0[o, :] = v[0, o, :] + d0[0, a, main] + d1[0, a, main] + (1.0 + A3) * d + B3 * z
        for l in range(1, layers):
            vd0[l - 1, o, :] = v[l, o, :] + d0[l, a, main]

    each_chunk(PAD, rows // STEP, third)


def pack_side(side, msg, total):
    for j in range(-(-total // W)):
        t = side[W * j : W * j + W, :].T
        msg[total + 8 * j : total + 8 * j + Q, :] = t[0:Q]
        msg[total + 8 * j + Q : total + 8 * j + 2 * Q, :] = t[W - Q : W]


def unpack_side(msg, total, u, ref):
    u[...] = jnp.zeros_like(u)
    for j in range(-(-total // W)):
        u[0:Q, :] = msg[total + 8 * j : total + 8 * j + Q, :]
        u[W - Q : W, :] = msg[total + 8 * j + Q : total + 8 * j + 2 * Q, :]
        n = min(W, total - W * j)
        t = u[...].T
        ref[H + W * j : H + W * j + n, W : 2 * W] = t[:n]


def mid_kernel(d0, part, gx, gy, inv, viae, bond, d1, z1, msg, ep, side, u):
    top = gx.shape[0] - 1
    total = part.shape[0] - 8 * (u.shape[1] * 5 // W)
    unpack_side(part, total, u, ep)

    def body(s):
        a = pl.ds(s, STEP)
        r = pl.ds(pl.multiple_of(s - H, 8), STEP)
        other = jnp.concatenate([part[r, :], ep[a, W : 2 * W]], axis=1)
        nb = weighted(at(d0, top), s, STEP, planes(gx), planes(gy), top)
        nb = nb + viae[top - 1, a, :] * d0[top - 1, a, :] + bond[a, :] * other
        z = inv[top, a, :] * nb
        d = A1 * d0[top, a, :] + B1 * z
        z1[a, :] = z
        d1[a, :] = d
        side[r, :] = d[:, W:]
        msg[r, :] = d[:, :W]

    each_chunk(H, total // STEP, body)
    pack_side(side, msg, total)


def late_kernel(
    d1, e11, z1, d13, z13, part, gx, gy, inv, viae, bond,
    d22, d23, z22, z23, msg, ep, u,
):
    top = gx.shape[0] - 1
    total = part.shape[0] - 8 * (u.shape[1] * 5 // W)
    unpack_side(part, total, u, ep)

    def body(s):
        a = pl.ds(s, STEP)
        r = pl.ds(pl.multiple_of(s - H, 8), STEP)
        under = d1[top - 2, a, :] + e11[a, :]
        this, above = d1[top - 1, a, :], d13[a, :]
        nb = weighted(at(d1, top - 1), s, STEP, planes(gx), planes(gy), top - 1)
        nb = nb + viae[top - 2, a, :] * under + viae[top - 1, a, :] * above
        z = z1[top - 1, a, :] - this + inv[top - 1, a, :] * nb
        z22[a, :] = z
        d22[a, :] = A2 * this + B2 * z
        other = jnp.concatenate([part[r, :], ep[a, W : 2 * W]], axis=1)
        nb = weighted(at(d13), s, STEP, planes(gx), planes(gy), top)
        nb = nb + viae[top - 1, a, :] * this + bond[a, :] * other
        z = z13[a, :] - above + inv[top, a, :] * nb
        z23[a, :] = z
        d23[a, :] = A2 * above + B2 * z

    each_chunk(H, total // STEP, body)
    rows = msg.shape[0]
    msg[...] = d23[PAD : PAD + rows, 0:W]


def final_kernel(
    v0, vd0, d1, e11, d13, d20, d21, d22, d23, z21, z22, z23, part, gx, gy, inv, viae, bond, out
):
    main = slice(0, W)
    top = gx.shape[0] - 1

    def body(i):
        s = pl.multiple_of(i + PAD, 8)
        a, o = pl.ds(s, STEP), pl.ds(i, STEP)
        out[0, o, :] = v0[o, :]
        d2 = [None, d21, d22, d23]
        z2 = [None, z21, z22, z23]
        first = [None, d1[1, a, main] + e11[a, main], d1[2, a, main], d13[a, main]]
        below = d20[o, :]
        for l in range(1, top + 1):
            nb = weighted(at(d2[l]), s, STEP, planes(gx), planes(gy), l)[:, main]
            nb = nb + viae[l - 1, a, main] * below
            below = d2[l][a, main]
            if l < top:
                nb = nb + viae[l, a, main] * d2[l + 1][a, main]
            else:
                nb = nb + bond[a, main] * part[o, :]
            z = z2[l][a, main] - below + inv[l, a, main] * nb
            out[l, o, :] = vd0[l - 1, o, :] + first[l] + (1.0 + A3) * below + B3 * z

    each_chunk(0, out.shape[1] // STEP, body)


def map_kernel(arrived, out, first, last, labels, vec, lab, acc, sem):
    devices = vec.shape[0]
    rows = out.shape[0]
    vec[...] = arrived[pl.ds(CAP * 8, devices, stride=ROWS_MSG), :].astype(jnp.int32)
    copy = pltpu.make_async_copy(vec, lab, sem)
    copy.start()
    acc[...] = jnp.zeros_like(acc)
    copy.wait()

    @pl.loop(0, devices // 8)
    def _(g):
        n = ROWS_MSG * 8
        data = arrived[pl.ds(pl.multiple_of(g * n, 8), n), :]
        for j in range(8):
            for r in range(CAP):
                slot = lab[g * 8 + j, r]
                labels[(g * 8 + j) * CAP + r] = slot
                a = pl.ds(pl.multiple_of(slot * 8, 8), 8)
                acc[a, :] += data[j * ROWS_MSG + r * 8 : j * ROWS_MSG + r * 8 + 8]

    out[...] = acc[0:rows, :]
    first[...] = acc[0:8, :]
    last[...] = acc[rows - 8 : rows, :]


def edges_kernel(cur, lo, hi, to_left, to_right, ext):
    rows = cur.shape[0]
    ext[0:H, :] = lo[...]
    ext[H : H + rows, :] = cur[...]
    ext[H + rows : rows + 2 * H, :] = hi[...]
    for j in range(to_left.shape[1] // W):
        t = ext[W * j : W * j + W, :].T
        to_left[:, W * j : W * j + W] = t[0:8]
        to_right[:, W * j : W * j + W] = t[W - 8 : W]


def effect_kernel(
    labels, cur, lo, hi, f_left, f_right, gx, gy, inv, viae, sb0, d2, z2,
    v0, picked, e11, d20, d21, z21,
    ec, e0, e1, z10, z11, e2, z20, u, acc,
):
    rows = cur.shape[0]
    total = rows + 2 * H
    main, edge = slice(0, W), slice(W, 2 * W)
    ec[H : 2 * H, main] = lo[...]
    ec[PAD : PAD + rows, main] = cur[...]
    ec[PAD + rows : PAD + rows + H, main] = hi[...]
    u[...] = jnp.zeros_like(u)
    for j in range(f_left.shape[1] // W):
        u[0:8, :] = f_right[:, W * j : W * j + W]
        u[W - 8 : W, :] = f_left[:, W * j : W * j + W]
        n = min(W, total - W * j)
        ec[H + W * j : H + W * j + n, edge] = u[...].T[:n]
    pgx, pgy = planes(gx), planes(gy)

    def zeroth(s):
        a = pl.ds(s, STEP)
        e0[a, :] = inv[0, a, :] * ec[a, :]

    each_chunk(H, total // STEP, zeroth)

    def first(s):
        a = pl.ds(s, STEP)
        here = e0[a, :]
        z = inv[0, a, :] * weighted(at(e0), s, STEP, pgx, pgy, 0)
        z10[a, :] = z
        e1[a, :] = A1 * here + B1 * z
        z = inv[1, a, :] * viae[0, a, :] * here
        z11[a, :] = z
        e11[a, :] = B1 * z

    each_chunk(H, total // STEP, first)

    def second(s):
        a = pl.ds(s, STEP)
        low, high, between = e1[a, :], e11[a, :], viae[0, a, :]
        nb = weighted(at(e1), s, STEP, pgx, pgy, 0) + between * high
        z = z10[a, :] - low + inv[0, a, :] * nb
        z20[a, :] = z
        e2[a, :] = A2 * low + B2 * z
        nb = weighted(at(e11), s, STEP, pgx, pgy, 1) + between * low
        z = z11[a, :] - high + inv[1, a, :] * nb
        z21[a, :] = z2[1, a, :] + z
        d21[a, :] = d2[1, a, :] + A2 * high + B2 * z

    each_chunk(H, total // STEP, second)

    def third(i):
        s = pl.multiple_of(i + PAD, 8)
        a, o = pl.ds(s, STEP), pl.ds(i, STEP)
        here = e2[a, main]
        upper = d21[a, main] - d2[1, a, main]
        nb = weighted(at(e2), s, STEP, pgx, pgy, 0)[:, main] + viae[0, a, main] * upper
        z = z20[a, main] - here + inv[0, a, main] * nb
        whole = sb0[o, :] + e0[a, main] + e1[a, main] + (1.0 + A3) * here + B3 * z
        v0[o, :] = whole
        acc[o, :] = whole
        d20[o, :] = d2[0, a, main] + here

    each_chunk(0, rows // STEP, third)
    acc[rows : rows + 8, :] = jnp.zeros((8, W), F32)

    @pl.loop(0, labels.shape[0], unroll=8)
    def _(k):
        picked[pl.ds(pl.multiple_of(k * 8, 8), 8), :] = acc[
            pl.ds(pl.multiple_of(labels[k] * 8, 8), 8), :
        ]


def give_kernel(dest, back, out):
    @pl.loop(0, out.shape[0], unroll=8)
    def _(k):
        out[k] = back[pl.ds(pl.multiple_of(dest[k] * 8, 8), 8), :]


def ring(axis, step):
    n = lax.axis_size(axis)
    return [(i, (i + step) % n) for i in range(n)]


def shift(x, axis, step):
    return lax.ppermute(x, axis, ring(axis, step))


def facing(x):
    n = lax.axis_size("yt")
    return lax.ppermute(x, "yt", [(i, i ^ (n // 2)) for i in range(n)])


def on_device(v, st, cx, cy, via, mask, blocks, owner, slot):
    layers, rows, cols = v.shape
    devices = lax.axis_size("gx") * lax.axis_size("yt")
    nb = blocks.shape[0]
    total = rows + 2 * H
    nr = total + 2 * H
    side_blocks = -(-total // W)
    place = jnp.stack(
        [
            lax.axis_index("gx") * rows,
            jnp.int32(rows * lax.axis_size("gx")),
            lax.axis_index("yt") * cols,
            jnp.int32(cols * lax.axis_size("yt")),
        ]
    ).astype(jnp.int32)

    outgoing, dest = call(
        send_kernel,
        [shape(devices * ROWS_MSG, W), jax.ShapeDtypeStruct((nb,), jnp.int32)],
        [owner.reshape(nb), slot, blocks],
        scratch=[
            pltpu.SMEM((devices,), jnp.int32),
            pltpu.VMEM((devices * CAP * 8, W), F32),
            pltpu.VMEM((devices, W), jnp.int32),
        ],
        specs={0: SMEM, 1: SMEM},
        out_specs=[pl.BlockSpec(memory_space=pltpu.VMEM), SMEM],
    )
    arrived = lax.all_to_all(outgoing, ALL, 0, 0, tiled=True)

    sources = [v, cx, cy, st, via]
    args = sources + [mask] + sources + [mask, v]
    specs = {}
    last = rows // 8 - 1
    for i in range(5):
        n = sources[i].shape[0]
        specs[i] = pl.BlockSpec((n, 8, W), lambda _: (0, 0, 0))
        specs[6 + i] = pl.BlockSpec((n, 8, W), lambda _: (0, last, 0))
    specs[5] = pl.BlockSpec((8, W), lambda _: (0, 0))
    specs[11] = pl.BlockSpec((8, W), lambda _: (last, 0))
    specs[12] = pl.BlockSpec((1, rows, W), lambda _: (layers - 1, 0, 0))
    count = 5 * layers
    first_rows, last_rows, v_top = pl.pallas_call(
        pack_x_kernel,
        grid=(1,),
        out_shape=[shape(count, 8, W), shape(count, 8, W), shape(rows, W)],
        in_specs=[specs[i] for i in range(13)],
        out_specs=[
            pl.BlockSpec((count, 8, W), lambda _: (0, 0, 0)),
            pl.BlockSpec((count, 8, W), lambda _: (0, 0, 0)),
            pl.BlockSpec((rows, W), lambda _: (0, 0)),
        ],
        cost_estimate=pl.CostEstimate(flops=1, bytes_accessed=1_000_000, transcendentals=0),
    )(*args)
    lo = shift(last_rows, "gx", 1)
    hi = shift(first_rows, "gx", -1)
    v_part = facing(v_top)
    v_part_rims = facing(jnp.concatenate([lo[layers - 1], hi[layers - 1]], 0))
    tiles = [v, cx, cy, st, via, mask, v_part, lo, hi, v_part_rims]
    to_left, to_right = call(pack_y_kernel, [shape(total, W), shape(total, W)], tiles)
    f_left = shift(to_right, "yt", 1)
    f_right = shift(to_left, "yt", -1)

    ext = lambda n: shape(n, nr, 2 * W)
    one = shape(nr, 2 * W)
    buffer = lambda *d: pltpu.VMEM(d, F32)
    msg_shape = shape(total + 8 * side_blocks, W)
    gx, gy, inv, viae, bond, d0, d1, z1, d2, z2, sb0, vd0, msg0 = call(
        base_kernel,
        [ext(layers), ext(layers), ext(layers), ext(layers - 1), one, ext(layers), ext(3), ext(3),
         ext(2), ext(2), shape(rows, W), shape(layers - 1, rows, W), msg_shape],
        [place, *tiles, f_left, f_right],
        scratch=[buffer(layers, nr, 2 * W)] * 4
        + [buffer(nr, 2 * W), buffer(side_blocks * W, W)],
        specs={0: SMEM},
        vmem=56,
        cost=20_000_000,
    )
    part0 = facing(msg0)
    d13, z13, msg1 = call(
        mid_kernel,
        [one, one, msg_shape],
        [d0, part0, gx, gy, inv, viae, bond],
        scratch=[buffer(nr, 2 * W), buffer(side_blocks * W, W), buffer(W, W)],
    )
    part1 = facing(msg1)

    cur, cur_first, cur_last, labels = call(
        map_kernel,
        [shape(rows, W), shape(8, W), shape(8, W), jax.ShapeDtypeStruct((devices * CAP,), jnp.int32)],
        [arrived],
        scratch=[
            pltpu.VMEM((devices, W), jnp.int32),
            pltpu.SMEM((devices, W), jnp.int32),
            buffer(rows + 8, W),
            pltpu.SemaphoreType.DMA,
        ],
        out_specs=[pl.BlockSpec(memory_space=pltpu.VMEM)] * 3 + [SMEM],
    )
    cur_lo = shift(cur_last, "gx", 1)
    cur_hi = shift(cur_first, "gx", -1)
    cur_left, cur_right = call(
        edges_kernel,
        [shape(8, side_blocks * W)] * 2,
        [cur, cur_lo, cur_hi],
        scratch=[buffer(side_blocks * W, W)],
    )
    cur_f_left = shift(cur_right, "yt", 1)
    cur_f_right = shift(cur_left, "yt", -1)
    v0, picked, e11, d20, d21, z21 = call(
        effect_kernel,
        [shape(rows, W), shape(devices * CAP * 8, W), one, shape(rows, W), one, one],
        [labels, cur, cur_lo, cur_hi, cur_f_left, cur_f_right, gx, gy, inv, viae, sb0, d2, z2],
        scratch=[buffer(nr, 2 * W)] * 7 + [buffer(W, W), buffer(rows + 8, W)],
        specs={0: SMEM},
        vmem=56,
    )
    back = lax.all_to_all(picked, ALL, 0, 0, tiled=True)

    d22, d23, z22, z23, msg2 = call(
        late_kernel,
        [one, one, one, one, shape(rows, W)],
        [d1, e11, z1, d13, z13, part1, gx, gy, inv, viae, bond],
        scratch=[buffer(nr, 2 * W), buffer(W, W)],
        vmem=56,
        cost=10_000_000,
    )
    part2 = facing(msg2)
    voltage = call(
        final_kernel,
        shape(layers, rows, W),
        [v0, vd0, d1, e11, d13, d20, d21, d22, d23, z21, z22, z23, part2, gx, gy, inv, viae, bond],
        vmem=56,
        cost=10_000_000,
    )
    block_voltage = call(
        give_kernel, shape(nb, 8, W), [dest, back], specs={0: SMEM}
    )
    return voltage, block_voltage


def solution(mesh):
    tile = P(None, "gx", "yt")
    return jax.shard_map(
        on_device,
        mesh=mesh,
        in_specs=(tile, tile, tile, tile, tile, P("gx", "yt"), P(ALL, None, None), P(ALL, None), P(ALL)),
        out_specs=(tile, P(ALL, None, None)),
        check_vma=False,
    )
```

```python
import jax
import jax.numpy as jnp
from jax import lax
from jax.experimental import pallas as pl
from jax.experimental.pallas import tpu as pltpu
from jax.sharding import PartitionSpec as P

CAP = 2
BOND = 2.0
CENTER = 1.0
HALFWIDTH = 0.97
SIGMA = CENTER / HALFWIDTH
RHO0 = 1.0 / SIGMA
RHO1 = 1.0 / (2.0 * SIGMA - RHO0)
RHO2 = 1.0 / (2.0 * SIGMA - RHO1)
RHO3 = 1.0 / (2.0 * SIGMA - RHO2)
A1, B1 = RHO1 * RHO0, 2.0 * RHO1 / HALFWIDTH
A2, B2 = RHO2 * RHO1, 2.0 * RHO2 / HALFWIDTH
A3, B3 = RHO3 * RHO2, 2.0 * RHO3 / HALFWIDTH

VMEM_BASE, VMEM_TOP, VMEM_EFFECT, VMEM_FINAL = 58, 58, 58, 58

ALL = ("gx", "yt")
F32 = jnp.float32
W = 128
H = 8
PAD = 16
Q = 4
WIDE = 48
STEP = 64
ROWS_MSG = CAP * 8 + 1


def call(kernel, out, args, scratch=(), specs=None, out_specs=None, vmem=6, cost=1_000_000):
    specs = specs or {}
    in_specs = [
        specs.get(i, pl.BlockSpec(memory_space=pltpu.VMEM)) for i in range(len(args))
    ]
    many = isinstance(out, (list, tuple))
    outs = list(out) if many else [out]
    o_specs = out_specs or [pl.BlockSpec(memory_space=pltpu.VMEM)] * len(outs)
    return pl.pallas_call(
        kernel,
        out_shape=outs if many else outs[0],
        in_specs=in_specs,
        out_specs=o_specs if many else o_specs[0],
        scratch_shapes=list(scratch),
        name=kernel.__name__,
        compiler_params=pltpu.CompilerParams(vmem_limit_bytes=vmem << 20),
        cost_estimate=pl.CostEstimate(flops=cost, bytes_accessed=cost, transcendentals=0),
    )(*args)


def shape(*dims):
    return jax.ShapeDtypeStruct(dims, F32)


SMEM = pl.BlockSpec(memory_space=pltpu.SMEM)


def from_right(x):
    return pltpu.roll(x, x.shape[-1] - 1, axis=1)


def from_left(x):
    return pltpu.roll(x, 1, axis=1)


def lanes(rows, width=W):
    return lax.broadcasted_iota(jnp.int32, (rows, width), 1)


def each_chunk(first, rows, body, step):
    @pl.loop(0, rows // step)
    def _(k):
        body(pl.multiple_of(first + k * step, 8))


def send_kernel(owner_ref, slot_ref, blocks_ref, out_ref, dest_ref, count_ref, buf, slots):
    devices = count_ref.shape[0]

    @pl.loop(0, devices, unroll=8)
    def _(o):
        count_ref[o] = 0

    buf[...] = jnp.zeros_like(buf)
    slots[...] = jnp.full(slots.shape, 64, jnp.int32)
    lane = lanes(1)

    @pl.loop(0, blocks_ref.shape[0], unroll=4)
    def _(k):
        owner = owner_ref[k]
        rank = count_ref[owner]
        count_ref[owner] = rank + 1
        dest = owner * CAP + rank
        dest_ref[k] = dest
        buf[pl.ds(pl.multiple_of(dest * 8, 8), 8), :] = blocks_ref[k]
        row = slots[pl.ds(owner, 1), :]
        slots[pl.ds(owner, 1), :] = jnp.where(lane == rank, slot_ref[k], row)

    @pl.loop(0, devices // 8)
    def _(g):
        data = buf[pl.ds(pl.multiple_of(g * CAP * 64, 8), CAP * 64), :]
        label = slots[pl.ds(pl.multiple_of(g * 8, 8), 8), :].astype(F32)
        pieces = []
        for j in range(8):
            pieces += [data[CAP * 8 * j : CAP * 8 * (j + 1)], label[j : j + 1]]
        out_ref[pl.ds(pl.multiple_of(g * ROWS_MSG * 8, 8), ROWS_MSG * 8), :] = (
            jnp.concatenate(pieces, axis=0)
        )


def pack_x_kernel(*refs):
    firsts, lasts, v3 = refs[:6], refs[6:12], refs[12]
    first_out, last_out, v3_out, v3_first, v3_last = refs[13:]
    for group, out in ((firsts, first_out), (lasts, last_out)):
        p = 0
        for ref in group[:5]:
            n = ref.shape[0]
            out[p : p + n] = ref[...]
            p += n
        out[p] = BOND * group[5][...].astype(F32)
    rows = v3.shape[1]
    v3_out[...] = v3[0]
    v3_first[...] = v3[0, 0:H, :]
    v3_last[...] = v3[0, rows - H : rows, :]


def pack_y_kernel(v, cx, cy, st, via, mask, vp, lo, hi, vlo, vhi, to_left, to_right):
    rows = v.shape[1]

    def pack(planes, at, n):
        lane = lanes(n)
        left = jnp.zeros((n, W), F32)
        right = jnp.zeros((n, W), F32)
        for p, x in enumerate(planes):
            here = (lane >= Q * p) & (lane < Q * p + Q)
            left = jnp.where(here, x if p == 0 else pltpu.roll(x, Q * p, axis=1), left)
            right = jnp.where(here, pltpu.roll(x, (Q * p + Q) % W, axis=1), right)
        to_left[pl.ds(at, n), :] = left
        to_right[pl.ds(at, n), :] = right

    def tile(i):
        at = pl.ds(i, STEP)
        planes = [ref[l, at, :] for ref in (v, cx, cy, st, via) for l in range(ref.shape[0])]
        planes += [BOND * mask[at, :].astype(F32), vp[at, :]]
        pack(planes, pl.multiple_of(i + H, 8), STEP)

    each_chunk(0, rows, tile, STEP)
    count = lo.shape[0]
    pack([lo[p] for p in range(count)] + [vlo[...]], 0, H)
    pack([hi[p] for p in range(count)] + [vhi[...]], H + rows, H)


def rows_of(ref, l=None):
    if l is None:
        return lambda s, n: ref[pl.ds(s, n), :]
    return lambda s, n: ref[l, pl.ds(s, n), :]


def weighted(x, s, n, gx, gy):
    low = pl.multiple_of(s - 8, 8)
    near = rows_of(x)(low, n + 16)
    gnear = rows_of(gx)(low, n + 8)
    c = near[8 : 8 + n]
    g = rows_of(gy)(s, n)
    up = gnear[8 : 8 + n] * near[9 : 9 + n]
    down = (gnear * near[0 : n + 8])[7 : 7 + n]
    return up + down + g * from_right(c) + from_left(g * c)


def base_kernel(*refs):
    place, v, cx, cy, st, via, mask, vp, lo, hi, vlo, vhi, f_left, f_right = refs[:14]
    refs = list(refs[14:])
    layers, rows = v.shape[0], v.shape[1]
    total = rows + 2 * H

    def take(n):
        got = refs[:n]
        del refs[:n]
        return got

    gx, gy, inv, viae = take(layers), take(layers), take(layers), take(layers - 1)
    bond, d02, d03, d11, d12, z12, d20, d21, z21, sb0, vd0, msg = take(12)
    ev, ecx, ecy, est = take(layers), take(layers), take(layers), take(layers)
    evp, side, d00, d01, d10, z10, z11, z20, e20 = take(9)
    d0 = [d00, d01, d02, d03]
    d1, z1 = [d10, d11, d12], [z10, z11, z12]
    d2, z2 = [e20, d21], [z20, z21]
    dests = [*ev, *ecx, *ecy, *est, *viae, bond, evp]
    main, edge = slice(0, W), slice(W, 2 * W)

    def sides(s):
        r = pl.multiple_of(s - H, 8)
        a = f_right[pl.ds(r, WIDE), :]
        b = f_left[pl.ds(r, WIDE), :]
        low = lanes(WIDE) < W // 2
        for p, dest in enumerate(dests):
            x = a if p == 0 else pltpu.roll(a, W - Q * p, axis=1)
            y = pltpu.roll(b, W - Q - Q * p, axis=1)
            dest[pl.ds(s, WIDE), edge] = jnp.where(low, x, y)

    each_chunk(H, total, sides, WIDE)

    def tile(i):
        a = pl.ds(i, STEP)
        xs = [ref[l, a, :] for ref in (v, cx, cy, st, via) for l in range(ref.shape[0])]
        xs += [BOND * mask[a, :].astype(F32), vp[a, :]]
        for x, dest in zip(xs, dests):
            dest[pl.ds(pl.multiple_of(i + PAD, 8), STEP), main] = x

    each_chunk(0, rows, tile, STEP)
    for p, dest in enumerate(dests):
        is_vp = p == len(dests) - 1
        dest[H : 2 * H, main] = vlo[...] if is_vp else lo[p]
        dest[PAD + rows : PAD + rows + H, main] = vhi[...] if is_vp else hi[p]

    x_first, x_total, y_first, y_total = place[0], place[1], place[2], place[3]
    col = lanes(1, 2 * W)
    col = y_first + jnp.where(col < W + W // 2, col, col - 2 * W)
    nxt = lax.rem(col + 1 + y_total, y_total)
    seam = W // 2
    keep_y = jnp.where((nxt != seam) & (nxt != seam + y_total // 2), 0.5, 0.0).astype(F32)

    def conductances(s):
        row = x_first + s - PAD + lax.broadcasted_iota(jnp.int32, (WIDE, 1), 0)
        keep_x = jnp.where((row != -1) & (row != x_total - 1), 0.5, 0.0).astype(F32)
        for l in range(layers):
            c = ecx[l][pl.ds(s, WIDE + 8), :]
            gx[l][pl.ds(s, WIDE), :] = keep_x * (c[0:WIDE] + c[1 : WIDE + 1])
            c = ecy[l][pl.ds(s, WIDE), :]
            gy[l][pl.ds(s, WIDE), :] = keep_y * (c + from_right(c))

    each_chunk(H, total, conductances, WIDE)

    def start(s):
        n = WIDE
        a = pl.ds(s, n)
        for l in range(layers):
            near = gx[l][pl.ds(pl.multiple_of(s - 8, 8), n + 8), :]
            up, down, right = near[8 : 8 + n], near[7 : 7 + n], gy[l][a, :]
            off = up + down + right + from_left(right)
            nb = weighted(ev[l], s, n, gx[l], gy[l])
            if l < layers - 1:
                off = off + viae[l][a, :]
                nb = nb + viae[l][a, :] * ev[l + 1][a, :]
            else:
                off = off + bond[a, :]
                nb = nb + bond[a, :] * evp[a, :]
            if l > 0:
                off = off + viae[l - 1][a, :]
                nb = nb + viae[l - 1][a, :] * ev[l - 1][a, :]
            c = ev[l][a, :]
            inverse = 1.0 / (est[l][a, :] + off)
            inv[l][a, :] = inverse
            d0[l][a, :] = (nb - off * c) * inverse

    each_chunk(H, total, start, WIDE)

    def links(d, l, s, n):
        nb = weighted(d[l], s, n, gx[l], gy[l])
        if l < layers - 1:
            nb = nb + viae[l][pl.ds(s, n), :] * d[l + 1][pl.ds(s, n), :]
        if l > 0:
            nb = nb + viae[l - 1][pl.ds(s, n), :] * d[l - 1][pl.ds(s, n), :]
        return inv[l][pl.ds(s, n), :] * nb

    def first(s):
        a = pl.ds(s, WIDE)
        r = pl.ds(pl.multiple_of(s - H, 8), WIDE)
        side[r, :] = d03[a, edge]
        msg[r, :] = d03[a, main]
        for l in range(layers - 1):
            z = links(d0, l, s, WIDE)
            z1[l][a, :] = z
            d1[l][a, :] = A1 * d0[l][a, :] + B1 * z

    each_chunk(H, total, first, WIDE)
    pack_side(side, msg, total)

    def second(s):
        a = pl.ds(s, WIDE)
        for l in range(2):
            z = z1[l][a, :] - d1[l][a, :] + links(d1, l, s, WIDE)
            z2[l][a, :] = z
            d2[l][a, :] = A2 * d1[l][a, :] + B2 * z

    each_chunk(H, total, second, WIDE)

    def third(s):
        a = pl.ds(s, STEP)
        o = pl.ds(pl.multiple_of(s - PAD, 8), STEP)
        nb = weighted(e20, s, STEP, gx[0], gy[0])[:, main]
        nb = inv[0][a, main] * (nb + viae[0][a, main] * d21[a, main])
        d = e20[a, main]
        z = z20[a, main] - d + nb
        d20[o, :] = d
        sb0[o, :] = v[0, o, :] + d00[a, main] + d10[a, main] + (1.0 + A3) * d + B3 * z
        for l in range(1, layers):
            vd0[l - 1, o, :] = v[l, o, :] + d0[l][a, main]

    each_chunk(PAD, rows, third, STEP)


def pack_side(side, msg, total):
    for j in range(-(-total // W)):
        t = side[W * j : W * j + W, :].T
        msg[total + 8 * j : total + 8 * j + Q, :] = t[0:Q]
        msg[total + 8 * j + Q : total + 8 * j + 2 * Q, :] = t[W - Q : W]


def unpack_side(msg, total, u, ref):
    u[...] = jnp.zeros_like(u)
    for j in range(-(-total // W)):
        u[0:Q, :] = msg[total + 8 * j : total + 8 * j + Q, :]
        u[W - Q : W, :] = msg[total + 8 * j + Q : total + 8 * j + 2 * Q, :]
        n = min(W, total - W * j)
        t = u[...].T
        ref[H + W * j : H + W * j + n, W : 2 * W] = t[:n]


def top_kernel(low, here, z, part, gx, gy, inv, via, bond, *rest):
    again = z is not None
    if again:
        d_out, z_out, msg, weight, ep, side, u = rest
    else:
        d_out, z_out, msg, ep, side, u = rest
    total = part.shape[0] - 8 * (side.shape[0] // W)
    unpack_side(part, total, u, ep)

    def body(s):
        a = pl.ds(s, WIDE)
        r = pl.ds(pl.multiple_of(s - H, 8), WIDE)
        other = jnp.concatenate([part[r, :], ep[a, W : 2 * W]], axis=1)
        nb = weighted(here, s, WIDE, gx, gy) + via[a, :] * low[a, :] + bond[a, :] * other
        c = here[a, :]
        x = inv[a, :] * nb
        if again:
            x = z[a, :] - c + x
        d = (A2 if again else A1) * c + (B2 if again else B1) * x
        z_out[a, :] = x
        d_out[a, :] = d
        if not again:
            side[r, :] = d[:, W:]
            msg[r, :] = d[:, :W]

    each_chunk(H, total, body, WIDE)
    if not again:
        pack_side(side, msg, total)
    else:
        rows = msg.shape[0]
        msg[...] = d_out[PAD : PAD + rows, 0:W]
        weight[...] = inv[PAD : PAD + rows, 0:W] * bond[PAD : PAD + rows, 0:W]


def first_top_kernel(low, here, *rest):
    top_kernel(low, here, None, *rest)


def second_top_kernel(*refs):
    top_kernel(*refs)


def final_kernel(
    v0, vd0, d11, d12, z12, e11, d13, d20, d21, d23, z21, z23,
    gx1, gx2, gx3, gy1, gy2, gy3, inv1, inv2, inv3, via0, via1, via2,
    out, d22, z22,
):
    main = slice(0, W)
    rows = out.shape[1]

    def middle(s):
        a = pl.ds(s, WIDE)
        this = d12[a, :]
        nb = weighted(d12, s, WIDE, gx2, gy2)
        nb = nb + via1[a, :] * (d11[a, :] + e11[a, :]) + via2[a, :] * d13[a, :]
        z = z12[a, :] - this + inv2[a, :] * nb
        z22[a, :] = z
        d22[a, :] = A2 * this + B2 * z

    each_chunk(H, rows + 2 * H, middle, WIDE)
    gx, gy, inv = [None, gx1, gx2, gx3], [None, gy1, gy2, gy3], [None, inv1, inv2, inv3]
    via = [via0, via1, via2]
    d2, z2 = [None, d21, d22, d23], [None, z21, z22, z23]

    def body(i):
        s = pl.multiple_of(i + PAD, 8)
        a, o = pl.ds(s, STEP), pl.ds(i, STEP)
        out[0, o, :] = v0[o, :]
        first = [None, d11[a, main] + e11[a, main], d12[a, main], d13[a, main]]
        below = d20[o, :]
        for l in range(1, 4):
            nb = weighted(d2[l], s, STEP, gx[l], gy[l])[:, main]
            nb = nb + via[l - 1][a, main] * below
            below = d2[l][a, main]
            if l < 3:
                nb = nb + via[l][a, main] * d2[l + 1][a, main]
            z = z2[l][a, main] - below + inv[l][a, main] * nb
            out[l, o, :] = vd0[l - 1, o, :] + first[l] + (1.0 + A3) * below + B3 * z

    each_chunk(0, rows, body, STEP)


def bond_kernel(field, part, weight, out):
    out[0] = field[0] + B3 * weight[...] * part[...]


def map_kernel(arrived, out, first, last, labels, vec, lab, acc, sem):
    devices = vec.shape[0]
    rows = out.shape[0]
    vec[...] = arrived[pl.ds(CAP * 8, devices, stride=ROWS_MSG), :].astype(jnp.int32)
    copy = pltpu.make_async_copy(vec, lab, sem)
    copy.start()
    acc[...] = jnp.zeros_like(acc)
    copy.wait()

    @pl.loop(0, devices // 8)
    def _(g):
        n = ROWS_MSG * 8
        data = arrived[pl.ds(pl.multiple_of(g * n, 8), n), :]
        for j in range(8):
            for r in range(CAP):
                slot = lab[g * 8 + j, r]
                labels[(g * 8 + j) * CAP + r] = slot
                a = pl.ds(pl.multiple_of(slot * 8, 8), 8)
                acc[a, :] += data[j * ROWS_MSG + r * 8 : j * ROWS_MSG + r * 8 + 8]

    out[...] = acc[0:rows, :]
    first[...] = acc[0:8, :]
    last[...] = acc[rows - 8 : rows, :]


def edges_kernel(cur, lo, hi, to_left, to_right, ext):
    rows = cur.shape[0]
    ext[0:H, :] = lo[...]
    ext[H : H + rows, :] = cur[...]
    ext[H + rows : rows + 2 * H, :] = hi[...]
    for j in range(to_left.shape[1] // W):
        t = ext[W * j : W * j + W, :].T
        to_left[:, W * j : W * j + W] = t[0:8]
        to_right[:, W * j : W * j + W] = t[W - 8 : W]


def effect_kernel(
    labels, cur, lo, hi, f_left, f_right, gx0, gx1, gy0, gy1, inv0, inv1, via0, sb0, d20, d21, z21,
    v0, picked, e11, d20_out, d21_out, z21_out,
    ec, e0, e1, z10, z11, e2, z20, e21, u, acc,
):
    rows = cur.shape[0]
    total = rows + 2 * H
    main, edge = slice(0, W), slice(W, 2 * W)
    ec[H : 2 * H, main] = lo[...]
    ec[PAD : PAD + rows, main] = cur[...]
    ec[PAD + rows : PAD + rows + H, main] = hi[...]
    u[...] = jnp.zeros_like(u)
    for j in range(f_left.shape[1] // W):
        u[0:8, :] = f_right[:, W * j : W * j + W]
        u[W - 8 : W, :] = f_left[:, W * j : W * j + W]
        n = min(W, total - W * j)
        ec[H + W * j : H + W * j + n, edge] = u[...].T[:n]

    def zeroth(s):
        a = pl.ds(s, WIDE)
        e0[a, :] = inv0[a, :] * ec[a, :]

    each_chunk(H, total, zeroth, WIDE)

    def first(s):
        a = pl.ds(s, WIDE)
        here = e0[a, :]
        z = inv0[a, :] * weighted(e0, s, WIDE, gx0, gy0)
        z10[a, :] = z
        e1[a, :] = A1 * here + B1 * z
        z = inv1[a, :] * via0[a, :] * here
        z11[a, :] = z
        e11[a, :] = B1 * z

    each_chunk(H, total, first, WIDE)

    def second(s):
        a = pl.ds(s, WIDE)
        low, high, between = e1[a, :], e11[a, :], via0[a, :]
        nb = weighted(e1, s, WIDE, gx0, gy0) + between * high
        z = z10[a, :] - low + inv0[a, :] * nb
        z20[a, :] = z
        e2[a, :] = A2 * low + B2 * z
        nb = weighted(e11, s, WIDE, gx1, gy1) + between * low
        z = z11[a, :] - high + inv1[a, :] * nb
        z21_out[a, :] = z21[a, :] + z
        d = A2 * high + B2 * z
        e21[a, :] = d
        d21_out[a, :] = d21[a, :] + d

    each_chunk(H, total, second, WIDE)

    def third(i):
        s = pl.multiple_of(i + PAD, 8)
        a, o = pl.ds(s, STEP), pl.ds(i, STEP)
        here = e2[a, main]
        nb = weighted(e2, s, STEP, gx0, gy0)[:, main] + via0[a, main] * e21[a, main]
        z = z20[a, main] - here + inv0[a, main] * nb
        whole = sb0[o, :] + e0[a, main] + e1[a, main] + (1.0 + A3) * here + B3 * z
        v0[o, :] = whole
        acc[o, :] = whole
        d20_out[o, :] = d20[o, :] + here

    each_chunk(0, rows, third, STEP)
    acc[rows : rows + 8, :] = jnp.zeros((8, W), F32)

    @pl.loop(0, labels.shape[0], unroll=8)
    def _(k):
        picked[pl.ds(pl.multiple_of(k * 8, 8), 8), :] = acc[
            pl.ds(pl.multiple_of(labels[k] * 8, 8), 8), :
        ]


def give_kernel(dest, back, out):
    @pl.loop(0, out.shape[0], unroll=8)
    def _(k):
        out[k] = back[pl.ds(pl.multiple_of(dest[k] * 8, 8), 8), :]


def ring(axis, step):
    n = lax.axis_size(axis)
    return [(i, (i + step) % n) for i in range(n)]


def shift(x, axis, step):
    return lax.ppermute(x, axis, ring(axis, step))


def facing(x, step=0):
    n, m = lax.axis_size("gx"), lax.axis_size("yt")
    pairs = [
        (g * m + t, ((g + step) % n) * m + (t ^ (m // 2))) for g in range(n) for t in range(m)
    ]
    return lax.ppermute(x, ALL, pairs)


def on_device(v, st, cx, cy, via, mask, blocks, owner, slot):
    layers, rows, cols = v.shape
    devices = lax.axis_size("gx") * lax.axis_size("yt")
    nb = blocks.shape[0]
    total = rows + 2 * H
    nr = total + 2 * H
    side_blocks = -(-total // W)
    place = jnp.stack(
        [
            lax.axis_index("gx") * rows,
            jnp.int32(rows * lax.axis_size("gx")),
            lax.axis_index("yt") * cols,
            jnp.int32(cols * lax.axis_size("yt")),
        ]
    ).astype(jnp.int32)

    outgoing, dest = call(
        send_kernel,
        [shape(devices * ROWS_MSG, W), jax.ShapeDtypeStruct((nb,), jnp.int32)],
        [owner.reshape(nb), slot, blocks],
        scratch=[
            pltpu.SMEM((devices,), jnp.int32),
            pltpu.VMEM((devices * CAP * 8, W), F32),
            pltpu.VMEM((devices, W), jnp.int32),
        ],
        specs={0: SMEM, 1: SMEM},
        out_specs=[pl.BlockSpec(memory_space=pltpu.VMEM), SMEM],
    )
    sources = [v, cx, cy, st, via]
    args = sources + [mask] + sources + [mask, v]
    specs = {}
    last = rows // 8 - 1
    for i in range(5):
        n = sources[i].shape[0]
        specs[i] = pl.BlockSpec((n, 8, W), lambda _: (0, 0, 0))
        specs[6 + i] = pl.BlockSpec((n, 8, W), lambda _: (0, last, 0))
    specs[5] = pl.BlockSpec((8, W), lambda _: (0, 0))
    specs[11] = pl.BlockSpec((8, W), lambda _: (last, 0))
    specs[12] = pl.BlockSpec((1, rows, W), lambda _: (layers - 1, 0, 0))
    count = 5 * layers
    first_rows, last_rows, v_top, v_first, v_last = pl.pallas_call(
        pack_x_kernel,
        grid=(1,),
        out_shape=[shape(count, 8, W)] * 2 + [shape(rows, W), shape(H, W), shape(H, W)],
        in_specs=[specs[i] for i in range(13)],
        out_specs=[
            pl.BlockSpec((count, 8, W), lambda _: (0, 0, 0)),
            pl.BlockSpec((count, 8, W), lambda _: (0, 0, 0)),
            pl.BlockSpec((rows, W), lambda _: (0, 0)),
            pl.BlockSpec((H, W), lambda _: (0, 0)),
            pl.BlockSpec((H, W), lambda _: (0, 0)),
        ],
        name="pack_x_kernel",
        compiler_params=pltpu.CompilerParams(vmem_limit_bytes=58 << 20),
        cost_estimate=pl.CostEstimate(flops=1, bytes_accessed=1_000_000, transcendentals=0),
    )(*args)
    lo = shift(last_rows, "gx", 1)
    hi = shift(first_rows, "gx", -1)
    v_part = facing(v_top)
    v_lo, v_hi = facing(v_last, 1), facing(v_first, -1)
    tiles = [v, cx, cy, st, via, mask, v_part, lo, hi, v_lo, v_hi]
    to_left, to_right = call(pack_y_kernel, [shape(total, W), shape(total, W)], tiles, vmem=8)
    f_left = shift(to_right, "yt", 1)
    f_right = shift(to_left, "yt", -1)
    outgoing, f_left, f_right = lax.optimization_barrier((outgoing, f_left, f_right))
    arrived = lax.all_to_all(
        outgoing.reshape(devices, ROWS_MSG, 1, W), ALL, 0, 0, tiled=True
    ).reshape(devices * ROWS_MSG, W)

    one = shape(nr, 2 * W)
    tile = shape(rows, W)
    buffer = lambda *d: pltpu.VMEM(d, F32)
    msg_shape = shape(total + 8 * side_blocks, W)
    outs = call(
        base_kernel,
        [one] * (4 * layers + 5) + [tile, one, one, tile, shape(layers - 1, rows, W), msg_shape],
        [place, *tiles, f_left, f_right],
        scratch=[buffer(nr, 2 * W)] * (4 * layers + 1)
        + [buffer(side_blocks * W, W)]
        + [buffer(nr, 2 * W)] * 7,
        specs={0: SMEM},
        vmem=VMEM_BASE,
        cost=20_000_000,
    )
    gx, gy, inv, via_e = outs[0:4], outs[4:8], outs[8:12], outs[12:15]
    bond, d02, d03, d11, d12, z12, d20, d21, z21, sb0, vd0, msg0 = outs[15:]
    part0 = facing(msg0)

    cur, cur_first, cur_last, labels = call(
        map_kernel,
        [tile, shape(8, W), shape(8, W), jax.ShapeDtypeStruct((devices * CAP,), jnp.int32)],
        [arrived],
        scratch=[
            pltpu.VMEM((devices, W), jnp.int32),
            pltpu.SMEM((devices, W), jnp.int32),
            buffer(rows + 8, W),
            pltpu.SemaphoreType.DMA,
        ],
        out_specs=[pl.BlockSpec(memory_space=pltpu.VMEM)] * 3 + [SMEM],
    )
    cur_lo = shift(cur_last, "gx", 1)
    cur_hi = shift(cur_first, "gx", -1)
    cur_lo, cur_hi, part0 = lax.optimization_barrier((cur_lo, cur_hi, part0))
    top = [gx[3], gy[3], inv[3], via_e[2], bond]
    d13, z13, msg1 = call(
        first_top_kernel,
        [one, one, msg_shape],
        [d02, d03, part0, *top],
        scratch=[buffer(nr, 2 * W), buffer(side_blocks * W, W), buffer(W, W)],
        vmem=VMEM_TOP,
    )
    part1 = facing(msg1)
    d23, z23, msg2, weight = call(
        second_top_kernel,
        [one, one, tile, tile],
        [d12, d13, z13, part1, *top],
        scratch=[buffer(nr, 2 * W), buffer(side_blocks * W, W), buffer(W, W)],
        vmem=VMEM_TOP,
    )

    cur_left, cur_right = call(
        edges_kernel,
        [shape(8, side_blocks * W)] * 2,
        [cur, cur_lo, cur_hi],
        scratch=[buffer(side_blocks * W, W)],
    )
    cur_f_left = shift(cur_right, "yt", 1)
    cur_f_right = shift(cur_left, "yt", -1)
    v0, picked, e11, d20, d21, z21 = call(
        effect_kernel,
        [tile, shape(devices * CAP * 8, W), one, tile, one, one],
        [labels, cur, cur_lo, cur_hi, cur_f_left, cur_f_right, *gx[:2], *gy[:2], *inv[:2],
         via_e[0], sb0, d20, d21, z21],
        scratch=[buffer(nr, 2 * W)] * 8 + [buffer(W, W), buffer(rows + 8, W)],
        specs={0: SMEM},
        vmem=VMEM_EFFECT,
    )
    part2 = facing(msg2)
    back = lax.all_to_all(picked, ALL, 0, 0, tiled=True)

    voltage = call(
        final_kernel,
        shape(layers, rows, W),
        [v0, vd0, d11, d12, z12, e11, d13, d20, d21, d23, z21, z23,
         *gx[1:], *gy[1:], *inv[1:], *via_e],
        scratch=[buffer(nr, 2 * W)] * 2,
        vmem=VMEM_FINAL,
        cost=10_000_000,
    )
    voltage = pl.pallas_call(
        bond_kernel,
        grid=(1,),
        out_shape=shape(layers, rows, W),
        in_specs=[
            pl.BlockSpec((1, rows, W), lambda _: (layers - 1, 0, 0)),
            pl.BlockSpec((rows, W), lambda _: (0, 0)),
            pl.BlockSpec((rows, W), lambda _: (0, 0)),
        ],
        out_specs=pl.BlockSpec((1, rows, W), lambda _: (layers - 1, 0, 0)),
        input_output_aliases={0: 0},
        name="bond_kernel",
        compiler_params=pltpu.CompilerParams(vmem_limit_bytes=6 << 20),
    )(voltage, part2, weight)
    block_voltage = call(
        give_kernel, shape(nb, 8, W), [dest, back], specs={0: SMEM}
    )
    return voltage, block_voltage


def solution(mesh):
    tile = P(None, "gx", "yt")
    return jax.shard_map(
        on_device,
        mesh=mesh,
        in_specs=(tile, tile, tile, tile, tile, P("gx", "yt"), P(ALL, None, None), P(ALL, None), P(ALL)),
        out_specs=(tile, P(ALL, None, None)),
        check_vma=False,
    )
```

```python
import jax
import jax.numpy as jnp
from jax import lax
from jax.experimental import pallas as pl
from jax.experimental.pallas import tpu as pltpu
from jax.sharding import PartitionSpec as P

CAP = 2
BOND = 2.0
CENTER = 1.0
HALFWIDTH = 0.97
SIGMA = CENTER / HALFWIDTH
RHO0 = 1.0 / SIGMA
RHO1 = 1.0 / (2.0 * SIGMA - RHO0)
RHO2 = 1.0 / (2.0 * SIGMA - RHO1)
RHO3 = 1.0 / (2.0 * SIGMA - RHO2)
A1, B1 = RHO1 * RHO0, 2.0 * RHO1 / HALFWIDTH
A2, B2 = RHO2 * RHO1, 2.0 * RHO2 / HALFWIDTH
A3, B3 = RHO3 * RHO2, 2.0 * RHO3 / HALFWIDTH

VMEM_BASE, VMEM_TOP, VMEM_EFFECT, VMEM_FINAL = 58, 58, 58, 58

ALL = ("gx", "yt")
F32 = jnp.float32
W = 128
H = 8
PAD = 16
Q = 4
WIDE = 48
STEP = 64
ROWS_MSG = CAP * 8 + 1


def call(kernel, out, args, scratch=(), specs=None, out_specs=None, vmem=6, cost=1_000_000):
    specs = specs or {}
    in_specs = [
        specs.get(i, pl.BlockSpec(memory_space=pltpu.VMEM)) for i in range(len(args))
    ]
    many = isinstance(out, (list, tuple))
    outs = list(out) if many else [out]
    o_specs = out_specs or [pl.BlockSpec(memory_space=pltpu.VMEM)] * len(outs)
    return pl.pallas_call(
        kernel,
        out_shape=outs if many else outs[0],
        in_specs=in_specs,
        out_specs=o_specs if many else o_specs[0],
        scratch_shapes=list(scratch),
        name=kernel.__name__,
        compiler_params=pltpu.CompilerParams(vmem_limit_bytes=vmem << 20),
        cost_estimate=pl.CostEstimate(flops=cost, bytes_accessed=cost, transcendentals=0),
    )(*args)


def shape(*dims):
    return jax.ShapeDtypeStruct(dims, F32)


SMEM = pl.BlockSpec(memory_space=pltpu.SMEM)
ANY = pl.BlockSpec(memory_space=pl.ANY)


class Copies:
    def __init__(self, sems):
        self.sems, self.made = sems, []

    def start(self, *pairs):
        begun = []
        for source, target in pairs:
            copy = pltpu.make_async_copy(source, target, self.sems.at[len(self.made)])
            copy.start()
            self.made.append(copy)
            begun.append(copy)
        return begun


def wait(copies):
    for copy in copies:
        copy.wait()


def from_right(x):
    return pltpu.roll(x, x.shape[-1] - 1, axis=1)


def from_left(x):
    return pltpu.roll(x, 1, axis=1)


def lanes(rows, width=W):
    return lax.broadcasted_iota(jnp.int32, (rows, width), 1)


def each_chunk(first, rows, body, step):
    @pl.loop(0, rows // step)
    def _(k):
        body(pl.multiple_of(first + k * step, 8))


def send_kernel(owner_ref, slot_ref, blocks_ref, out_ref, dest_ref, count_ref, buf, slots):
    devices = count_ref.shape[0]

    @pl.loop(0, devices, unroll=8)
    def _(o):
        count_ref[o] = 0

    buf[...] = jnp.zeros_like(buf)
    slots[...] = jnp.full(slots.shape, 64, jnp.int32)
    lane = lanes(1)

    @pl.loop(0, blocks_ref.shape[0], unroll=4)
    def _(k):
        owner = owner_ref[k]
        rank = count_ref[owner]
        count_ref[owner] = rank + 1
        dest = owner * CAP + rank
        dest_ref[k] = dest
        buf[pl.ds(pl.multiple_of(dest * 8, 8), 8), :] = blocks_ref[k]
        row = slots[pl.ds(owner, 1), :]
        slots[pl.ds(owner, 1), :] = jnp.where(lane == rank, slot_ref[k], row)

    @pl.loop(0, devices // 8)
    def _(g):
        data = buf[pl.ds(pl.multiple_of(g * CAP * 64, 8), CAP * 64), :]
        label = slots[pl.ds(pl.multiple_of(g * 8, 8), 8), :].astype(F32)
        pieces = []
        for j in range(8):
            pieces += [data[CAP * 8 * j : CAP * 8 * (j + 1)], label[j : j + 1]]
        out_ref[pl.ds(pl.multiple_of(g * ROWS_MSG * 8, 8), ROWS_MSG * 8), :] = (
            jnp.concatenate(pieces, axis=0)
        )


def pack_x_kernel(*refs):
    firsts, lasts, v3 = refs[:6], refs[6:12], refs[12]
    first_out, last_out, v3_out, v3_first, v3_last = refs[13:]
    for group, out in ((firsts, first_out), (lasts, last_out)):
        p = 0
        for ref in group[:5]:
            n = ref.shape[0]
            out[p : p + n] = ref[...]
            p += n
        out[p] = BOND * group[5][...].astype(F32)
    rows = v3.shape[1]
    v3_out[...] = v3[0]
    v3_first[...] = v3[0, 0:H, :]
    v3_last[...] = v3[0, rows - H : rows, :]


def pack_y_kernel(v, cx, cy, st, via, mask, vp, lo, hi, vlo, vhi, to_left, to_right):
    rows = v.shape[1]

    def pack(planes, at, n):
        lane = lanes(n)
        left = jnp.zeros((n, W), F32)
        right = jnp.zeros((n, W), F32)
        for p, x in enumerate(planes):
            turned = x if p == 0 else pltpu.roll(x, Q * p, axis=1)
            left = jnp.where(lane // Q == p, turned, left)
            right = jnp.where(lane // Q == (p - 1) % (W // Q), turned, right)
        to_left[pl.ds(at, n), :] = left
        to_right[pl.ds(at, n), :] = right

    def tile(i):
        at = pl.ds(i, STEP)
        planes = [ref[l, at, :] for ref in (v, cx, cy, st, via) for l in range(ref.shape[0])]
        planes += [BOND * mask[at, :].astype(F32), vp[at, :]]
        pack(planes, pl.multiple_of(i + H, 8), STEP)

    each_chunk(0, rows, tile, STEP)
    count = lo.shape[0]
    pack([lo[p] for p in range(count)] + [vlo[...]], 0, H)
    pack([hi[p] for p in range(count)] + [vhi[...]], H + rows, H)


def rows_of(ref, l=None):
    if l is None:
        return lambda s, n: ref[pl.ds(s, n), :]
    return lambda s, n: ref[l, pl.ds(s, n), :]


def weighted(x, s, n, gx, gy):
    low = pl.multiple_of(s - 8, 8)
    near = rows_of(x)(low, n + 16)
    gnear = rows_of(gx)(low, n + 8)
    c = near[8 : 8 + n]
    g = rows_of(gy)(s, n)
    up = gnear[8 : 8 + n] * near[9 : 9 + n]
    down = (gnear * near[0 : n + 8])[7 : 7 + n]
    return up + down + g * from_right(c) + from_left(g * c)


def base_kernel(*refs):
    place, v, cx, cy, st, via, mask, vp, lo, hi, vlo, vhi, f_left, f_right = refs[:14]
    refs = list(refs[14:])
    layers, rows = v.shape[0], v.shape[1]
    total = rows + 2 * H

    def take(n):
        got = refs[:n]
        del refs[:n]
        return got

    outs = take(4 * layers + 11)
    helds = take(4 * layers + 11)
    ev, ecx, ecy, est = take(layers), take(layers), take(layers), take(layers)
    evp, side, d00, d01, d10, z10, z11, z20, e20, sems = take(10)
    copies = Copies(sems)
    home = dict(zip(map(id, helds), outs))

    def give(*held):
        return copies.start(*[(h, home[id(h)]) for h in held])

    refs = list(helds)
    gx, gy, inv, viae = take(layers), take(layers), take(layers), take(layers - 1)
    bond, d02, d03, d11, d12, z12, d20, d21, z21, sb0, vd0, msg = take(12)
    d0 = [d00, d01, d02, d03]
    d1, z1 = [d10, d11, d12], [z10, z11, z12]
    d2, z2 = [e20, d21], [z20, z21]
    dests = [*ev, *ecx, *ecy, *est, *viae, bond, evp]
    main, edge = slice(0, W), slice(W, 2 * W)
    sources = [ref.at[l] for ref in (v, cx, cy, st, via) for l in range(ref.shape[0])]
    arriving = copies.start(
        *[
            (source, dest.at[pl.ds(PAD, rows), pl.ds(0, W)])
            for source, dest in zip([*sources, vp], [*dests[:-2], evp])
        ]
    )

    def sides(s):
        r = pl.multiple_of(s - H, 8)
        a = f_right[pl.ds(r, WIDE), :]
        b = f_left[pl.ds(r, WIDE), :]
        even = lanes(WIDE) // Q % 2 == 0
        both = [jnp.where(even, a, b), jnp.where(even, b, a)]
        for p, dest in enumerate(dests):
            x = both[p % 2]
            dest[pl.ds(s, WIDE), edge] = x if p == 0 else pltpu.roll(x, W - Q * p, axis=1)

    each_chunk(H, total, sides, WIDE)

    def bonds(i):
        weight = BOND * mask[pl.ds(i, STEP), :].astype(F32)
        bond[pl.ds(pl.multiple_of(i + PAD, 8), STEP), main] = weight

    each_chunk(0, rows, bonds, STEP)
    for p, dest in enumerate(dests):
        is_vp = p == len(dests) - 1
        dest[H : 2 * H, main] = vlo[...] if is_vp else lo[p]
        dest[PAD + rows : PAD + rows + H, main] = vhi[...] if is_vp else hi[p]

    wait(arriving)

    x_first, x_total, y_first, y_total = place[0], place[1], place[2], place[3]
    col = lanes(1, 2 * W)
    col = y_first + jnp.where(col < W + W // 2, col, col - 2 * W)
    nxt = lax.rem(col + 1 + y_total, y_total)
    seam = W // 2
    keep_y = jnp.where((nxt != seam) & (nxt != seam + y_total // 2), 0.5, 0.0).astype(F32)

    def conductances(s):
        row = x_first + s - PAD + lax.broadcasted_iota(jnp.int32, (WIDE, 1), 0)
        keep_x = jnp.where((row != -1) & (row != x_total - 1), 0.5, 0.0).astype(F32)
        for l in range(layers):
            c = ecx[l][pl.ds(s, WIDE + 8), :]
            gx[l][pl.ds(s, WIDE), :] = keep_x * (c[0:WIDE] + c[1 : WIDE + 1])
            c = ecy[l][pl.ds(s, WIDE), :]
            gy[l][pl.ds(s, WIDE), :] = keep_y * (c + from_right(c))

    each_chunk(H, total, conductances, WIDE)
    leaving = give(*gx, *gy, *viae, bond)

    def start(s):
        n = WIDE
        a = pl.ds(s, n)
        for l in range(layers):
            near = gx[l][pl.ds(pl.multiple_of(s - 8, 8), n + 8), :]
            up, down, right = near[8 : 8 + n], near[7 : 7 + n], gy[l][a, :]
            off = up + down + right + from_left(right)
            nb = weighted(ev[l], s, n, gx[l], gy[l])
            if l < layers - 1:
                off = off + viae[l][a, :]
                nb = nb + viae[l][a, :] * ev[l + 1][a, :]
            else:
                off = off + bond[a, :]
                nb = nb + bond[a, :] * evp[a, :]
            if l > 0:
                off = off + viae[l - 1][a, :]
                nb = nb + viae[l - 1][a, :] * ev[l - 1][a, :]
            c = ev[l][a, :]
            inverse = 1.0 / (est[l][a, :] + off)
            inv[l][a, :] = inverse
            d0[l][a, :] = (nb - off * c) * inverse

    each_chunk(H, total, start, WIDE)
    leaving += give(*inv, d02, d03)

    def links(d, l, s, n):
        nb = weighted(d[l], s, n, gx[l], gy[l])
        if l < layers - 1:
            nb = nb + viae[l][pl.ds(s, n), :] * d[l + 1][pl.ds(s, n), :]
        if l > 0:
            nb = nb + viae[l - 1][pl.ds(s, n), :] * d[l - 1][pl.ds(s, n), :]
        return inv[l][pl.ds(s, n), :] * nb

    def first(s):
        a = pl.ds(s, WIDE)
        r = pl.ds(pl.multiple_of(s - H, 8), WIDE)
        side[r, :] = d03[a, edge]
        msg[r, :] = d03[a, main]
        for l in range(layers - 1):
            z = links(d0, l, s, WIDE)
            z1[l][a, :] = z
            d1[l][a, :] = A1 * d0[l][a, :] + B1 * z

    each_chunk(H, total, first, WIDE)
    pack_side(side, msg, total)
    leaving += give(d11, d12, z12, msg)

    def second(s):
        a = pl.ds(s, WIDE)
        for l in range(2):
            z = z1[l][a, :] - d1[l][a, :] + links(d1, l, s, WIDE)
            z2[l][a, :] = z
            d2[l][a, :] = A2 * d1[l][a, :] + B2 * z

    each_chunk(H, total, second, WIDE)
    leaving += give(d21, z21)

    def third(s):
        a = pl.ds(s, STEP)
        o = pl.ds(pl.multiple_of(s - PAD, 8), STEP)
        nb = weighted(e20, s, STEP, gx[0], gy[0])[:, main]
        nb = inv[0][a, main] * (nb + viae[0][a, main] * d21[a, main])
        d = e20[a, main]
        z = z20[a, main] - d + nb
        d20[o, :] = d
        sb0[o, :] = ev[0][a, main] + d00[a, main] + d10[a, main] + (1.0 + A3) * d + B3 * z
        for l in range(1, layers):
            vd0[l - 1, o, :] = ev[l][a, main] + d0[l][a, main]

    each_chunk(PAD, rows, third, STEP)
    leaving += give(d20, sb0, vd0)
    wait(leaving)


def pack_side(side, msg, total):
    for j in range(-(-total // W)):
        t = side[W * j : W * j + W, :].T
        msg[total + 8 * j : total + 8 * j + Q, :] = t[0:Q]
        msg[total + 8 * j + Q : total + 8 * j + 2 * Q, :] = t[W - Q : W]


def unpack_side(msg, total, u, ref):
    u[...] = jnp.zeros_like(u)
    for j in range(-(-total // W)):
        u[0:Q, :] = msg[total + 8 * j : total + 8 * j + Q, :]
        u[W - Q : W, :] = msg[total + 8 * j + Q : total + 8 * j + 2 * Q, :]
        n = min(W, total - W * j)
        t = u[...].T
        ref[H + W * j : H + W * j + n, W : 2 * W] = t[:n]


def top_kernel(low, here, z, part, gx, gy, inv, via, bond, *rest):
    again = z is not None
    if again:
        d_out, z_out, msg, weight, ep, side, u = rest
    else:
        d_out, z_out, msg, ep, side, u = rest
    total = part.shape[0] - 8 * (side.shape[0] // W)
    unpack_side(part, total, u, ep)

    def body(s):
        a = pl.ds(s, WIDE)
        r = pl.ds(pl.multiple_of(s - H, 8), WIDE)
        other = jnp.concatenate([part[r, :], ep[a, W : 2 * W]], axis=1)
        nb = weighted(here, s, WIDE, gx, gy) + via[a, :] * low[a, :] + bond[a, :] * other
        c = here[a, :]
        x = inv[a, :] * nb
        if again:
            x = z[a, :] - c + x
        d = (A2 if again else A1) * c + (B2 if again else B1) * x
        z_out[a, :] = x
        d_out[a, :] = d
        if not again:
            side[r, :] = d[:, W:]
            msg[r, :] = d[:, :W]

    each_chunk(H, total, body, WIDE)
    if not again:
        pack_side(side, msg, total)
    else:
        rows = msg.shape[0]
        msg[...] = d_out[PAD : PAD + rows, 0:W]
        weight[...] = inv[PAD : PAD + rows, 0:W] * bond[PAD : PAD + rows, 0:W]


def first_top_kernel(low, here, *rest):
    top_kernel(low, here, None, *rest)


def second_top_kernel(*refs):
    top_kernel(*refs)


def final_kernel(
    v0, vd0, d11, d12, z12, e11, d13, d20, b21, e21, d23, z21, ze21, z23,
    gx1, gx2, gx3, gy1, gy2, gy3, inv1, inv2, inv3, via0, via1, via2,
    out, d22, z22, d21,
):
    main = slice(0, W)
    rows = out.shape[1]

    def middle(s):
        a = pl.ds(s, WIDE)
        this = d12[a, :]
        nb = weighted(d12, s, WIDE, gx2, gy2)
        nb = nb + via1[a, :] * (d11[a, :] + e11[a, :]) + via2[a, :] * d13[a, :]
        z = z12[a, :] - this + inv2[a, :] * nb
        z22[a, :] = z
        d22[a, :] = A2 * this + B2 * z
        d21[a, :] = b21[a, :] + e21[a, :]

    each_chunk(H, rows + 2 * H, middle, WIDE)
    gx, gy, inv = [None, gx1, gx2, gx3], [None, gy1, gy2, gy3], [None, inv1, inv2, inv3]
    via = [via0, via1, via2]
    d2, z2 = [None, d21, d22, d23], [None, None, z22, z23]

    def body(i):
        s = pl.multiple_of(i + PAD, 8)
        a, o = pl.ds(s, STEP), pl.ds(i, STEP)
        out[0, o, :] = v0[o, :]
        first = [None, d11[a, main] + e11[a, main], d12[a, main], d13[a, main]]
        below = d20[o, :]
        for l in range(1, 4):
            nb = weighted(d2[l], s, STEP, gx[l], gy[l])[:, main]
            nb = nb + via[l - 1][a, main] * below
            below = d2[l][a, main]
            if l < 3:
                nb = nb + via[l][a, main] * d2[l + 1][a, main]
            z = (z21[a, main] + ze21[o, :] if l == 1 else z2[l][a, main]) - below + inv[l][a, main] * nb
            out[l, o, :] = vd0[l - 1, o, :] + first[l] + (1.0 + A3) * below + B3 * z

    each_chunk(0, rows, body, STEP)


def map_kernel(arrived, out, first, last, labels, vec, lab, a0, a1, a2, a3, sem):
    devices = vec.shape[0]
    rows = out.shape[0]
    vec[...] = arrived[pl.ds(CAP * 8, devices, stride=ROWS_MSG), :].astype(jnp.int32)
    copy = pltpu.make_async_copy(vec, lab, sem)
    copy.start()
    parts = (a0, a1, a2, a3)
    for acc in parts:
        acc[...] = jnp.zeros_like(acc)
    copy.wait()

    @pl.loop(0, devices // 8)
    def _(g):
        n = ROWS_MSG * 8
        data = arrived[pl.ds(pl.multiple_of(g * n, 8), n), :]
        for j in range(8):
            for r in range(CAP):
                slot = lab[g * 8 + j, r]
                labels[(g * 8 + j) * CAP + r] = slot
                a = pl.ds(pl.multiple_of(slot * 8, 8), 8)
                acc = parts[(j * CAP + r) % 4]
                acc[a, :] += data[j * ROWS_MSG + r * 8 : j * ROWS_MSG + r * 8 + 8]

    out[...] = (a0[0:rows, :] + a1[0:rows, :]) + (a2[0:rows, :] + a3[0:rows, :])
    first[...] = out[0:8, :]
    last[...] = out[rows - 8 : rows, :]


def edges_kernel(cur, lo, hi, to_left, to_right, ext):
    rows = cur.shape[0]
    ext[0:H, :] = lo[...]
    ext[H : H + rows, :] = cur[...]
    ext[H + rows : rows + 2 * H, :] = hi[...]
    for j in range(to_left.shape[1] // W):
        t = ext[W * j : W * j + W, :].T
        to_left[:, W * j : W * j + W] = t[0:8]
        to_right[:, W * j : W * j + W] = t[W - 8 : W]


def effect_kernel(
    labels, cur, lo, hi, f_left, f_right, *refs
):
    coefficients, (v0, picked, e11_out, e21_out, z21, d20_out) = refs[:9], refs[9:15]
    held, refs = refs[15:24], refs[24:]
    inv0, gx0, gy0, via0, inv1, gx1, gy1, sb0, d20 = held
    ec, e0, e1, z10, z11, e2, z20, e11, e21, u, acc, sems = refs
    copies = Copies(sems)
    arriving = copies.start(*zip(coefficients, held))
    rows = cur.shape[0]
    total = rows + 2 * H
    main, edge = slice(0, W), slice(W, 2 * W)
    ec[H : 2 * H, main] = lo[...]
    ec[PAD : PAD + rows, main] = cur[...]
    ec[PAD + rows : PAD + rows + H, main] = hi[...]
    u[...] = jnp.zeros_like(u)
    for j in range(f_left.shape[1] // W):
        u[0:8, :] = f_right[:, W * j : W * j + W]
        u[W - 8 : W, :] = f_left[:, W * j : W * j + W]
        n = min(W, total - W * j)
        ec[H + W * j : H + W * j + n, edge] = u[...].T[:n]

    wait(arriving[0:1])

    def zeroth(s):
        a = pl.ds(s, WIDE)
        e0[a, :] = inv0[a, :] * ec[a, :]

    each_chunk(H, total, zeroth, WIDE)
    wait(arriving[1:5])

    def first(s):
        a = pl.ds(s, WIDE)
        here = e0[a, :]
        z = inv0[a, :] * weighted(e0, s, WIDE, gx0, gy0)
        z10[a, :] = z
        e1[a, :] = A1 * here + B1 * z
        z = inv1[a, :] * via0[a, :] * here
        z11[a, :] = z
        e11[a, :] = B1 * z

    each_chunk(H, total, first, WIDE)
    wait(arriving[5:7])

    def second(s):
        a = pl.ds(s, WIDE)
        low, high, between = e1[a, :], e11[a, :], via0[a, :]
        nb = weighted(e1, s, WIDE, gx0, gy0) + between * high
        z = z10[a, :] - low + inv0[a, :] * nb
        z20[a, :] = z
        e2[a, :] = A2 * low + B2 * z
        nb = weighted(e11, s, WIDE, gx1, gy1) + between * low
        z = z11[a, :] - high + inv1[a, :] * nb
        z11[a, :] = z
        e21[a, :] = A2 * high + B2 * z

    each_chunk(H, total, second, WIDE)
    leaving = copies.start((e11, e11_out), (e21, e21_out))
    wait(arriving[7:])

    def third(i):
        s = pl.multiple_of(i + PAD, 8)
        a, o = pl.ds(s, STEP), pl.ds(i, STEP)
        here = e2[a, main]
        nb = weighted(e2, s, STEP, gx0, gy0)[:, main] + via0[a, main] * e21[a, main]
        z = z20[a, main] - here + inv0[a, main] * nb
        whole = sb0[o, :] + e0[a, main] + e1[a, main] + (1.0 + A3) * here + B3 * z
        v0[o, :] = whole
        acc[o, :] = whole
        d20_out[o, :] = d20[o, :] + here
        z21[o, :] = z11[a, main]

    each_chunk(0, rows, third, STEP)
    acc[rows : rows + 8, :] = jnp.zeros((8, W), F32)

    @pl.loop(0, labels.shape[0], unroll=8)
    def _(k):
        picked[pl.ds(pl.multiple_of(k * 8, 8), 8), :] = acc[
            pl.ds(pl.multiple_of(labels[k] * 8, 8), 8), :
        ]

    wait(leaving)


def last_kernel(dest, back, field, part, weight, out, top):
    top[0] = field[0] + B3 * weight[...] * part[...]

    @pl.loop(0, out.shape[0], unroll=8)
    def _(k):
        out[k] = back[pl.ds(pl.multiple_of(dest[k] * 8, 8), 8), :]


def ring(axis, step):
    n = lax.axis_size(axis)
    return [(i, (i + step) % n) for i in range(n)]


def shift(x, axis, step):
    return lax.ppermute(x, axis, ring(axis, step))


def facing(x, step=0):
    n, m = lax.axis_size("gx"), lax.axis_size("yt")
    pairs = [
        (g * m + t, ((g + step) % n) * m + (t ^ (m // 2))) for g in range(n) for t in range(m)
    ]
    return lax.ppermute(x, ALL, pairs)


def on_device(v, st, cx, cy, via, mask, blocks, owner, slot):
    layers, rows, cols = v.shape
    devices = lax.axis_size("gx") * lax.axis_size("yt")
    nb = blocks.shape[0]
    total = rows + 2 * H
    nr = total + 2 * H
    side_blocks = -(-total // W)
    place = jnp.stack(
        [
            lax.axis_index("gx") * rows,
            jnp.int32(rows * lax.axis_size("gx")),
            lax.axis_index("yt") * cols,
            jnp.int32(cols * lax.axis_size("yt")),
        ]
    ).astype(jnp.int32)

    outgoing, dest = call(
        send_kernel,
        [shape(devices * ROWS_MSG, W), jax.ShapeDtypeStruct((nb,), jnp.int32)],
        [owner.reshape(nb), slot, blocks],
        scratch=[
            pltpu.SMEM((devices,), jnp.int32),
            pltpu.VMEM((devices * CAP * 8, W), F32),
            pltpu.VMEM((devices, W), jnp.int32),
        ],
        specs={0: SMEM, 1: SMEM},
        out_specs=[pl.BlockSpec(memory_space=pltpu.VMEM), SMEM],
    )
    sources = [v, cx, cy, st, via]
    args = sources + [mask] + sources + [mask, v]
    specs = {}
    last = rows // 8 - 1
    for i in range(5):
        n = sources[i].shape[0]
        specs[i] = pl.BlockSpec((n, 8, W), lambda _: (0, 0, 0))
        specs[6 + i] = pl.BlockSpec((n, 8, W), lambda _: (0, last, 0))
    specs[5] = pl.BlockSpec((8, W), lambda _: (0, 0))
    specs[11] = pl.BlockSpec((8, W), lambda _: (last, 0))
    specs[12] = pl.BlockSpec((1, rows, W), lambda _: (layers - 1, 0, 0))
    count = 5 * layers
    first_rows, last_rows, v_top, v_first, v_last = pl.pallas_call(
        pack_x_kernel,
        grid=(1,),
        out_shape=[shape(count, 8, W)] * 2 + [shape(rows, W), shape(H, W), shape(H, W)],
        in_specs=[specs[i] for i in range(13)],
        out_specs=[
            pl.BlockSpec((count, 8, W), lambda _: (0, 0, 0)),
            pl.BlockSpec((count, 8, W), lambda _: (0, 0, 0)),
            pl.BlockSpec((rows, W), lambda _: (0, 0)),
            pl.BlockSpec((H, W), lambda _: (0, 0)),
            pl.BlockSpec((H, W), lambda _: (0, 0)),
        ],
        name="pack_x_kernel",
        compiler_params=pltpu.CompilerParams(vmem_limit_bytes=58 << 20),
        cost_estimate=pl.CostEstimate(flops=1, bytes_accessed=1_000_000, transcendentals=0),
    )(*args)
    lo = shift(last_rows, "gx", 1)
    hi = shift(first_rows, "gx", -1)
    v_part = facing(v_top)
    v_lo, v_hi = facing(v_last, 1), facing(v_first, -1)
    tiles = [v, cx, cy, st, via, mask, v_part, lo, hi, v_lo, v_hi]
    to_left, to_right = call(pack_y_kernel, [shape(total, W), shape(total, W)], tiles, vmem=8)
    f_left = shift(to_right, "yt", 1)
    f_right = shift(to_left, "yt", -1)
    outgoing, f_left, f_right = lax.optimization_barrier((outgoing, f_left, f_right))
    arrived = lax.all_to_all(
        outgoing.reshape(devices, ROWS_MSG, 1, W), ALL, 0, 0, tiled=True
    ).reshape(devices * ROWS_MSG, W)

    one = shape(nr, 2 * W)
    tile = shape(rows, W)
    buffer = lambda *d: pltpu.VMEM(d, F32)
    msg_shape = shape(total + 8 * side_blocks, W)
    held = [one] * (4 * layers + 5)
    held += [tile, one, one, tile, shape(layers - 1, rows, W), msg_shape]
    outs = call(
        base_kernel,
        held,
        [place, *tiles, f_left, f_right],
        scratch=[buffer(*h.shape) for h in held]
        + [buffer(nr, 2 * W)] * (4 * layers + 1)
        + [buffer(side_blocks * W, W)]
        + [buffer(nr, 2 * W)] * 7
        + [pltpu.SemaphoreType.DMA((9 * layers + 20,))],
        specs={0: SMEM, 1: ANY, 2: ANY, 3: ANY, 4: ANY, 5: ANY, 7: ANY},
        out_specs=[ANY] * len(held),
        vmem=VMEM_BASE,
        cost=20_000_000,
    )
    gx, gy, inv, via_e = outs[0:4], outs[4:8], outs[8:12], outs[12:15]
    bond, d02, d03, d11, d12, z12, d20, d21, z21, sb0, vd0, msg0 = outs[15:]
    part0 = facing(msg0)

    cur, cur_first, cur_last, labels = call(
        map_kernel,
        [tile, shape(8, W), shape(8, W), jax.ShapeDtypeStruct((devices * CAP,), jnp.int32)],
        [arrived],
        scratch=[
            pltpu.VMEM((devices, W), jnp.int32),
            pltpu.SMEM((devices, W), jnp.int32),
            *[buffer(rows + 8, W)] * 4,
            pltpu.SemaphoreType.DMA,
        ],
        out_specs=[pl.BlockSpec(memory_space=pltpu.VMEM)] * 3 + [SMEM],
    )
    cur_lo = shift(cur_last, "gx", 1)
    cur_hi = shift(cur_first, "gx", -1)
    top = [gx[3], gy[3], inv[3], via_e[2], bond]
    d13, z13, msg1 = call(
        first_top_kernel,
        [one, one, msg_shape],
        [d02, d03, part0, *top],
        scratch=[buffer(nr, 2 * W), buffer(side_blocks * W, W), buffer(W, W)],
        vmem=VMEM_TOP,
    )
    cur_left, cur_right = call(
        edges_kernel,
        [shape(8, side_blocks * W)] * 2,
        [cur, cur_lo, cur_hi],
        scratch=[buffer(side_blocks * W, W)],
    )
    cur_left, cur_right, msg1 = lax.optimization_barrier((cur_left, cur_right, msg1))
    part1 = facing(msg1)
    d23, z23, msg2, weight = call(
        second_top_kernel,
        [one, one, tile, tile],
        [d12, d13, z13, part1, *top],
        scratch=[buffer(nr, 2 * W), buffer(side_blocks * W, W), buffer(W, W)],
        vmem=VMEM_TOP,
    )
    cur_f_left = shift(cur_right, "yt", 1)
    cur_f_right = shift(cur_left, "yt", -1)
    v0, picked, e11, e21, ze21, d20 = call(
        effect_kernel,
        [tile, shape(devices * CAP * 8, W), one, one, tile, tile],
        [labels, cur, cur_lo, cur_hi, cur_f_left, cur_f_right,
         inv[0], gx[0], gy[0], via_e[0], inv[1], gx[1], gy[1], sb0, d20],
        scratch=[buffer(nr, 2 * W)] * 7
        + [buffer(rows, W)] * 2
        + [buffer(nr, 2 * W)] * 9
        + [buffer(W, W), buffer(rows + 8, W), pltpu.SemaphoreType.DMA((11,))],
        specs={0: SMEM} | {i: ANY for i in range(6, 15)},
        out_specs=[pl.BlockSpec(memory_space=pltpu.VMEM)] * 2
        + [ANY] * 2
        + [pl.BlockSpec(memory_space=pltpu.VMEM)] * 2,
        vmem=VMEM_EFFECT,
    )
    picked, _ = lax.optimization_barrier((picked, part1))
    part2 = facing(msg2)
    back = lax.all_to_all(picked, ALL, 0, 0, tiled=True)

    voltage = call(
        final_kernel,
        shape(layers, rows, W),
        [v0, vd0, d11, d12, z12, e11, d13, d20, d21, e21, d23, z21, ze21, z23,
         *gx[1:], *gy[1:], *inv[1:], *via_e],
        scratch=[buffer(nr, 2 * W)] * 3,
        vmem=VMEM_FINAL,
        cost=10_000_000,
    )
    whole = pl.BlockSpec(memory_space=pltpu.VMEM)
    upper = pl.BlockSpec((1, rows, W), lambda _: (layers - 1, 0, 0))
    block_voltage, voltage = pl.pallas_call(
        last_kernel,
        grid=(1,),
        out_shape=[shape(nb, 8, W), shape(layers, rows, W)],
        in_specs=[SMEM, whole, upper, whole, whole],
        out_specs=[whole, upper],
        input_output_aliases={2: 1},
        name="last_kernel",
        compiler_params=pltpu.CompilerParams(vmem_limit_bytes=58 << 20),
    )(dest, back, voltage, part2, weight)
    return voltage, block_voltage


def solution(mesh):
    tile = P(None, "gx", "yt")
    return jax.shard_map(
        on_device,
        mesh=mesh,
        in_specs=(tile, tile, tile, tile, tile, P("gx", "yt"), P(ALL, None, None), P(ALL, None), P(ALL)),
        out_specs=(tile, P(ALL, None, None)),
        check_vma=False,
    )
```

```python
import jax
import jax.numpy as jnp
from jax import lax
from jax.experimental import pallas as pl
from jax.experimental.pallas import tpu as pltpu
from jax.sharding import PartitionSpec as P

CAP = 2
BOND = 2.0
CENTER = 1.0
HALFWIDTH = 0.97
SIGMA = CENTER / HALFWIDTH
RHO0 = 1.0 / SIGMA
RHO1 = 1.0 / (2.0 * SIGMA - RHO0)
RHO2 = 1.0 / (2.0 * SIGMA - RHO1)
RHO3 = 1.0 / (2.0 * SIGMA - RHO2)
A1, B1 = RHO1 * RHO0, 2.0 * RHO1 / HALFWIDTH
A2, B2 = RHO2 * RHO1, 2.0 * RHO2 / HALFWIDTH
A3, B3 = RHO3 * RHO2, 2.0 * RHO3 / HALFWIDTH

VMEM_BASE, VMEM_TOP, VMEM_EFFECT, VMEM_FINAL = 58, 58, 58, 58

ALL = ("gx", "yt")
F32 = jnp.float32
W = 128
H = 8
PAD = 16
Q = 4
WIDE = 48
STEP = 64
ROWS_MSG = CAP * 8 + 1


def call(kernel, out, args, scratch=(), specs=None, out_specs=None, vmem=6, cost=1_000_000):
    specs = specs or {}
    in_specs = [
        specs.get(i, pl.BlockSpec(memory_space=pltpu.VMEM)) for i in range(len(args))
    ]
    many = isinstance(out, (list, tuple))
    outs = list(out) if many else [out]
    o_specs = out_specs or [pl.BlockSpec(memory_space=pltpu.VMEM)] * len(outs)
    return pl.pallas_call(
        kernel,
        out_shape=outs if many else outs[0],
        in_specs=in_specs,
        out_specs=o_specs if many else o_specs[0],
        scratch_shapes=list(scratch),
        name=kernel.__name__,
        compiler_params=pltpu.CompilerParams(vmem_limit_bytes=vmem << 20),
        cost_estimate=pl.CostEstimate(flops=cost, bytes_accessed=cost, transcendentals=0),
    )(*args)


def shape(*dims):
    return jax.ShapeDtypeStruct(dims, F32)


SMEM = pl.BlockSpec(memory_space=pltpu.SMEM)
ANY = pl.BlockSpec(memory_space=pl.ANY)
HBM = pl.BlockSpec(memory_space=pltpu.HBM)


class Copies:
    def __init__(self, sems):
        self.sems, self.made = sems, []

    def start(self, *pairs):
        begun = []
        for source, target in pairs:
            copy = pltpu.make_async_copy(source, target, self.sems.at[len(self.made)])
            copy.start()
            self.made.append(copy)
            begun.append(copy)
        return begun


def wait(copies):
    for copy in copies:
        copy.wait()


def from_right(x):
    return pltpu.roll(x, x.shape[-1] - 1, axis=1)


def from_left(x):
    return pltpu.roll(x, 1, axis=1)


def lanes(rows, width=W):
    return lax.broadcasted_iota(jnp.int32, (rows, width), 1)


def each_chunk(first, rows, body, step):
    @pl.loop(0, rows // step)
    def _(k):
        body(pl.multiple_of(first + k * step, 8))


def send_kernel(owner_ref, slot_ref, blocks_ref, out_hbm, dest_ref, count_ref, buf, slots, out_ref, sems):
    devices = count_ref.shape[0]

    @pl.loop(0, devices, unroll=8)
    def _(o):
        count_ref[o] = 0

    buf[...] = jnp.zeros_like(buf)
    slots[...] = jnp.full(slots.shape, 64, jnp.int32)
    lane = lanes(1)

    @pl.loop(0, blocks_ref.shape[0], unroll=4)
    def _(k):
        owner = owner_ref[k]
        rank = count_ref[owner]
        count_ref[owner] = rank + 1
        dest = owner * CAP + rank
        dest_ref[k] = dest
        buf[pl.ds(pl.multiple_of(dest * 8, 8), 8), :] = blocks_ref[k]
        row = slots[pl.ds(owner, 1), :]
        slots[pl.ds(owner, 1), :] = jnp.where(lane == rank, slot_ref[k], row)

    def assemble(g):
        data = buf[pl.ds(pl.multiple_of(g * CAP * 64, 8), CAP * 64), :]
        label = slots[pl.ds(pl.multiple_of(g * 8, 8), 8), :].astype(F32)
        pieces = []
        for j in range(8):
            pieces += [data[CAP * 8 * j : CAP * 8 * (j + 1)], label[j : j + 1]]
        out_ref[pl.ds(pl.multiple_of(g * ROWS_MSG * 8, 8), ROWS_MSG * 8), :] = (
            jnp.concatenate(pieces, axis=0)
        )

    copies = Copies(sems)
    groups = devices // 8 // 4
    for part in range(4):
        pl.loop(part * groups, (part + 1) * groups)(assemble)
        n = groups * 8 * ROWS_MSG
        a = pl.ds(part * n, n)
        copies.start((out_ref.at[a, :], out_hbm.at[a, :]))
    wait(copies.made)


def pack_x_kernel(*refs):
    firsts, lasts, v3 = refs[:6], refs[6:12], refs[12]
    first_out, last_out, v3_out = refs[13:]
    for group, out in ((firsts, first_out), (lasts, last_out)):
        p = 0
        for ref in group[:5]:
            n = ref.shape[0]
            out[p : p + n] = ref[...]
            p += n
        out[p] = BOND * group[5][...].astype(F32)
    v3_out[...] = v3[0]


def pack_y_kernel(v, cx, cy, st, via, mask, lo, hi, to_left, to_right):
    rows = v.shape[1]

    def pack(planes, at, n):
        lane = lanes(n)
        left = jnp.zeros((n, W), F32)
        right = jnp.zeros((n, W), F32)
        for p, x in enumerate(planes):
            turned = x if p == 0 else pltpu.roll(x, Q * p, axis=1)
            left = jnp.where(lane // Q == p, turned, left)
            right = jnp.where(lane // Q == (p - 1) % (W // Q), turned, right)
        to_left[pl.ds(at, n), :] = left
        to_right[pl.ds(at, n), :] = right

    def tile(i):
        at = pl.ds(i, STEP)
        planes = [ref[l, at, :] for ref in (v, cx, cy, st, via) for l in range(ref.shape[0])]
        planes += [BOND * mask[at, :].astype(F32)]
        pack(planes, pl.multiple_of(i + H, 8), STEP)

    each_chunk(0, rows, tile, STEP)
    count = lo.shape[0]
    pack([lo[p] for p in range(count)], 0, H)
    pack([hi[p] for p in range(count)], H + rows, H)


def rows_of(ref, l=None):
    if l is None:
        return lambda s, n: ref[pl.ds(s, n), :]
    return lambda s, n: ref[l, pl.ds(s, n), :]


def weighted(x, s, n, gx, gy):
    low = pl.multiple_of(s - 8, 8)
    near = rows_of(x)(low, n + 16)
    gnear = rows_of(gx)(low, n + 8)
    c = near[8 : 8 + n]
    g = rows_of(gy)(s, n)
    up = gnear[8 : 8 + n] * near[9 : 9 + n]
    down = (gnear * near[0 : n + 8])[7 : 7 + n]
    return up + down + g * from_right(c) + from_left(g * c)


def base_kernel(*refs):
    place, v, cx, cy, st, via, mask, vp, lo, hi, f_left, f_right = refs[:12]
    refs = list(refs[12:])
    layers, rows = v.shape[0], v.shape[1]
    total = rows + 2 * H

    def take(n):
        got = refs[:n]
        del refs[:n]
        return got

    outs = take(4 * layers + 11)
    [v3_out] = take(1)
    helds = take(4 * layers + 11)
    ev, ecx, ecy, est = take(layers), take(layers), take(layers), take(layers)
    evp, side, d00, d01, d10, z10, z11, z20, e20, sems = take(10)
    copies = Copies(sems)
    home = dict(zip(map(id, helds), outs))

    def give(*held):
        return copies.start(*[(h, home[id(h)]) for h in held])

    refs = list(helds)
    gx, gy, inv, viae = take(layers), take(layers), take(layers), take(layers - 1)
    bond, d02, d03, d11, d12, z12, d20, d21, z21, sb0, vd0, msg = take(12)
    d0 = [d00, d01, d02, d03]
    d1, z1 = [d10, d11, d12], [z10, z11, z12]
    d2, z2 = [e20, d21], [z20, z21]
    dests = [*ev, *ecx, *ecy, *est, *viae, bond]
    main, edge = slice(0, W), slice(W, 2 * W)
    sources = [ref.at[l] for ref in (v, cx, cy, st, via) for l in range(ref.shape[0])]
    arriving = copies.start(
        *[
            (source, dest.at[pl.ds(PAD, rows), pl.ds(0, W)])
            for source, dest in zip([*sources, vp], [*dests[:-1], evp])
        ]
    )

    def sides(s):
        r = pl.multiple_of(s - H, 8)
        a = f_right[pl.ds(r, WIDE), :]
        b = f_left[pl.ds(r, WIDE), :]
        even = lanes(WIDE) // Q % 2 == 0
        both = [jnp.where(even, a, b), jnp.where(even, b, a)]
        for p, dest in enumerate(dests):
            x = both[p % 2]
            dest[pl.ds(s, WIDE), edge] = x if p == 0 else pltpu.roll(x, W - Q * p, axis=1)
        evp[pl.ds(s, WIDE), edge] = jnp.zeros((WIDE, W), F32)

    each_chunk(H, total, sides, WIDE)

    def bonds(i):
        weight = BOND * mask[pl.ds(i, STEP), :].astype(F32)
        bond[pl.ds(pl.multiple_of(i + PAD, 8), STEP), main] = weight

    each_chunk(0, rows, bonds, STEP)
    for p, dest in enumerate(dests):
        dest[H : 2 * H, main] = lo[p]
        dest[PAD + rows : PAD + rows + H, main] = hi[p]
    evp[H : 2 * H, main] = jnp.zeros((H, W), F32)
    evp[PAD + rows : PAD + rows + H, main] = jnp.zeros((H, W), F32)
    wait(arriving)

    x_first, x_total, y_first, y_total = place[0], place[1], place[2], place[3]
    col = lanes(1, 2 * W)
    col = y_first + jnp.where(col < W + W // 2, col, col - 2 * W)
    nxt = lax.rem(col + 1 + y_total, y_total)
    seam = W // 2
    keep_y = jnp.where((nxt != seam) & (nxt != seam + y_total // 2), 0.5, 0.0).astype(F32)

    def conductances(s):
        row = x_first + s - PAD + lax.broadcasted_iota(jnp.int32, (WIDE, 1), 0)
        keep_x = jnp.where((row != -1) & (row != x_total - 1), 0.5, 0.0).astype(F32)
        for l in range(layers):
            c = ecx[l][pl.ds(s, WIDE + 8), :]
            gx[l][pl.ds(s, WIDE), :] = keep_x * (c[0:WIDE] + c[1 : WIDE + 1])
            c = ecy[l][pl.ds(s, WIDE), :]
            gy[l][pl.ds(s, WIDE), :] = keep_y * (c + from_right(c))

    each_chunk(H, total, conductances, WIDE)
    leaving = give(*gx, *gy, *viae, bond)
    leaving += copies.start((ev[layers - 1], v3_out))

    def start(s):
        n = WIDE
        a = pl.ds(s, n)
        for l in range(layers):
            near = gx[l][pl.ds(pl.multiple_of(s - 8, 8), n + 8), :]
            up, down, right = near[8 : 8 + n], near[7 : 7 + n], gy[l][a, :]
            off = up + down + right + from_left(right)
            nb = weighted(ev[l], s, n, gx[l], gy[l])
            if l < layers - 1:
                off = off + viae[l][a, :]
                nb = nb + viae[l][a, :] * ev[l + 1][a, :]
            else:
                off = off + bond[a, :]
                nb = nb + bond[a, :] * evp[a, :]
            if l > 0:
                off = off + viae[l - 1][a, :]
                nb = nb + viae[l - 1][a, :] * ev[l - 1][a, :]
            c = ev[l][a, :]
            inverse = 1.0 / (est[l][a, :] + off)
            inv[l][a, :] = inverse
            d0[l][a, :] = (nb - off * c) * inverse

    each_chunk(H, total, start, WIDE)
    leaving += give(*inv, d02, d03)

    def links(d, l, s, n):
        nb = weighted(d[l], s, n, gx[l], gy[l])
        if l < layers - 1:
            nb = nb + viae[l][pl.ds(s, n), :] * d[l + 1][pl.ds(s, n), :]
        if l > 0:
            nb = nb + viae[l - 1][pl.ds(s, n), :] * d[l - 1][pl.ds(s, n), :]
        return inv[l][pl.ds(s, n), :] * nb

    def first(s):
        a = pl.ds(s, WIDE)
        r = pl.ds(pl.multiple_of(s - H, 8), WIDE)
        side[r, :] = d03[a, edge]
        msg[r, :] = d03[a, main]
        for l in range(layers - 1):
            z = links(d0, l, s, WIDE)
            z1[l][a, :] = z
            d1[l][a, :] = A1 * d0[l][a, :] + B1 * z

    each_chunk(H, total, first, WIDE)
    pack_side(side, msg, total, total)
    row = total + 8 * (side.shape[0] // W)
    for product in (False, True):
        def rim(x, product=product):
            part = ev[layers - 1][x]
            return inv[layers - 1][x] * bond[x] if product else part

        msg[row : row + H, :] = rim((slice(H, 2 * H), main))
        msg[row + H : row + 2 * H, :] = rim((slice(PAD + rows, PAD + rows + H), main))

        def lay(s, rim=rim):
            side[pl.ds(pl.multiple_of(s - H, 8), WIDE), :] = rim((pl.ds(s, WIDE), edge))

        each_chunk(H, total, lay, WIDE)
        pack_side(side, msg, row + 2 * H, total)
        row += 2 * H + 8 * (side.shape[0] // W)
    leaving += give(d11, d12, z12, msg)

    def second(s):
        a = pl.ds(s, WIDE)
        for l in range(2):
            z = z1[l][a, :] - d1[l][a, :] + links(d1, l, s, WIDE)
            z2[l][a, :] = z
            d2[l][a, :] = A2 * d1[l][a, :] + B2 * z

    each_chunk(H, total, second, WIDE)
    leaving += give(d21, z21)

    def third(s):
        a = pl.ds(s, STEP)
        o = pl.ds(pl.multiple_of(s - PAD, 8), STEP)
        nb = weighted(e20, s, STEP, gx[0], gy[0])[:, main]
        nb = inv[0][a, main] * (nb + viae[0][a, main] * d21[a, main])
        d = e20[a, main]
        z = z20[a, main] - d + nb
        d20[o, :] = d
        sb0[o, :] = ev[0][a, main] + d00[a, main] + d10[a, main] + (1.0 + A3) * d + B3 * z
        for l in range(1, layers):
            vd0[l - 1, o, :] = ev[l][a, main] + d0[l][a, main]

    each_chunk(PAD, rows, third, STEP)
    leaving += give(d20, sb0, vd0)
    wait(leaving)


def pack_side(side, msg, row, total):
    for j in range(-(-total // W)):
        t = side[W * j : W * j + W, :].T
        msg[row + 8 * j : row + 8 * j + Q, :] = t[0:Q]
        msg[row + 8 * j + Q : row + 8 * j + 2 * Q, :] = t[W - Q : W]


def unpack_side(msg, row, total, u):
    blocks = []
    for j in range(-(-total // W)):
        u[0:Q, :] = msg[row + 8 * j : row + 8 * j + Q, :]
        u[W - Q : W, :] = msg[row + 8 * j + Q : row + 8 * j + 2 * Q, :]
        blocks.append((H + W * j, min(W, total - W * j), u[...].T))
    return blocks


def first_top_kernel(low, here, v3, part, gx, gy, inv, via, bond, d_out, z_out, msg, delta, d0, ep, side, u, sem):
    fetch = pltpu.make_async_copy(here, d0, sem)
    fetch.start()
    rows = part.shape[0] - 3 * (2 * H + 8 * (side.shape[0] // W))
    total = rows + 2 * H
    sides = 8 * (side.shape[0] // W)
    main, edge = slice(0, W), slice(W, 2 * W)
    u[...] = jnp.zeros_like(u)
    row = total + sides
    own = unpack_side(part, row + 2 * H, total, u)
    others = unpack_side(part, row + 2 * H + sides + 2 * H, total, u)
    theirs = unpack_side(part, total, total, u)
    fetch.wait()
    delta[PAD : PAD + rows, main] = jnp.zeros((rows, W), F32)
    ep[PAD : PAD + rows, main] = part[H : H + rows, :]

    def halo(a, cols, v_part, weight_part, d_part):
        x = inv[a, cols] * bond[a, cols] * v_part
        delta[a, cols] = x
        d0[a, cols] = d0[a, cols] + x
        ep[a, cols] = d_part + weight_part * v3[a, cols]

    for k, first in ((0, H), (1, PAD + rows)):
        at = row + H * k
        halo(
            slice(first, first + H), main, part[at : at + H, :],
            part[at + 2 * H + sides : at + 3 * H + sides, :], part[first - H : first, :],
        )
    for (first, n, a), (_, _, b), (_, _, c) in zip(own, others, theirs):
        halo(slice(first, first + n), edge, a[:n], b[:n], c[:n])

    def body(s):
        a = pl.ds(s, WIDE)
        r = pl.ds(pl.multiple_of(s - H, 8), WIDE)
        nb = weighted(d0, s, WIDE, gx, gy) + via[a, :] * low[a, :] + bond[a, :] * ep[a, :]
        x = inv[a, :] * nb
        d = A1 * d0[a, :] + B1 * x
        z_out[a, :] = x
        d_out[a, :] = d
        side[r, :] = d[:, W:]
        msg[r, :] = d[:, :W]

    each_chunk(H, total, body, WIDE)
    pack_side(side, msg, total, total)


def second_top_kernel(low, inv_low, delta, here, z, part, gx, gy, inv, via, bond, d_out, z_out, msg, weight, ep, u):
    rows = msg.shape[0]
    total = rows + 2 * H
    u[...] = jnp.zeros_like(u)
    for first, n, x in unpack_side(part, total, total, u):
        ep[first : first + n, :] = x[:n]

    def body(s):
        a = pl.ds(s, WIDE)
        r = pl.ds(pl.multiple_of(s - H, 8), WIDE)
        other = jnp.concatenate([part[r, :], ep[a, :]], axis=1)
        under = low[a, :] + B1 * inv_low[a, :] * via[a, :] * delta[a, :]
        nb = weighted(here, s, WIDE, gx, gy) + via[a, :] * under + bond[a, :] * other
        c = here[a, :]
        x = z[a, :] - c + inv[a, :] * nb
        z_out[a, :] = x
        d_out[a, :] = A2 * c + B2 * x

    each_chunk(H, total, body, WIDE)
    msg[...] = d_out[PAD : PAD + rows, 0:W]
    weight[...] = inv[PAD : PAD + rows, 0:W] * bond[PAD : PAD + rows, 0:W]


def final_kernel(
    v0, vd0, d11, b12, z12, e11, d13, d20, b21, e21, d23, z21, ze21, z23, delta,
    gx1, gx2, gx3, gy1, gy2, gy3, inv1, inv2, inv3, via0, via1, via2,
    out, d22, z22, d21, d12,
):
    main = slice(0, W)
    rows = out.shape[1]

    def amend(s):
        a = pl.ds(s, WIDE)
        c = inv2[a, :] * via2[a, :] * delta[a, :]
        z22[a, :] = z12[a, :] + c
        c = B1 * c
        d12[a, :] = b12[a, :] + c
        d21[a, :] = b21[a, :] + e21[a, :] + B2 * inv1[a, :] * via1[a, :] * c

    each_chunk(H, rows + 2 * H, amend, WIDE)

    def middle(s):
        a = pl.ds(s, WIDE)
        this = d12[a, :]
        nb = weighted(d12, s, WIDE, gx2, gy2)
        nb = nb + via1[a, :] * (d11[a, :] + e11[a, :]) + via2[a, :] * d13[a, :]
        z = z22[a, :] - this + inv2[a, :] * nb
        z22[a, :] = z
        d22[a, :] = A2 * this + B2 * z

    each_chunk(H, rows + 2 * H, middle, WIDE)
    gx, gy, inv = [None, gx1, gx2, gx3], [None, gy1, gy2, gy3], [None, inv1, inv2, inv3]
    via = [via0, via1, via2]
    d2, z2 = [None, d21, d22, d23], [None, None, z22, z23]

    def body(i):
        s = pl.multiple_of(i + PAD, 8)
        a, o = pl.ds(s, STEP), pl.ds(i, STEP)
        out[0, o, :] = v0[o, :]
        first = [None, d11[a, main] + e11[a, main], d12[a, main], d13[a, main]]
        below = d20[o, :]
        for l in range(1, 4):
            nb = weighted(d2[l], s, STEP, gx[l], gy[l])[:, main]
            nb = nb + via[l - 1][a, main] * below
            below = d2[l][a, main]
            if l < 3:
                nb = nb + via[l][a, main] * d2[l + 1][a, main]
            z = (z21[a, main] + ze21[o, :] if l == 1 else z2[l][a, main]) - below + inv[l][a, main] * nb
            out[l, o, :] = vd0[l - 1, o, :] + first[l] + (1.0 + A3) * below + B3 * z

    each_chunk(0, rows, body, STEP)


def map_kernel(arrived, out, first, last, labels, vec, lab, a0, a1, a2, a3, sem):
    devices = vec.shape[0]
    rows = out.shape[0]
    vec[...] = arrived[pl.ds(CAP * 8, devices, stride=ROWS_MSG), :].astype(jnp.int32)
    copy = pltpu.make_async_copy(vec, lab, sem)
    copy.start()
    parts = (a0, a1, a2, a3)
    for acc in parts:
        acc[...] = jnp.zeros_like(acc)
    copy.wait()

    @pl.loop(0, devices // 8)
    def _(g):
        n = ROWS_MSG * 8
        data = arrived[pl.ds(pl.multiple_of(g * n, 8), n), :]
        for j in range(8):
            for r in range(CAP):
                slot = lab[g * 8 + j, r]
                labels[(g * 8 + j) * CAP + r] = slot
                a = pl.ds(pl.multiple_of(slot * 8, 8), 8)
                acc = parts[(j * CAP + r) % 4]
                acc[a, :] += data[j * ROWS_MSG + r * 8 : j * ROWS_MSG + r * 8 + 8]

    out[...] = (a0[0:rows, :] + a1[0:rows, :]) + (a2[0:rows, :] + a3[0:rows, :])
    first[...] = out[0:8, :]
    last[...] = out[rows - 8 : rows, :]


def edges_kernel(cur, lo, hi, to_left, to_right, ext):
    rows = cur.shape[0]
    ext[0:H, :] = lo[...]
    ext[H : H + rows, :] = cur[...]
    ext[H + rows : rows + 2 * H, :] = hi[...]
    for j in range(to_left.shape[1] // W):
        t = ext[W * j : W * j + W, :].T
        to_left[:, W * j : W * j + W] = t[0:8]
        to_right[:, W * j : W * j + W] = t[W - 8 : W]


def effect_kernel(
    labels, cur, lo, hi, f_left, f_right, *refs
):
    coefficients, (v0, picked, e11_out, e21_out, z21, d20_out) = refs[:9], refs[9:15]
    held, refs = refs[15:24], refs[24:]
    inv0, gx0, gy0, via0, inv1, gx1, gy1, sb0, d20 = held
    ec, e0, e1, z10, z11, e2, z20, e11, e21, u, acc, sems = refs
    copies = Copies(sems)
    arriving = copies.start(*zip(coefficients, held))
    rows = cur.shape[0]
    total = rows + 2 * H
    main, edge = slice(0, W), slice(W, 2 * W)
    ec[H : 2 * H, main] = lo[...]
    ec[PAD : PAD + rows, main] = cur[...]
    ec[PAD + rows : PAD + rows + H, main] = hi[...]
    u[...] = jnp.zeros_like(u)
    for j in range(f_left.shape[1] // W):
        u[0:8, :] = f_right[:, W * j : W * j + W]
        u[W - 8 : W, :] = f_left[:, W * j : W * j + W]
        n = min(W, total - W * j)
        ec[H + W * j : H + W * j + n, edge] = u[...].T[:n]

    wait(arriving[0:1])

    def zeroth(s):
        a = pl.ds(s, WIDE)
        e0[a, :] = inv0[a, :] * ec[a, :]

    each_chunk(H, total, zeroth, WIDE)
    wait(arriving[1:5])

    def first(s):
        a = pl.ds(s, WIDE)
        here = e0[a, :]
        z = inv0[a, :] * weighted(e0, s, WIDE, gx0, gy0)
        z10[a, :] = z
        e1[a, :] = A1 * here + B1 * z
        z = inv1[a, :] * via0[a, :] * here
        z11[a, :] = z
        e11[a, :] = B1 * z

    each_chunk(H, total, first, WIDE)
    wait(arriving[5:7])

    def second(s):
        a = pl.ds(s, WIDE)
        low, high, between = e1[a, :], e11[a, :], via0[a, :]
        nb = weighted(e1, s, WIDE, gx0, gy0) + between * high
        z = z10[a, :] - low + inv0[a, :] * nb
        z20[a, :] = z
        e2[a, :] = A2 * low + B2 * z
        nb = weighted(e11, s, WIDE, gx1, gy1) + between * low
        z = z11[a, :] - high + inv1[a, :] * nb
        z11[a, :] = z
        e21[a, :] = A2 * high + B2 * z

    each_chunk(H, total, second, WIDE)
    leaving = copies.start((e11, e11_out), (e21, e21_out))
    wait(arriving[7:])

    def third(i):
        s = pl.multiple_of(i + PAD, 8)
        a, o = pl.ds(s, STEP), pl.ds(i, STEP)
        here = e2[a, main]
        nb = weighted(e2, s, STEP, gx0, gy0)[:, main] + via0[a, main] * e21[a, main]
        z = z20[a, main] - here + inv0[a, main] * nb
        whole = sb0[o, :] + e0[a, main] + e1[a, main] + (1.0 + A3) * here + B3 * z
        v0[o, :] = whole
        acc[o, :] = whole
        d20_out[o, :] = d20[o, :] + here
        z21[o, :] = z11[a, main]

    each_chunk(0, rows, third, STEP)
    acc[rows : rows + 8, :] = jnp.zeros((8, W), F32)

    @pl.loop(0, labels.shape[0], unroll=8)
    def _(k):
        picked[pl.ds(pl.multiple_of(k * 8, 8), 8), :] = acc[
            pl.ds(pl.multiple_of(labels[k] * 8, 8), 8), :
        ]

    wait(leaving)


def last_kernel(dest, back, field, part, weight, out, top):
    top[0] = field[0] + B3 * weight[...] * part[...]

    @pl.loop(0, out.shape[0], unroll=8)
    def _(k):
        out[k] = back[pl.ds(pl.multiple_of(dest[k] * 8, 8), 8), :]


def ring(axis, step):
    n = lax.axis_size(axis)
    return [(i, (i + step) % n) for i in range(n)]


def shift(x, axis, step):
    return lax.ppermute(x, axis, ring(axis, step))


def facing(x, step=0):
    n, m = lax.axis_size("gx"), lax.axis_size("yt")
    pairs = [
        (g * m + t, ((g + step) % n) * m + (t ^ (m // 2))) for g in range(n) for t in range(m)
    ]
    return lax.ppermute(x, ALL, pairs)


def on_device(v, st, cx, cy, via, mask, blocks, owner, slot):
    layers, rows, cols = v.shape
    devices = lax.axis_size("gx") * lax.axis_size("yt")
    nb = blocks.shape[0]
    total = rows + 2 * H
    nr = total + 2 * H
    side_blocks = -(-total // W)
    place = jnp.stack(
        [
            lax.axis_index("gx") * rows,
            jnp.int32(rows * lax.axis_size("gx")),
            lax.axis_index("yt") * cols,
            jnp.int32(cols * lax.axis_size("yt")),
        ]
    ).astype(jnp.int32)

    outgoing, dest = call(
        send_kernel,
        [shape(devices * ROWS_MSG, W), jax.ShapeDtypeStruct((nb,), jnp.int32)],
        [owner.reshape(nb), slot, blocks],
        scratch=[
            pltpu.SMEM((devices,), jnp.int32),
            pltpu.VMEM((devices * CAP * 8, W), F32),
            pltpu.VMEM((devices, W), jnp.int32),
            pltpu.VMEM((devices * ROWS_MSG, W), F32),
            pltpu.SemaphoreType.DMA((4,)),
        ],
        specs={0: SMEM, 1: SMEM},
        out_specs=[HBM, SMEM],
    )
    sources = [v, cx, cy, st, via]
    args = sources + [mask] + sources + [mask, v]
    specs = {}
    last = rows // 8 - 1
    for i in range(5):
        n = sources[i].shape[0]
        specs[i] = pl.BlockSpec((n, 8, W), lambda _: (0, 0, 0))
        specs[6 + i] = pl.BlockSpec((n, 8, W), lambda _: (0, last, 0))
    specs[5] = pl.BlockSpec((8, W), lambda _: (0, 0))
    specs[11] = pl.BlockSpec((8, W), lambda _: (last, 0))
    specs[12] = pl.BlockSpec((1, rows, W), lambda _: (layers - 1, 0, 0))
    count = 5 * layers
    first_rows, last_rows, v_top = pl.pallas_call(
        pack_x_kernel,
        grid=(1,),
        out_shape=[shape(count, 8, W)] * 2 + [shape(rows, W)],
        in_specs=[specs[i] for i in range(13)],
        out_specs=[
            pl.BlockSpec((count, 8, W), lambda _: (0, 0, 0)),
            pl.BlockSpec((count, 8, W), lambda _: (0, 0, 0)),
            pl.BlockSpec((rows, W), lambda _: (0, 0)),
        ],
        name="pack_x_kernel",
        compiler_params=pltpu.CompilerParams(vmem_limit_bytes=58 << 20),
        cost_estimate=pl.CostEstimate(flops=1, bytes_accessed=1_000_000, transcendentals=0),
    )(*args)
    lo = shift(last_rows, "gx", 1)
    hi = shift(first_rows, "gx", -1)
    lo, hi, v_top, outgoing = lax.optimization_barrier((lo, hi, v_top, outgoing))
    v_part = facing(v_top)
    tiles = [v, cx, cy, st, via, mask]
    to_left, to_right = call(
        pack_y_kernel, [shape(total, W), shape(total, W)], [*tiles, lo, hi], vmem=8
    )
    f_left = shift(to_right, "yt", 1)
    f_right = shift(to_left, "yt", -1)
    outgoing, f_left, f_right, v_part = lax.optimization_barrier(
        (outgoing, f_left, f_right, v_part)
    )
    arrived = lax.all_to_all(
        outgoing.reshape(devices, ROWS_MSG, 1, W), ALL, 0, 0, tiled=True
    ).reshape(devices * ROWS_MSG, W)

    one = shape(nr, 2 * W)
    tile = shape(rows, W)
    buffer = lambda *d: pltpu.VMEM(d, F32)
    msg_shape = shape(total + 8 * side_blocks, W)
    held = [one] * (4 * layers + 5)
    msg0_shape = shape(3 * (total + 8 * side_blocks) - 2 * rows, W)
    held += [tile, one, one, tile, shape(layers - 1, rows, W), msg0_shape]
    outs = call(
        base_kernel,
        [*held, one],
        [place, *tiles, v_part, lo, hi, f_left, f_right],
        scratch=[buffer(*h.shape) for h in held]
        + [buffer(nr, 2 * W)] * (4 * layers + 1)
        + [buffer(side_blocks * W, W)]
        + [buffer(nr, 2 * W)] * 7
        + [pltpu.SemaphoreType.DMA((9 * layers + 20,))],
        specs={0: SMEM, 1: ANY, 2: ANY, 3: ANY, 4: ANY, 5: ANY, 7: ANY},
        out_specs=[ANY] * (len(held) + 1),
        vmem=VMEM_BASE,
        cost=20_000_000,
    )
    gx, gy, inv, via_e = outs[0:4], outs[4:8], outs[8:12], outs[12:15]
    bond, d02, d03, d11, d12, z12, d20, d21, z21, sb0, vd0, msg0, v3 = outs[15:]
    part0 = facing(msg0)

    cur, cur_first, cur_last, labels = call(
        map_kernel,
        [tile, shape(8, W), shape(8, W), jax.ShapeDtypeStruct((devices * CAP,), jnp.int32)],
        [arrived],
        scratch=[
            pltpu.VMEM((devices, W), jnp.int32),
            pltpu.SMEM((devices, W), jnp.int32),
            *[buffer(rows + 8, W)] * 4,
            pltpu.SemaphoreType.DMA,
        ],
        out_specs=[pl.BlockSpec(memory_space=pltpu.VMEM)] * 3 + [SMEM],
    )
    cur_lo = shift(cur_last, "gx", 1)
    cur_hi = shift(cur_first, "gx", -1)
    top = [gx[3], gy[3], inv[3], via_e[2], bond]
    cur_left, cur_right = call(
        edges_kernel,
        [shape(8, side_blocks * W)] * 2,
        [cur, cur_lo, cur_hi],
        scratch=[buffer(side_blocks * W, W)],
    )
    cur_left, cur_right, part0 = lax.optimization_barrier((cur_left, cur_right, part0))
    d13, z13, msg1, delta = call(
        first_top_kernel,
        [one, one, msg_shape, one],
        [d02, d03, v3, part0, *top],
        scratch=[buffer(nr, 2 * W)] * 2
        + [buffer(side_blocks * W, W), buffer(W, W), pltpu.SemaphoreType.DMA],
        specs={1: ANY},
        vmem=VMEM_TOP,
    )
    part1 = facing(msg1)
    d23, z23, msg2, weight = call(
        second_top_kernel,
        [one, one, tile, tile],
        [d12, inv[2], delta, d13, z13, part1, *top],
        scratch=[buffer(nr, W), buffer(W, W)],
        vmem=VMEM_TOP,
    )

    cur_f_left = shift(cur_right, "yt", 1)
    cur_f_right = shift(cur_left, "yt", -1)
    v0, picked, e11, e21, ze21, d20 = call(
        effect_kernel,
        [tile, shape(devices * CAP * 8, W), one, one, tile, tile],
        [labels, cur, cur_lo, cur_hi, cur_f_left, cur_f_right,
         inv[0], gx[0], gy[0], via_e[0], inv[1], gx[1], gy[1], sb0, d20],
        scratch=[buffer(nr, 2 * W)] * 7
        + [buffer(rows, W)] * 2
        + [buffer(nr, 2 * W)] * 9
        + [buffer(W, W), buffer(rows + 8, W), pltpu.SemaphoreType.DMA((11,))],
        specs={0: SMEM} | {i: ANY for i in range(6, 15)},
        out_specs=[pl.BlockSpec(memory_space=pltpu.VMEM)] * 2
        + [ANY] * 2
        + [pl.BlockSpec(memory_space=pltpu.VMEM)] * 2,
        vmem=VMEM_EFFECT,
    )
    picked, part1 = lax.optimization_barrier((picked, part1))
    part2 = facing(msg2)
    back = lax.all_to_all(picked, ALL, 0, 0, tiled=True)

    voltage = call(
        final_kernel,
        shape(layers, rows, W),
        [v0, vd0, d11, d12, z12, e11, d13, d20, d21, e21, d23, z21, ze21, z23, delta,
         *gx[1:], *gy[1:], *inv[1:], *via_e],
        scratch=[buffer(nr, 2 * W)] * 4,
        vmem=VMEM_FINAL,
        cost=10_000_000,
    )
    whole = pl.BlockSpec(memory_space=pltpu.VMEM)
    upper = pl.BlockSpec((1, rows, W), lambda _: (layers - 1, 0, 0))
    block_voltage, voltage = pl.pallas_call(
        last_kernel,
        grid=(1,),
        out_shape=[shape(nb, 8, W), shape(layers, rows, W)],
        in_specs=[SMEM, whole, upper, whole, whole],
        out_specs=[whole, upper],
        input_output_aliases={2: 1},
        name="last_kernel",
        compiler_params=pltpu.CompilerParams(vmem_limit_bytes=58 << 20),
    )(dest, back, voltage, part2, weight)
    return voltage, block_voltage


def solution(mesh):
    tile = P(None, "gx", "yt")
    return jax.shard_map(
        on_device,
        mesh=mesh,
        in_specs=(tile, tile, tile, tile, tile, P("gx", "yt"), P(ALL, None, None), P(ALL, None), P(ALL)),
        out_specs=(tile, P(ALL, None, None)),
        check_vma=False,
    )
```

```python
import jax
import jax.numpy as jnp
from jax import lax
from jax.experimental import pallas as pl
from jax.experimental.pallas import tpu as pltpu
from jax.sharding import PartitionSpec as P

CAP = 2
TAIL = 24
BOND = 2.0
CENTER = 1.0
HALFWIDTH = 0.97
SIGMA = CENTER / HALFWIDTH
RHO0 = 1.0 / SIGMA
RHO1 = 1.0 / (2.0 * SIGMA - RHO0)
RHO2 = 1.0 / (2.0 * SIGMA - RHO1)
RHO3 = 1.0 / (2.0 * SIGMA - RHO2)
A1, B1 = RHO1 * RHO0, 2.0 * RHO1 / HALFWIDTH
A2, B2 = RHO2 * RHO1, 2.0 * RHO2 / HALFWIDTH
A3, B3 = RHO3 * RHO2, 2.0 * RHO3 / HALFWIDTH

VMEM_BASE, VMEM_TOP, VMEM_EFFECT, VMEM_FINAL = 58, 20, 16, 58

ALL = ("gx", "yt")
F32 = jnp.float32
W = 128
H = 8
PAD = 16
Q = 4
WIDE = 48
STEP = 64
ROWS_MSG = CAP * 8 + 1


def call(kernel, out, args, scratch=(), specs=None, out_specs=None, vmem=6, cost=1_000_000, far=()):
    specs = specs or {}
    in_specs = [
        specs.get(i, pl.BlockSpec(memory_space=pltpu.VMEM)) for i in range(len(args))
    ]
    args = [
        pltpu.with_memory_space_constraint(x, pltpu.HBM) if i in far else x
        for i, x in enumerate(args)
    ]
    many = isinstance(out, (list, tuple))
    outs = list(out) if many else [out]
    o_specs = out_specs or [pl.BlockSpec(memory_space=pltpu.VMEM)] * len(outs)
    return pl.pallas_call(
        kernel,
        out_shape=outs if many else outs[0],
        in_specs=in_specs,
        out_specs=o_specs if many else o_specs[0],
        scratch_shapes=list(scratch),
        name=kernel.__name__,
        compiler_params=pltpu.CompilerParams(vmem_limit_bytes=vmem << 20),
        cost_estimate=pl.CostEstimate(flops=cost, bytes_accessed=cost, transcendentals=0),
    )(*args)


def shape(*dims):
    return jax.ShapeDtypeStruct(dims, F32)


SMEM = pl.BlockSpec(memory_space=pltpu.SMEM)
ANY = pl.BlockSpec(memory_space=pl.ANY)
HBM = pl.BlockSpec(memory_space=pltpu.HBM)


class Copies:
    def __init__(self, sems):
        self.sems, self.made = sems, []

    def start(self, *pairs):
        begun = []
        for source, target in pairs:
            copy = pltpu.make_async_copy(source, target, self.sems.at[len(self.made)])
            copy.start()
            self.made.append(copy)
            begun.append(copy)
        return begun


def wait(copies):
    for copy in copies:
        copy.wait()


def from_right(x):
    return pltpu.roll(x, x.shape[-1] - 1, axis=1)


def from_left(x):
    return pltpu.roll(x, 1, axis=1)


def lanes(rows, width=W):
    return lax.broadcasted_iota(jnp.int32, (rows, width), 1)


def each_chunk(first, rows, body, step):
    @pl.loop(0, rows // step)
    def _(k):
        body(pl.multiple_of(first + k * step, 8))


def send_kernel(owner_ref, slot_ref, blocks_ref, out_hbm, dest_ref, count_ref, buf, slots, out_ref, sems):
    devices = count_ref.shape[0]

    @pl.loop(0, devices, unroll=8)
    def _(o):
        count_ref[o] = 0

    buf[...] = jnp.zeros_like(buf)
    slots[...] = jnp.full(slots.shape, 64, jnp.int32)
    lane = lanes(1)

    @pl.loop(0, blocks_ref.shape[0], unroll=4)
    def _(k):
        owner = owner_ref[k]
        rank = count_ref[owner]
        count_ref[owner] = rank + 1
        dest = owner * CAP + rank
        dest_ref[k] = dest
        buf[pl.ds(pl.multiple_of(dest * 8, 8), 8), :] = blocks_ref[k]
        row = slots[pl.ds(owner, 1), :]
        slots[pl.ds(owner, 1), :] = jnp.where(lane == rank, slot_ref[k], row)

    def assemble(g):
        data = buf[pl.ds(pl.multiple_of(g * CAP * 64, 8), CAP * 64), :]
        label = slots[pl.ds(pl.multiple_of(g * 8, 8), 8), :].astype(F32)
        pieces = []
        for j in range(8):
            pieces += [data[CAP * 8 * j : CAP * 8 * (j + 1)], label[j : j + 1]]
        out_ref[pl.ds(pl.multiple_of(g * ROWS_MSG * 8, 8), ROWS_MSG * 8), :] = (
            jnp.concatenate(pieces, axis=0)
        )

    copies = Copies(sems)
    groups = devices // 8 // 4
    for part in range(4):
        pl.loop(part * groups, (part + 1) * groups)(assemble)
        n = groups * 8 * ROWS_MSG
        a = pl.ds(part * n, n)
        copies.start((out_ref.at[a, :], out_hbm.at[a, :]))
    wait(copies.made)


def pack_x_kernel(*refs):
    firsts, lasts, v3 = refs[:6], refs[6:12], refs[12]
    first_out, last_out, v3_out = refs[13:]
    for group, out in ((firsts, first_out), (lasts, last_out)):
        p = 0
        for ref in group[:5]:
            n = ref.shape[0]
            out[p : p + n] = ref[...]
            p += n
        out[p] = BOND * group[5][...].astype(F32)
    rows = v3.shape[1]
    v3_out[0:rows, :] = v3[0]
    v3_out[rows:, :] = jnp.zeros((v3_out.shape[0] - rows, W), F32)


def pack_y_kernel(v, cx, cy, st, via, mask, lo, hi, to_left, to_right):
    rows = v.shape[1]

    def pack(planes, at, n):
        lane = lanes(n)
        left = jnp.zeros((n, W), F32)
        right = jnp.zeros((n, W), F32)
        for p, x in enumerate(planes):
            turned = x if p == 0 else pltpu.roll(x, Q * p, axis=1)
            left = jnp.where(lane // Q == p, turned, left)
            right = jnp.where(lane // Q == (p - 1) % (W // Q), turned, right)
        to_left[pl.ds(at, n), :] = left
        to_right[pl.ds(at, n), :] = right

    def tile(i):
        at = pl.ds(i, STEP)
        planes = [ref[l, at, :] for ref in (v, cx, cy, st, via) for l in range(ref.shape[0])]
        planes += [BOND * mask[at, :].astype(F32)]
        pack(planes, pl.multiple_of(i + H, 8), STEP)

    each_chunk(0, rows, tile, STEP)
    count = lo.shape[0]
    pack([lo[p] for p in range(count)], 0, H)
    pack([hi[p] for p in range(count)], H + rows, H)


def rows_of(ref, l=None):
    if l is None:
        return lambda s, n: ref[pl.ds(s, n), :]
    return lambda s, n: ref[l, pl.ds(s, n), :]


def weighted(x, s, n, gx, gy):
    low = pl.multiple_of(s - 8, 8)
    near = rows_of(x)(low, n + 16)
    gnear = rows_of(gx)(low, n + 8)
    c = near[8 : 8 + n]
    g = rows_of(gy)(s, n)
    up = gnear[8 : 8 + n] * near[9 : 9 + n]
    down = (gnear * near[0 : n + 8])[7 : 7 + n]
    return up + down + g * from_right(c) + from_left(g * c)


def base_kernel(*refs):
    place, v, cx, cy, st, via, mask, vp, lo, hi, f_left, f_right = refs[:12]
    refs = list(refs[12:])
    layers, rows = v.shape[0], v.shape[1]
    total = rows + 2 * H

    def take(n):
        got = refs[:n]
        del refs[:n]
        return got

    outs = take(4 * layers + 11)
    [v3_out] = take(1)
    helds = take(4 * layers + 11)
    ev, ecx, ecy, est = take(layers), take(layers), take(layers), take(layers)
    evp, side, d00, d01, d10, z10, z11, z20, e20, sems = take(10)
    copies = Copies(sems)
    home = dict(zip(map(id, helds), outs))

    def give(*held):
        return copies.start(*[(h, home[id(h)]) for h in held])

    refs = list(helds)
    gx, gy, inv, viae = take(layers), take(layers), take(layers), take(layers - 1)
    bond, d02, d03, d11, d12, z12, d20, d21, z21, sb0, vd0, msg = take(12)
    d0 = [d00, d01, d02, d03]
    d1, z1 = [d10, d11, d12], [z10, z11, z12]
    d2, z2 = [e20, d21], [z20, z21]
    dests = [*ev, *ecx, *ecy, *est, *viae, bond]
    main, edge = slice(0, W), slice(W, 2 * W)
    sources = [ref.at[l] for ref in (v, cx, cy, st, via) for l in range(ref.shape[0])]
    arriving = copies.start(
        *[
            (source, dest.at[pl.ds(PAD, rows), pl.ds(0, W)])
            for source, dest in zip([*sources, vp.at[pl.ds(0, rows), :]], [*dests[:-1], evp])
        ]
    )

    def sides(s):
        r = pl.multiple_of(s - H, 8)
        a = f_right[pl.ds(r, WIDE), :]
        b = f_left[pl.ds(r, WIDE), :]
        even = lanes(WIDE) // Q % 2 == 0
        both = [jnp.where(even, a, b), jnp.where(even, b, a)]
        for p, dest in enumerate(dests):
            x = both[p % 2]
            dest[pl.ds(s, WIDE), edge] = x if p == 0 else pltpu.roll(x, W - Q * p, axis=1)
        evp[pl.ds(s, WIDE), edge] = jnp.zeros((WIDE, W), F32)

    each_chunk(H, total, sides, WIDE)

    def bonds(i):
        weight = BOND * mask[pl.ds(i, STEP), :].astype(F32)
        bond[pl.ds(pl.multiple_of(i + PAD, 8), STEP), main] = weight

    each_chunk(0, rows, bonds, STEP)
    for p, dest in enumerate(dests):
        dest[H : 2 * H, main] = lo[p]
        dest[PAD + rows : PAD + rows + H, main] = hi[p]
    evp[H : 2 * H, main] = jnp.zeros((H, W), F32)
    evp[PAD + rows : PAD + rows + H, main] = jnp.zeros((H, W), F32)
    wait(arriving)

    x_first, x_total, y_first, y_total = place[0], place[1], place[2], place[3]
    col = lanes(1, 2 * W)
    col = y_first + jnp.where(col < W + W // 2, col, col - 2 * W)
    nxt = lax.rem(col + 1 + y_total, y_total)
    seam = W // 2
    keep_y = jnp.where((nxt != seam) & (nxt != seam + y_total // 2), 0.5, 0.0).astype(F32)

    def conductances(s):
        row = x_first + s - PAD + lax.broadcasted_iota(jnp.int32, (WIDE, 1), 0)
        keep_x = jnp.where((row != -1) & (row != x_total - 1), 0.5, 0.0).astype(F32)
        for l in range(layers):
            c = ecx[l][pl.ds(s, WIDE + 8), :]
            gx[l][pl.ds(s, WIDE), :] = keep_x * (c[0:WIDE] + c[1 : WIDE + 1])
            c = ecy[l][pl.ds(s, WIDE), :]
            gy[l][pl.ds(s, WIDE), :] = keep_y * (c + from_right(c))

    each_chunk(H, total, conductances, WIDE)
    leaving = give(*gx, *gy, *viae, bond)
    leaving += copies.start((ev[layers - 1], v3_out))

    def start(s):
        n = WIDE
        a = pl.ds(s, n)
        for l in range(layers):
            near = gx[l][pl.ds(pl.multiple_of(s - 8, 8), n + 8), :]
            up, down, right = near[8 : 8 + n], near[7 : 7 + n], gy[l][a, :]
            off = up + down + right + from_left(right)
            nb = weighted(ev[l], s, n, gx[l], gy[l])
            if l < layers - 1:
                off = off + viae[l][a, :]
                nb = nb + viae[l][a, :] * ev[l + 1][a, :]
            else:
                off = off + bond[a, :]
                nb = nb + bond[a, :] * evp[a, :]
            if l > 0:
                off = off + viae[l - 1][a, :]
                nb = nb + viae[l - 1][a, :] * ev[l - 1][a, :]
            c = ev[l][a, :]
            inverse = 1.0 / (est[l][a, :] + off)
            inv[l][a, :] = inverse
            d0[l][a, :] = (nb - off * c) * inverse

    each_chunk(H, total, start, WIDE)
    leaving += give(*inv, d02, d03)

    def links(d, l, s, n):
        nb = weighted(d[l], s, n, gx[l], gy[l])
        if l < layers - 1:
            nb = nb + viae[l][pl.ds(s, n), :] * d[l + 1][pl.ds(s, n), :]
        if l > 0:
            nb = nb + viae[l - 1][pl.ds(s, n), :] * d[l - 1][pl.ds(s, n), :]
        return inv[l][pl.ds(s, n), :] * nb

    def first(s):
        a = pl.ds(s, WIDE)
        r = pl.ds(pl.multiple_of(s - H, 8), WIDE)
        side[r, :] = d03[a, edge]
        msg[r, :] = d03[a, main]
        for l in range(layers - 1):
            z = links(d0, l, s, WIDE)
            z1[l][a, :] = z
            d1[l][a, :] = A1 * d0[l][a, :] + B1 * z

    each_chunk(H, total, first, WIDE)
    pack_side(side, msg, total, total)
    row = total + 8 * (side.shape[0] // W)
    for product in (False, True):
        def rim(x, product=product):
            part = ev[layers - 1][x]
            return inv[layers - 1][x] * bond[x] if product else part

        msg[row : row + H, :] = rim((slice(H, 2 * H), main))
        msg[row + H : row + 2 * H, :] = rim((slice(PAD + rows, PAD + rows + H), main))

        def lay(s, rim=rim):
            side[pl.ds(pl.multiple_of(s - H, 8), WIDE), :] = rim((pl.ds(s, WIDE), edge))

        each_chunk(H, total, lay, WIDE)
        pack_side(side, msg, row + 2 * H, total)
        row += 2 * H + 8 * (side.shape[0] // W)
    leaving += give(d11, d12, z12, msg)

    def second(s):
        a = pl.ds(s, WIDE)
        for l in range(2):
            z = z1[l][a, :] - d1[l][a, :] + links(d1, l, s, WIDE)
            z2[l][a, :] = z
            d2[l][a, :] = A2 * d1[l][a, :] + B2 * z

    each_chunk(H, total, second, WIDE)
    leaving += give(d21, z21)

    def third(s):
        a = pl.ds(s, STEP)
        o = pl.ds(pl.multiple_of(s - PAD, 8), STEP)
        nb = weighted(e20, s, STEP, gx[0], gy[0])[:, main]
        nb = inv[0][a, main] * (nb + viae[0][a, main] * d21[a, main])
        d = e20[a, main]
        z = z20[a, main] - d + nb
        d20[o, :] = d
        sb0[o, :] = ev[0][a, main] + d00[a, main] + d10[a, main] + (1.0 + A3) * d + B3 * z
        for l in range(1, layers):
            vd0[l - 1, o, :] = ev[l][a, main] + d0[l][a, main]

    each_chunk(PAD, rows, third, STEP)
    leaving += give(d20, sb0, vd0)
    wait(leaving)


def pack_side(side, msg, row, total):
    for j in range(-(-total // W)):
        t = side[W * j : W * j + W, :].T
        msg[row + 8 * j : row + 8 * j + Q, :] = t[0:Q]
        msg[row + 8 * j + Q : row + 8 * j + 2 * Q, :] = t[W - Q : W]


def unpack_side(msg, row, total, u):
    blocks = []
    for j in range(-(-total // W)):
        u[0:Q, :] = msg[row + 8 * j : row + 8 * j + Q, :]
        u[W - Q : W, :] = msg[row + 8 * j + Q : row + 8 * j + 2 * Q, :]
        blocks.append((H + W * j, min(W, total - W * j), u[...].T))
    return blocks


def first_top_kernel(part, *refs):
    inputs, (d_hbm, z_hbm, delta_hbm, msg), held = refs[:8], refs[8:12], refs[12:20]
    low, d0, v3, gx, gy, inv, via, bond = held
    d_out, z_out, delta, ep, side, u, sems = refs[20:]
    copies = Copies(sems)
    arriving = copies.start(*zip(inputs, held))
    rows = part.shape[0] - 3 * (2 * H + 8 * (side.shape[0] // W))
    total = rows + 2 * H
    sides = 8 * (side.shape[0] // W)
    main, edge = slice(0, W), slice(W, 2 * W)
    u[...] = jnp.zeros_like(u)
    row = total + sides
    own = unpack_side(part, row + 2 * H, total, u)
    others = unpack_side(part, row + 2 * H + sides + 2 * H, total, u)
    theirs = unpack_side(part, total, total, u)
    wait(arriving)
    delta[PAD : PAD + rows, main] = jnp.zeros((rows, W), F32)
    ep[PAD : PAD + rows, main] = part[H : H + rows, :]

    def halo(a, cols, v_part, weight_part, d_part):
        x = inv[a, cols] * bond[a, cols] * v_part
        delta[a, cols] = x
        d0[a, cols] = d0[a, cols] + x
        ep[a, cols] = d_part + weight_part * v3[a, cols]

    for k, first in ((0, H), (1, PAD + rows)):
        at = row + H * k
        halo(
            slice(first, first + H), main, part[at : at + H, :],
            part[at + 2 * H + sides : at + 3 * H + sides, :], part[first - H : first, :],
        )
    for (first, n, a), (_, _, b), (_, _, c) in zip(own, others, theirs):
        halo(slice(first, first + n), edge, a[:n], b[:n], c[:n])

    def body(s):
        a = pl.ds(s, WIDE)
        r = pl.ds(pl.multiple_of(s - H, 8), WIDE)
        nb = weighted(d0, s, WIDE, gx, gy) + via[a, :] * low[a, :] + bond[a, :] * ep[a, :]
        x = inv[a, :] * nb
        d = A1 * d0[a, :] + B1 * x
        z_out[a, :] = x
        d_out[a, :] = d
        side[r, :] = d[:, W:]
        msg[r, :] = d[:, :W]

    each_chunk(H, total, body, WIDE)
    leaving = copies.start((d_out, d_hbm), (z_out, z_hbm), (delta, delta_hbm))
    pack_side(side, msg, total, total)
    wait(leaving)


def second_top_kernel(low, inv_low, delta, here, z, part, gx, gy, inv, via, bond, d_out, z_out, msg, weight, ep, u):
    rows = msg.shape[0]
    total = rows + 2 * H
    u[...] = jnp.zeros_like(u)
    for first, n, x in unpack_side(part, total, total, u):
        ep[first : first + n, :] = x[:n]

    def body(s):
        a = pl.ds(s, WIDE)
        r = pl.ds(pl.multiple_of(s - H, 8), WIDE)
        other = jnp.concatenate([part[r, :], ep[a, :]], axis=1)
        under = low[a, :] + B1 * inv_low[a, :] * via[a, :] * delta[a, :]
        nb = weighted(here, s, WIDE, gx, gy) + via[a, :] * under + bond[a, :] * other
        c = here[a, :]
        x = z[a, :] - c + inv[a, :] * nb
        z_out[a, :] = x
        d_out[a, :] = A2 * c + B2 * x

    each_chunk(H, total, body, WIDE)
    msg[...] = d_out[PAD : PAD + rows, 0:W]
    weight[...] = inv[PAD : PAD + rows, 0:W] * bond[PAD : PAD + rows, 0:W]


def final_kernel(
    v0, vd0, d11, b12, z12, e11, d13, d20, b21, e21, d23, z21, ze21, z23, delta,
    gx1, gx2, gx3, gy1, gy2, gy3, inv1, inv2, inv3, via0, via1, via2,
    out, d22, z22, d21, d12,
):
    main = slice(0, W)
    rows = out.shape[1]

    def amend(s):
        a = pl.ds(s, WIDE)
        c = inv2[a, :] * via2[a, :] * delta[a, :]
        z22[a, :] = z12[a, :] + c
        c = B1 * c
        d12[a, :] = b12[a, :] + c
        d21[a, :] = b21[a, :] + e21[a, :] + B2 * inv1[a, :] * via1[a, :] * c

    each_chunk(H, rows + 2 * H, amend, WIDE)

    def middle(s):
        a = pl.ds(s, WIDE)
        this = d12[a, :]
        nb = weighted(d12, s, WIDE, gx2, gy2)
        nb = nb + via1[a, :] * (d11[a, :] + e11[a, :]) + via2[a, :] * d13[a, :]
        z = z22[a, :] - this + inv2[a, :] * nb
        z22[a, :] = z
        d22[a, :] = A2 * this + B2 * z

    each_chunk(H, rows + 2 * H, middle, WIDE)
    gx, gy, inv = [None, gx1, gx2, gx3], [None, gy1, gy2, gy3], [None, inv1, inv2, inv3]
    via = [via0, via1, via2]
    d2, z2 = [None, d21, d22, d23], [None, None, z22, z23]

    def body(i):
        s = pl.multiple_of(i + PAD, 8)
        a, o = pl.ds(s, STEP), pl.ds(i, STEP)
        out[0, o, :] = v0[o, :]
        first = [None, d11[a, main] + e11[a, main], d12[a, main], d13[a, main]]
        below = d20[o, :]
        for l in range(1, 4):
            nb = weighted(d2[l], s, STEP, gx[l], gy[l])[:, main]
            nb = nb + via[l - 1][a, main] * below
            below = d2[l][a, main]
            if l < 3:
                nb = nb + via[l][a, main] * d2[l + 1][a, main]
            z = (z21[a, main] + ze21[o, :] if l == 1 else z2[l][a, main]) - below + inv[l][a, main] * nb
            out[l, o, :] = vd0[l - 1, o, :] + first[l] + (1.0 + A3) * below + B3 * z

    each_chunk(0, rows, body, STEP)


def map_kernel(arrived, out, first, last, labels, vec, lab, a0, a1, a2, a3, sem):
    devices = vec.shape[0]
    rows = out.shape[0]
    vec[...] = arrived[pl.ds(CAP * 8, devices, stride=ROWS_MSG), :].astype(jnp.int32)
    copy = pltpu.make_async_copy(vec, lab, sem)
    copy.start()
    parts = (a0, a1, a2, a3)
    for acc in parts:
        acc[...] = jnp.zeros_like(acc)
    copy.wait()

    @pl.loop(0, devices // 8)
    def _(g):
        n = ROWS_MSG * 8
        data = arrived[pl.ds(pl.multiple_of(g * n, 8), n), :]
        for j in range(8):
            for r in range(CAP):
                slot = lab[g * 8 + j, r]
                labels[(g * 8 + j) * CAP + r] = slot
                a = pl.ds(pl.multiple_of(slot * 8, 8), 8)
                acc = parts[(j * CAP + r) % 4]
                acc[a, :] += data[j * ROWS_MSG + r * 8 : j * ROWS_MSG + r * 8 + 8]

    out[...] = (a0[0:rows, :] + a1[0:rows, :]) + (a2[0:rows, :] + a3[0:rows, :])
    first[...] = out[0:8, :]
    last[...] = out[rows - 8 : rows, :]


def edges_kernel(cur, lo, hi, to_left, to_right, ext):
    rows = cur.shape[0]
    ext[0:H, :] = lo[...]
    ext[H : H + rows, :] = cur[...]
    ext[H + rows : rows + 2 * H, :] = hi[...]
    for j in range(to_left.shape[1] // W):
        t = ext[W * j : W * j + W, :].T
        to_left[:, W * j : W * j + W] = t[0:8]
        to_right[:, W * j : W * j + W] = t[W - 8 : W]


def effect_kernel(
    labels, cur, lo, hi, f_left, f_right, *refs
):
    (inv0, gx0, gy0, via0, inv1, gx1, gy1, sb0, d20), refs = refs[:9], refs[9:]
    v0_out, picked_out, e11_out, e21_out, z21_out, d20_out = refs[:6]
    ec, e0, e1, z10, z11, e2, z20, e11, e21, u, acc, z21, d20_sum, picked, sems = refs[6:]
    copies = Copies(sems)
    rows = cur.shape[0]
    total = rows + 2 * H
    main, edge = slice(0, W), slice(W, 2 * W)
    ec[H : 2 * H, main] = lo[...]
    ec[PAD : PAD + rows, main] = cur[...]
    ec[PAD + rows : PAD + rows + H, main] = hi[...]
    u[...] = jnp.zeros_like(u)
    for j in range(f_left.shape[1] // W):
        u[0:8, :] = f_right[:, W * j : W * j + W]
        u[W - 8 : W, :] = f_left[:, W * j : W * j + W]
        n = min(W, total - W * j)
        ec[H + W * j : H + W * j + n, edge] = u[...].T[:n]

    def zeroth(s):
        a = pl.ds(s, WIDE)
        e0[a, :] = inv0[a, :] * ec[a, :]

    each_chunk(H, total, zeroth, WIDE)
    def first(s):
        a = pl.ds(s, WIDE)
        here = e0[a, :]
        z = inv0[a, :] * weighted(e0, s, WIDE, gx0, gy0)
        z10[a, :] = z
        e1[a, :] = A1 * here + B1 * z
        z = inv1[a, :] * via0[a, :] * here
        z11[a, :] = z
        e11[a, :] = B1 * z

    each_chunk(H, total, first, WIDE)
    def second(s):
        a = pl.ds(s, WIDE)
        low, high, between = e1[a, :], e11[a, :], via0[a, :]
        nb = weighted(e1, s, WIDE, gx0, gy0) + between * high
        z = z10[a, :] - low + inv0[a, :] * nb
        z20[a, :] = z
        e2[a, :] = A2 * low + B2 * z
        nb = weighted(e11, s, WIDE, gx1, gy1) + between * low
        z = z11[a, :] - high + inv1[a, :] * nb
        z11[a, :] = z
        e21[a, :] = A2 * high + B2 * z

    each_chunk(H, total, second, WIDE)
    copies.start((e11, e11_out), (e21, e21_out))
    def third(i):
        s = pl.multiple_of(i + PAD, 8)
        a, o = pl.ds(s, STEP), pl.ds(i, STEP)
        here = e2[a, main]
        nb = weighted(e2, s, STEP, gx0, gy0)[:, main] + via0[a, main] * e21[a, main]
        z = z20[a, main] - here + inv0[a, main] * nb
        whole = sb0[o, :] + e0[a, main] + e1[a, main] + (1.0 + A3) * here + B3 * z
        acc[o, :] = whole
        d20_sum[o, :] = d20[o, :] + here
        z21[o, :] = z11[a, main]

    each_chunk(0, rows, third, STEP)
    copies.start((acc.at[pl.ds(0, rows), :], v0_out), (z21, z21_out), (d20_sum, d20_out))
    acc[rows : rows + 8, :] = jnp.zeros((8, W), F32)

    def pick(k):
        picked[pl.ds(pl.multiple_of(k * 8, 8), 8), :] = acc[
            pl.ds(pl.multiple_of(labels[k] * 8, 8), 8), :
        ]

    count = labels.shape[0] // 4
    for part in range(4):
        pl.loop(part * count, (part + 1) * count, unroll=8)(pick)
        a = pl.ds(part * count * 8, count * 8)
        copies.start((picked.at[a, :], picked_out.at[a, :]))
    wait(copies.made)


def last_kernel(dest, back, field, part, weight, out, top):
    top[0] = field[0] + B3 * weight[...] * part[...]

    @pl.loop(0, out.shape[0], unroll=8)
    def _(k):
        out[k] = back[pl.ds(pl.multiple_of(dest[k] * 8, 8), 8), :]


def ring(axis, step):
    n = lax.axis_size(axis)
    return [(i, (i + step) % n) for i in range(n)]


def shift(x, axis, step):
    return lax.ppermute(x, axis, ring(axis, step))


def facing(x, step=0):
    n, m = lax.axis_size("gx"), lax.axis_size("yt")
    pairs = [
        (g * m + t, ((g + step) % n) * m + (t ^ (m // 2))) for g in range(n) for t in range(m)
    ]
    return lax.ppermute(x, ALL, pairs)


def on_device(v, st, cx, cy, via, mask, blocks, owner, slot):
    layers, rows, cols = v.shape
    devices = lax.axis_size("gx") * lax.axis_size("yt")
    nb = blocks.shape[0]
    total = rows + 2 * H
    nr = total + 2 * H
    side_blocks = -(-total // W)
    place = jnp.stack(
        [
            lax.axis_index("gx") * rows,
            jnp.int32(rows * lax.axis_size("gx")),
            lax.axis_index("yt") * cols,
            jnp.int32(cols * lax.axis_size("yt")),
        ]
    ).astype(jnp.int32)

    outgoing, dest = call(
        send_kernel,
        [pltpu.HBM((devices * ROWS_MSG, W), F32), jax.ShapeDtypeStruct((nb,), jnp.int32)],
        [owner.reshape(nb), slot, blocks],
        scratch=[
            pltpu.SMEM((devices,), jnp.int32),
            pltpu.VMEM((devices * CAP * 8, W), F32),
            pltpu.VMEM((devices, W), jnp.int32),
            pltpu.VMEM((devices * ROWS_MSG, W), F32),
            pltpu.SemaphoreType.DMA((4,)),
        ],
        specs={0: SMEM, 1: SMEM},
        out_specs=[HBM, SMEM],
    )
    sources = [v, cx, cy, st, via]
    args = sources + [mask] + sources + [mask, v]
    specs = {}
    last = rows // 8 - 1
    for i in range(5):
        n = sources[i].shape[0]
        specs[i] = pl.BlockSpec((n, 8, W), lambda _: (0, 0, 0))
        specs[6 + i] = pl.BlockSpec((n, 8, W), lambda _: (0, last, 0))
    specs[5] = pl.BlockSpec((8, W), lambda _: (0, 0))
    specs[11] = pl.BlockSpec((8, W), lambda _: (last, 0))
    specs[12] = pl.BlockSpec((1, rows, W), lambda _: (layers - 1, 0, 0))
    count = 5 * layers
    first_rows, last_rows, v_top = pl.pallas_call(
        pack_x_kernel,
        grid=(1,),
        out_shape=[shape(count, 8, W)] * 2 + [shape(rows + TAIL, W)],
        in_specs=[specs[i] for i in range(13)],
        out_specs=[
            pl.BlockSpec((count, 8, W), lambda _: (0, 0, 0)),
            pl.BlockSpec((count, 8, W), lambda _: (0, 0, 0)),
            pl.BlockSpec((rows + TAIL, W), lambda _: (0, 0)),
        ],
        name="pack_x_kernel",
        compiler_params=pltpu.CompilerParams(vmem_limit_bytes=58 << 20),
        cost_estimate=pl.CostEstimate(flops=1, bytes_accessed=1_000_000, transcendentals=0),
    )(*args)
    lo = shift(last_rows, "gx", 1)
    hi = shift(first_rows, "gx", -1)
    lo, hi, v_top, outgoing = lax.optimization_barrier((lo, hi, v_top, outgoing))
    v_part = facing(v_top)
    tiles = [v, cx, cy, st, via, mask]
    to_left, to_right = call(
        pack_y_kernel, [shape(total, W), shape(total, W)], [*tiles, lo, hi], vmem=8
    )
    f_left = shift(to_right, "yt", 1)
    f_right = shift(to_left, "yt", -1)
    outgoing, f_left, f_right, v_part = lax.optimization_barrier(
        (outgoing, f_left, f_right, v_part)
    )
    arrived = lax.all_to_all(
        outgoing.reshape(devices, ROWS_MSG, 1, W), ALL, 0, 0, tiled=True
    ).reshape(devices * ROWS_MSG, W)

    one = shape(nr, 2 * W)
    tile = shape(rows, W)
    buffer = lambda *d: pltpu.VMEM(d, F32)
    msg_shape = shape(total + 8 * side_blocks, W)
    held = [one] * (4 * layers + 5)
    msg0_shape = shape(3 * (total + 8 * side_blocks) - 2 * rows, W)
    held += [tile, one, one, tile, shape(layers - 1, rows, W), msg0_shape]
    outs = call(
        base_kernel,
        [*held, one],
        [place, *tiles, v_part, lo, hi, f_left, f_right],
        scratch=[buffer(*h.shape) for h in held]
        + [buffer(nr, 2 * W)] * (4 * layers + 1)
        + [buffer(side_blocks * W, W)]
        + [buffer(nr, 2 * W)] * 7
        + [pltpu.SemaphoreType.DMA((9 * layers + 20,))],
        specs={0: SMEM, 1: ANY, 2: ANY, 3: ANY, 4: ANY, 5: ANY, 7: ANY},
        out_specs=[ANY] * (len(held) + 1),
        vmem=VMEM_BASE,
        cost=20_000_000,
    )
    gx, gy, inv, via_e = outs[0:4], outs[4:8], outs[8:12], outs[12:15]
    bond, d02, d03, d11, d12, z12, d20, d21, z21, sb0, vd0, msg0, v3 = outs[15:]
    part0 = facing(msg0)

    cur, cur_first, cur_last, labels = call(
        map_kernel,
        [tile, shape(8, W), shape(8, W), jax.ShapeDtypeStruct((devices * CAP,), jnp.int32)],
        [arrived],
        scratch=[
            pltpu.VMEM((devices, W), jnp.int32),
            pltpu.SMEM((devices, W), jnp.int32),
            *[buffer(rows + 8, W)] * 4,
            pltpu.SemaphoreType.DMA,
        ],
        out_specs=[pl.BlockSpec(memory_space=pltpu.VMEM)] * 3 + [SMEM],
    )
    cur_lo = shift(cur_last, "gx", 1)
    cur_hi = shift(cur_first, "gx", -1)
    top = [gx[3], gy[3], inv[3], via_e[2], bond]
    cur_left, cur_right = call(
        edges_kernel,
        [shape(8, side_blocks * W)] * 2,
        [cur, cur_lo, cur_hi],
        scratch=[buffer(side_blocks * W, W)],
    )
    labels, part0 = lax.optimization_barrier((labels, part0))
    far_one = pltpu.HBM((nr, 2 * W), F32)
    d13, z13, delta, msg1 = call(
        first_top_kernel,
        [far_one, far_one, far_one, msg_shape],
        [part0, d02, d03, v3, *top],
        scratch=[buffer(nr, 2 * W)] * 12
        + [buffer(side_blocks * W, W), buffer(W, W), pltpu.SemaphoreType.DMA((11,))],
        specs={i: ANY for i in range(1, 9)},
        out_specs=[ANY] * 3 + [pl.BlockSpec(memory_space=pltpu.VMEM)],
        vmem=VMEM_TOP,
        far=range(1, 9),
    )
    cur_left, cur_right, msg1 = lax.optimization_barrier((cur_left, cur_right, msg1))
    part1 = facing(msg1)
    d23, z23, msg2, weight = call(
        second_top_kernel,
        [one, one, tile, tile],
        [d12, inv[2], delta, d13, z13, part1, *top],
        scratch=[buffer(nr, W), buffer(W, W)],
        vmem=VMEM_FINAL,
    )

    cur_f_left = shift(cur_right, "yt", 1)
    cur_f_right = shift(cur_left, "yt", -1)
    v0, picked, e11, e21, ze21, d20 = call(
        effect_kernel,
        [pltpu.HBM(d, F32) for d in (
            (rows, W), (devices * CAP * 8, W), (nr, 2 * W), (nr, 2 * W), (rows, W), (rows, W))],
        [labels, cur, cur_lo, cur_hi, cur_f_left, cur_f_right,
         inv[0], gx[0], gy[0], via_e[0], inv[1], gx[1], gy[1], sb0, d20],
        scratch=[buffer(nr, 2 * W)] * 9
        + [buffer(W, W), buffer(rows + 8, W), buffer(rows, W), buffer(rows, W)]
        + [buffer(devices * CAP * 8, W), pltpu.SemaphoreType.DMA((9,))],
        specs={0: SMEM},
        out_specs=[ANY] * 6,
        vmem=VMEM_EFFECT,
    )
    picked, part1 = lax.optimization_barrier((picked, part1))
    part2 = facing(msg2)
    back = lax.all_to_all(picked, ALL, 0, 0, tiled=True)

    voltage = call(
        final_kernel,
        shape(layers, rows, W),
        [v0, vd0, d11, d12, z12, e11, d13, d20, d21, e21, d23, z21, ze21, z23, delta,
         *gx[1:], *gy[1:], *inv[1:], *via_e],
        scratch=[buffer(nr, 2 * W)] * 4,
        vmem=VMEM_FINAL,
        cost=10_000_000,
    )
    whole = pl.BlockSpec(memory_space=pltpu.VMEM)
    upper = pl.BlockSpec((1, rows, W), lambda _: (layers - 1, 0, 0))
    block_voltage, voltage = pl.pallas_call(
        last_kernel,
        grid=(1,),
        out_shape=[shape(nb, 8, W), shape(layers, rows, W)],
        in_specs=[SMEM, whole, upper, whole, whole],
        out_specs=[whole, upper],
        input_output_aliases={2: 1},
        name="last_kernel",
        compiler_params=pltpu.CompilerParams(vmem_limit_bytes=58 << 20),
    )(dest, back, voltage, part2, weight)
    return voltage, block_voltage


def solution(mesh):
    tile = P(None, "gx", "yt")
    return jax.shard_map(
        on_device,
        mesh=mesh,
        in_specs=(tile, tile, tile, tile, tile, P("gx", "yt"), P(ALL, None, None), P(ALL, None), P(ALL)),
        out_specs=(tile, P(ALL, None, None)),
        check_vma=False,
    )
```

```python
import jax
import jax.numpy as jnp
from jax import lax
from jax.experimental import pallas as pl
from jax.experimental.pallas import tpu as pltpu
from jax.sharding import PartitionSpec as P

CAP = 2
TAIL = 24
BOND = 2.0
CENTER = 1.0
HALFWIDTH = 0.97
SIGMA = CENTER / HALFWIDTH
RHO0 = 1.0 / SIGMA
RHO1 = 1.0 / (2.0 * SIGMA - RHO0)
RHO2 = 1.0 / (2.0 * SIGMA - RHO1)
RHO3 = 1.0 / (2.0 * SIGMA - RHO2)
A1, B1 = RHO1 * RHO0, 2.0 * RHO1 / HALFWIDTH
A2, B2 = RHO2 * RHO1, 2.0 * RHO2 / HALFWIDTH
A3, B3 = RHO3 * RHO2, 2.0 * RHO3 / HALFWIDTH

VMEM_BASE, VMEM_TOP, VMEM_EFFECT, VMEM_FINAL = 58, 20, 16, 58

ALL = ("gx", "yt")
F32 = jnp.float32
W = 128
H = 8
PAD = 16
Q = 4
WIDE = 88
STEP = 64
ROWS_MSG = CAP * 8 + 1


def call(kernel, out, args, scratch=(), specs=None, out_specs=None, vmem=6, cost=1_000_000, far=()):
    specs = specs or {}
    in_specs = [
        specs.get(i, pl.BlockSpec(memory_space=pltpu.VMEM)) for i in range(len(args))
    ]
    args = [
        pltpu.with_memory_space_constraint(x, pltpu.HBM) if i in far else x
        for i, x in enumerate(args)
    ]
    many = isinstance(out, (list, tuple))
    outs = list(out) if many else [out]
    o_specs = out_specs or [pl.BlockSpec(memory_space=pltpu.VMEM)] * len(outs)
    return pl.pallas_call(
        kernel,
        out_shape=outs if many else outs[0],
        in_specs=in_specs,
        out_specs=o_specs if many else o_specs[0],
        scratch_shapes=list(scratch),
        name=kernel.__name__,
        compiler_params=pltpu.CompilerParams(vmem_limit_bytes=vmem << 20),
        cost_estimate=pl.CostEstimate(flops=cost, bytes_accessed=cost, transcendentals=0),
    )(*args)


def shape(*dims):
    return jax.ShapeDtypeStruct(dims, F32)


SMEM = pl.BlockSpec(memory_space=pltpu.SMEM)
ANY = pl.BlockSpec(memory_space=pl.ANY)
HBM = pl.BlockSpec(memory_space=pltpu.HBM)


class Copies:
    def __init__(self, sems):
        self.sems, self.made = sems, []

    def start(self, *pairs):
        begun = []
        for source, target in pairs:
            copy = pltpu.make_async_copy(source, target, self.sems.at[len(self.made)])
            copy.start()
            self.made.append(copy)
            begun.append(copy)
        return begun


def wait(copies):
    for copy in copies:
        copy.wait()


def from_right(x):
    return pltpu.roll(x, x.shape[-1] - 1, axis=1)


def from_left(x):
    return pltpu.roll(x, 1, axis=1)


def lanes(rows, width=W):
    return lax.broadcasted_iota(jnp.int32, (rows, width), 1)


def each_chunk(first, rows, body, step):
    @pl.loop(0, rows // step)
    def _(k):
        body(pl.multiple_of(first + k * step, 8))


def send_kernel(
    owner_ref, slot_ref, blocks_ref, v_ref, out_hbm, dest_ref, top_hbm,
    count_ref, buf, slots, out_ref, top_ref, sems,
):
    devices = count_ref.shape[0]
    copies = Copies(sems)
    rows = v_ref.shape[1]
    top = v_ref.at[v_ref.shape[0] - 1]
    [fetch] = copies.start((top, top_ref.at[pl.ds(0, rows), :]))

    @pl.loop(0, devices, unroll=8)
    def _(o):
        count_ref[o] = 0

    buf[...] = jnp.zeros_like(buf)
    slots[...] = jnp.full(slots.shape, 64, jnp.int32)
    lane = lanes(1)

    @pl.loop(0, blocks_ref.shape[0], unroll=4)
    def _(k):
        owner = owner_ref[k]
        rank = count_ref[owner]
        count_ref[owner] = rank + 1
        dest = owner * CAP + rank
        dest_ref[k] = dest
        buf[pl.ds(pl.multiple_of(dest * 8, 8), 8), :] = blocks_ref[k]
        row = slots[pl.ds(owner, 1), :]
        slots[pl.ds(owner, 1), :] = jnp.where(lane == rank, slot_ref[k], row)

    def assemble(g):
        data = buf[pl.ds(pl.multiple_of(g * CAP * 64, 8), CAP * 64), :]
        label = slots[pl.ds(pl.multiple_of(g * 8, 8), 8), :].astype(F32)
        pieces = []
        for j in range(8):
            pieces += [data[CAP * 8 * j : CAP * 8 * (j + 1)], label[j : j + 1]]
        out_ref[pl.ds(pl.multiple_of(g * ROWS_MSG * 8, 8), ROWS_MSG * 8), :] = (
            jnp.concatenate(pieces, axis=0)
        )

    fetch.wait()
    top_ref[rows:, :] = jnp.zeros((TAIL, W), F32)
    leaving = copies.start((top_ref, top_hbm))
    groups = devices // 8 // 4
    for part in range(4):
        pl.loop(part * groups, (part + 1) * groups)(assemble)
        n = groups * 8 * ROWS_MSG
        a = pl.ds(part * n, n)
        leaving += copies.start((out_ref.at[a, :], out_hbm.at[a, :]))
    wait(leaving)


def pack_x_kernel(*refs):
    firsts, lasts = refs[:6], refs[6:12]
    first_out, last_out = refs[12:]
    for group, out in ((firsts, first_out), (lasts, last_out)):
        p = 0
        for ref in group[:5]:
            n = ref.shape[0]
            out[p : p + n] = ref[...]
            p += n
        out[p] = BOND * group[5][...].astype(F32)


def pack_y_kernel(v, cx, cy, st, via, mask, lo, hi, to_left, to_right):
    rows = v.shape[1]

    def pack(planes, at, n):
        lane = lanes(n)
        left = jnp.zeros((n, W), F32)
        right = jnp.zeros((n, W), F32)
        for p, x in enumerate(planes):
            turned = x if p == 0 else pltpu.roll(x, Q * p, axis=1)
            left = jnp.where(lane // Q == p, turned, left)
            right = jnp.where(lane // Q == (p - 1) % (W // Q), turned, right)
        to_left[pl.ds(at, n), :] = left
        to_right[pl.ds(at, n), :] = right

    def tile(i):
        at = pl.ds(i, STEP)
        planes = [ref[l, at, :] for ref in (v, cx, cy, st, via) for l in range(ref.shape[0])]
        planes += [BOND * mask[at, :].astype(F32)]
        pack(planes, pl.multiple_of(i + H, 8), STEP)

    each_chunk(0, rows, tile, STEP)
    count = lo.shape[0]
    pack([lo[p] for p in range(count)], 0, H)
    pack([hi[p] for p in range(count)], H + rows, H)


def rows_of(ref, l=None):
    if l is None:
        return lambda s, n: ref[pl.ds(s, n), :]
    return lambda s, n: ref[l, pl.ds(s, n), :]


def weighted(x, s, n, gx, gy):
    low = pl.multiple_of(s - 8, 8)
    near = rows_of(x)(low, n + 16)
    gnear = rows_of(gx)(low, n + 8)
    c = near[8 : 8 + n]
    g = rows_of(gy)(s, n)
    up = gnear[8 : 8 + n] * near[9 : 9 + n]
    down = (gnear * near[0 : n + 8])[7 : 7 + n]
    return up + down + g * from_right(c) + from_left(g * c)


def base_kernel(*refs):
    place, v, cx, cy, st, via, mask, vp, lo, hi, f_left, f_right = refs[:12]
    refs = list(refs[12:])
    layers, rows = v.shape[0], v.shape[1]
    total = rows + 2 * H

    def take(n):
        got = refs[:n]
        del refs[:n]
        return got

    outs = take(4 * layers + 11)
    [v3_out] = take(1)
    helds = take(4 * layers + 11)
    ev, ecx, ecy, est = take(layers), take(layers), take(layers), take(layers)
    evp, side, d00, d01, d10, z10, z11, z20, e20, sems = take(10)
    copies = Copies(sems)
    home = dict(zip(map(id, helds), outs))

    def give(*held):
        return copies.start(*[(h, home[id(h)]) for h in held])

    refs = list(helds)
    gx, gy, inv, viae = take(layers), take(layers), take(layers), take(layers - 1)
    bond, d02, d03, d11, d12, z12, d20, d21, z21, sb0, vd0, msg = take(12)
    d0 = [d00, d01, d02, d03]
    d1, z1 = [d10, d11, d12], [z10, z11, z12]
    d2, z2 = [e20, d21], [z20, z21]
    dests = [*ev, *ecx, *ecy, *est, *viae, bond]
    main, edge = slice(0, W), slice(W, 2 * W)
    sources = [ref.at[l] for ref in (v, cx, cy, st, via) for l in range(ref.shape[0])]
    arriving = copies.start(
        *[
            (source, dest.at[pl.ds(PAD, rows), pl.ds(0, W)])
            for source, dest in zip([*sources, vp.at[pl.ds(0, rows), :]], [*dests[:-1], evp])
        ]
    )

    def sides(s):
        r = pl.multiple_of(s - H, 8)
        a = f_right[pl.ds(r, WIDE), :]
        b = f_left[pl.ds(r, WIDE), :]
        even = lanes(WIDE) // Q % 2 == 0
        both = [jnp.where(even, a, b), jnp.where(even, b, a)]
        for p, dest in enumerate(dests):
            x = both[p % 2]
            dest[pl.ds(s, WIDE), edge] = x if p == 0 else pltpu.roll(x, W - Q * p, axis=1)
        evp[pl.ds(s, WIDE), edge] = jnp.zeros((WIDE, W), F32)

    each_chunk(H, total, sides, WIDE)

    def bonds(i):
        weight = BOND * mask[pl.ds(i, STEP), :].astype(F32)
        bond[pl.ds(pl.multiple_of(i + PAD, 8), STEP), main] = weight

    each_chunk(0, rows, bonds, STEP)
    for p, dest in enumerate(dests):
        dest[H : 2 * H, main] = lo[p]
        dest[PAD + rows : PAD + rows + H, main] = hi[p]
    evp[H : 2 * H, main] = jnp.zeros((H, W), F32)
    evp[PAD + rows : PAD + rows + H, main] = jnp.zeros((H, W), F32)
    wait(arriving)

    x_first, x_total, y_first, y_total = place[0], place[1], place[2], place[3]
    col = lanes(1, 2 * W)
    col = y_first + jnp.where(col < W + W // 2, col, col - 2 * W)
    nxt = lax.rem(col + 1 + y_total, y_total)
    seam = W // 2
    keep_y = jnp.where((nxt != seam) & (nxt != seam + y_total // 2), 0.5, 0.0).astype(F32)

    def conductances(s):
        row = x_first + s - PAD + lax.broadcasted_iota(jnp.int32, (WIDE, 1), 0)
        keep_x = jnp.where((row != -1) & (row != x_total - 1), 0.5, 0.0).astype(F32)
        for l in range(layers):
            c = ecx[l][pl.ds(s, WIDE + 8), :]
            gx[l][pl.ds(s, WIDE), :] = keep_x * (c[0:WIDE] + c[1 : WIDE + 1])
            c = ecy[l][pl.ds(s, WIDE), :]
            gy[l][pl.ds(s, WIDE), :] = keep_y * (c + from_right(c))

    each_chunk(H, total, conductances, WIDE)
    leaving = give(*gx, *gy, *viae, bond)
    leaving += copies.start((ev[layers - 1], v3_out))

    def start(s):
        n = WIDE
        a = pl.ds(s, n)
        for l in range(layers):
            near = gx[l][pl.ds(pl.multiple_of(s - 8, 8), n + 8), :]
            up, down, right = near[8 : 8 + n], near[7 : 7 + n], gy[l][a, :]
            off = up + down + right + from_left(right)
            nb = weighted(ev[l], s, n, gx[l], gy[l])
            if l < layers - 1:
                off = off + viae[l][a, :]
                nb = nb + viae[l][a, :] * ev[l + 1][a, :]
            else:
                off = off + bond[a, :]
                nb = nb + bond[a, :] * evp[a, :]
            if l > 0:
                off = off + viae[l - 1][a, :]
                nb = nb + viae[l - 1][a, :] * ev[l - 1][a, :]
            c = ev[l][a, :]
            inverse = 1.0 / (est[l][a, :] + off)
            inv[l][a, :] = inverse
            d0[l][a, :] = (nb - off * c) * inverse

    each_chunk(H, total, start, WIDE)
    leaving += give(*inv, d02, d03)

    def links(d, l, s, n):
        nb = weighted(d[l], s, n, gx[l], gy[l])
        if l < layers - 1:
            nb = nb + viae[l][pl.ds(s, n), :] * d[l + 1][pl.ds(s, n), :]
        if l > 0:
            nb = nb + viae[l - 1][pl.ds(s, n), :] * d[l - 1][pl.ds(s, n), :]
        return inv[l][pl.ds(s, n), :] * nb

    def first(s):
        a = pl.ds(s, WIDE)
        r = pl.ds(pl.multiple_of(s - H, 8), WIDE)
        side[r, :] = d03[a, edge]
        msg[r, :] = d03[a, main]
        for l in range(layers - 1):
            z = links(d0, l, s, WIDE)
            z1[l][a, :] = z
            d1[l][a, :] = A1 * d0[l][a, :] + B1 * z

    each_chunk(H, total, first, WIDE)
    pack_side(side, msg, total, total)
    row = total + 8 * (side.shape[0] // W)
    for product in (False, True):
        def rim(x, product=product):
            part = ev[layers - 1][x]
            return inv[layers - 1][x] * bond[x] if product else part

        msg[row : row + H, :] = rim((slice(H, 2 * H), main))
        msg[row + H : row + 2 * H, :] = rim((slice(PAD + rows, PAD + rows + H), main))

        def lay(s, rim=rim):
            side[pl.ds(pl.multiple_of(s - H, 8), WIDE), :] = rim((pl.ds(s, WIDE), edge))

        each_chunk(H, total, lay, WIDE)
        pack_side(side, msg, row + 2 * H, total)
        row += 2 * H + 8 * (side.shape[0] // W)
    leaving += give(d11, d12, z12, msg)

    def second(s):
        a = pl.ds(s, WIDE)
        for l in range(2):
            z = z1[l][a, :] - d1[l][a, :] + links(d1, l, s, WIDE)
            z2[l][a, :] = z
            d2[l][a, :] = A2 * d1[l][a, :] + B2 * z

    each_chunk(H, total, second, WIDE)
    leaving += give(d21, z21)

    def third(s):
        a = pl.ds(s, STEP)
        o = pl.ds(pl.multiple_of(s - PAD, 8), STEP)
        nb = weighted(e20, s, STEP, gx[0], gy[0])[:, main]
        nb = inv[0][a, main] * (nb + viae[0][a, main] * d21[a, main])
        d = e20[a, main]
        z = z20[a, main] - d + nb
        d20[o, :] = d
        sb0[o, :] = ev[0][a, main] + d00[a, main] + d10[a, main] + (1.0 + A3) * d + B3 * z
        for l in range(1, layers):
            vd0[l - 1, o, :] = ev[l][a, main] + d0[l][a, main]

    each_chunk(PAD, rows, third, STEP)
    leaving += give(d20, sb0, vd0)
    wait(leaving)


def pack_side(side, msg, row, total):
    for j in range(-(-total // W)):
        t = side[W * j : W * j + W, :].T
        msg[row + 8 * j : row + 8 * j + Q, :] = t[0:Q]
        msg[row + 8 * j + Q : row + 8 * j + 2 * Q, :] = t[W - Q : W]


def unpack_side(msg, row, total, u):
    blocks = []
    for j in range(-(-total // W)):
        u[0:Q, :] = msg[row + 8 * j : row + 8 * j + Q, :]
        u[W - Q : W, :] = msg[row + 8 * j + Q : row + 8 * j + 2 * Q, :]
        blocks.append((H + W * j, min(W, total - W * j), u[...].T))
    return blocks


def first_top_kernel(part, *refs):
    inputs, (d_hbm, z_hbm, delta_hbm, msg), held = refs[:8], refs[8:12], refs[12:20]
    low, d0, v3, gx, gy, inv, via, bond = held
    d_out, z_out, delta, ep, side, u, part_held, sems = refs[20:]
    copies = Copies(sems)
    [came] = copies.start((part, part_held))
    part = part_held
    arriving = copies.start(*zip(inputs, held))
    rows = part.shape[0] - 3 * (2 * H + 8 * (side.shape[0] // W))
    total = rows + 2 * H
    sides = 8 * (side.shape[0] // W)
    main, edge = slice(0, W), slice(W, 2 * W)
    u[...] = jnp.zeros_like(u)
    came.wait()
    row = total + sides
    own = unpack_side(part, row + 2 * H, total, u)
    others = unpack_side(part, row + 2 * H + sides + 2 * H, total, u)
    theirs = unpack_side(part, total, total, u)
    wait(arriving)
    delta[PAD : PAD + rows, main] = jnp.zeros((rows, W), F32)
    ep[PAD : PAD + rows, main] = part[H : H + rows, :]

    def halo(a, cols, v_part, weight_part, d_part):
        x = inv[a, cols] * bond[a, cols] * v_part
        delta[a, cols] = x
        d0[a, cols] = d0[a, cols] + x
        ep[a, cols] = d_part + weight_part * v3[a, cols]

    for k, first in ((0, H), (1, PAD + rows)):
        at = row + H * k
        halo(
            slice(first, first + H), main, part[at : at + H, :],
            part[at + 2 * H + sides : at + 3 * H + sides, :], part[first - H : first, :],
        )
    for (first, n, a), (_, _, b), (_, _, c) in zip(own, others, theirs):
        halo(slice(first, first + n), edge, a[:n], b[:n], c[:n])

    def body(s):
        a = pl.ds(s, WIDE)
        r = pl.ds(pl.multiple_of(s - H, 8), WIDE)
        nb = weighted(d0, s, WIDE, gx, gy) + via[a, :] * low[a, :] + bond[a, :] * ep[a, :]
        x = inv[a, :] * nb
        d = A1 * d0[a, :] + B1 * x
        z_out[a, :] = x
        d_out[a, :] = d
        side[r, :] = d[:, W:]
        msg[r, :] = d[:, :W]

    each_chunk(H, total, body, WIDE)
    leaving = copies.start((d_out, d_hbm), (z_out, z_hbm), (delta, delta_hbm))
    pack_side(side, msg, total, total)
    wait(leaving)


def second_top_kernel(low, inv_low, delta, here, z, part, gx, gy, inv, via, bond, d_out, z_out, msg, weight, ep, u):
    rows = msg.shape[0]
    total = rows + 2 * H
    u[...] = jnp.zeros_like(u)
    for first, n, x in unpack_side(part, total, total, u):
        ep[first : first + n, :] = x[:n]

    def body(s):
        a = pl.ds(s, WIDE)
        r = pl.ds(pl.multiple_of(s - H, 8), WIDE)
        other = jnp.concatenate([part[r, :], ep[a, :]], axis=1)
        under = low[a, :] + B1 * inv_low[a, :] * via[a, :] * delta[a, :]
        nb = weighted(here, s, WIDE, gx, gy) + via[a, :] * under + bond[a, :] * other
        c = here[a, :]
        x = z[a, :] - c + inv[a, :] * nb
        z_out[a, :] = x
        d_out[a, :] = A2 * c + B2 * x

    each_chunk(H, total, body, WIDE)
    msg[...] = d_out[PAD : PAD + rows, 0:W]
    weight[...] = inv[PAD : PAD + rows, 0:W] * bond[PAD : PAD + rows, 0:W]


def final_kernel(
    v0, vd0, d11, b12, z12, e11, d13, d20, b21, e21, d23, z21, ze21, z23, delta,
    gx1, gx2, gx3, gy1, gy2, gy3, inv1, inv2, inv3, via0, via1, via2,
    out, d22, z22, d21, d12,
):
    main = slice(0, W)
    rows = out.shape[1]

    def amend(s):
        a = pl.ds(s, WIDE)
        c = inv2[a, :] * via2[a, :] * delta[a, :]
        z22[a, :] = z12[a, :] + c
        c = B1 * c
        d12[a, :] = b12[a, :] + c
        d21[a, :] = b21[a, :] + e21[a, :] + B2 * inv1[a, :] * via1[a, :] * c

    each_chunk(H, rows + 2 * H, amend, WIDE)

    def middle(s):
        a = pl.ds(s, WIDE)
        this = d12[a, :]
        nb = weighted(d12, s, WIDE, gx2, gy2)
        nb = nb + via1[a, :] * (d11[a, :] + e11[a, :]) + via2[a, :] * d13[a, :]
        z = z22[a, :] - this + inv2[a, :] * nb
        z22[a, :] = z
        d22[a, :] = A2 * this + B2 * z

    each_chunk(H, rows + 2 * H, middle, WIDE)
    gx, gy, inv = [None, gx1, gx2, gx3], [None, gy1, gy2, gy3], [None, inv1, inv2, inv3]
    via = [via0, via1, via2]
    d2, z2 = [None, d21, d22, d23], [None, None, z22, z23]

    def body(i):
        s = pl.multiple_of(i + PAD, 8)
        a, o = pl.ds(s, STEP), pl.ds(i, STEP)
        out[0, o, :] = v0[o, :]
        first = [None, d11[a, main] + e11[a, main], d12[a, main], d13[a, main]]
        below = d20[o, :]
        for l in range(1, 4):
            nb = weighted(d2[l], s, STEP, gx[l], gy[l])[:, main]
            nb = nb + via[l - 1][a, main] * below
            below = d2[l][a, main]
            if l < 3:
                nb = nb + via[l][a, main] * d2[l + 1][a, main]
            z = (z21[a, main] + ze21[o, :] if l == 1 else z2[l][a, main]) - below + inv[l][a, main] * nb
            out[l, o, :] = vd0[l - 1, o, :] + first[l] + (1.0 + A3) * below + B3 * z

    each_chunk(0, rows, body, STEP)


def map_kernel(arrived, out, first, last, labels, vec, lab, a0, a1, a2, a3, sem):
    devices = vec.shape[0]
    rows = out.shape[0]
    vec[...] = arrived[pl.ds(CAP * 8, devices, stride=ROWS_MSG), :].astype(jnp.int32)
    copy = pltpu.make_async_copy(vec, lab, sem)
    copy.start()
    parts = (a0, a1, a2, a3)
    for acc in parts:
        acc[...] = jnp.zeros_like(acc)
    copy.wait()

    @pl.loop(0, devices // 8)
    def _(g):
        n = ROWS_MSG * 8
        data = arrived[pl.ds(pl.multiple_of(g * n, 8), n), :]
        for j in range(8):
            for r in range(CAP):
                slot = lab[g * 8 + j, r]
                labels[(g * 8 + j) * CAP + r] = slot
                a = pl.ds(pl.multiple_of(slot * 8, 8), 8)
                acc = parts[(j * CAP + r) % 4]
                acc[a, :] += data[j * ROWS_MSG + r * 8 : j * ROWS_MSG + r * 8 + 8]

    out[...] = (a0[0:rows, :] + a1[0:rows, :]) + (a2[0:rows, :] + a3[0:rows, :])
    first[...] = out[0:8, :]
    last[...] = out[rows - 8 : rows, :]


def edges_kernel(cur, lo, hi, to_left, to_right, ext):
    rows = cur.shape[0]
    ext[0:H, :] = lo[...]
    ext[H : H + rows, :] = cur[...]
    ext[H + rows : rows + 2 * H, :] = hi[...]
    for j in range(to_left.shape[1] // W):
        t = ext[W * j : W * j + W, :].T
        to_left[:, W * j : W * j + W] = t[0:8]
        to_right[:, W * j : W * j + W] = t[W - 8 : W]


def effect_kernel(
    labels, cur, lo, hi, f_left, f_right, *refs
):
    (inv0, gx0, gy0, via0, inv1, gx1, gy1, sb0, d20), refs = refs[:9], refs[9:]
    v0_out, picked_out, e11_out, e21_out, z21_out, d20_out = refs[:6]
    ec, e0, e1, z10, z11, e2, z20, e11, e21, u, acc, z21, d20_sum, picked, sems = refs[6:]
    copies = Copies(sems)
    rows = cur.shape[0]
    total = rows + 2 * H
    main, edge = slice(0, W), slice(W, 2 * W)
    ec[H : 2 * H, main] = lo[...]
    ec[PAD : PAD + rows, main] = cur[...]
    ec[PAD + rows : PAD + rows + H, main] = hi[...]
    u[...] = jnp.zeros_like(u)
    for j in range(f_left.shape[1] // W):
        u[0:8, :] = f_right[:, W * j : W * j + W]
        u[W - 8 : W, :] = f_left[:, W * j : W * j + W]
        n = min(W, total - W * j)
        ec[H + W * j : H + W * j + n, edge] = u[...].T[:n]

    def zeroth(s):
        a = pl.ds(s, WIDE)
        e0[a, :] = inv0[a, :] * ec[a, :]

    each_chunk(H, total, zeroth, WIDE)
    def first(s):
        a = pl.ds(s, WIDE)
        here = e0[a, :]
        z = inv0[a, :] * weighted(e0, s, WIDE, gx0, gy0)
        z10[a, :] = z
        e1[a, :] = A1 * here + B1 * z
        z = inv1[a, :] * via0[a, :] * here
        z11[a, :] = z
        e11[a, :] = B1 * z

    each_chunk(H, total, first, WIDE)
    def second(s):
        a = pl.ds(s, WIDE)
        low, high, between = e1[a, :], e11[a, :], via0[a, :]
        nb = weighted(e1, s, WIDE, gx0, gy0) + between * high
        z = z10[a, :] - low + inv0[a, :] * nb
        z20[a, :] = z
        e2[a, :] = A2 * low + B2 * z
        nb = weighted(e11, s, WIDE, gx1, gy1) + between * low
        z = z11[a, :] - high + inv1[a, :] * nb
        z11[a, :] = z
        e21[a, :] = A2 * high + B2 * z

    each_chunk(H, total, second, WIDE)
    copies.start((e11, e11_out), (e21, e21_out))
    def third(i):
        s = pl.multiple_of(i + PAD, 8)
        a, o = pl.ds(s, STEP), pl.ds(i, STEP)
        here = e2[a, main]
        nb = weighted(e2, s, STEP, gx0, gy0)[:, main] + via0[a, main] * e21[a, main]
        z = z20[a, main] - here + inv0[a, main] * nb
        whole = sb0[o, :] + e0[a, main] + e1[a, main] + (1.0 + A3) * here + B3 * z
        acc[o, :] = whole
        d20_sum[o, :] = d20[o, :] + here
        z21[o, :] = z11[a, main]

    each_chunk(0, rows, third, STEP)
    copies.start((acc.at[pl.ds(0, rows), :], v0_out), (z21, z21_out), (d20_sum, d20_out))
    acc[rows : rows + 8, :] = jnp.zeros((8, W), F32)

    def pick(k):
        picked[pl.ds(pl.multiple_of(k * 8, 8), 8), :] = acc[
            pl.ds(pl.multiple_of(labels[k] * 8, 8), 8), :
        ]

    count = labels.shape[0] // 4
    for part in range(4):
        pl.loop(part * count, (part + 1) * count, unroll=8)(pick)
        a = pl.ds(part * count * 8, count * 8)
        copies.start((picked.at[a, :], picked_out.at[a, :]))
    wait(copies.made)


def last_kernel(dest, back, field, part, weight, out, top):
    top[0] = field[0] + B3 * weight[...] * part[...]

    @pl.loop(0, out.shape[0], unroll=8)
    def _(k):
        out[k] = back[pl.ds(pl.multiple_of(dest[k] * 8, 8), 8), :]


def ring(axis, step):
    n = lax.axis_size(axis)
    return [(i, (i + step) % n) for i in range(n)]


def shift(x, axis, step):
    return lax.ppermute(x, axis, ring(axis, step))


def facing(x, step=0):
    n, m = lax.axis_size("gx"), lax.axis_size("yt")
    pairs = [
        (g * m + t, ((g + step) % n) * m + (t ^ (m // 2))) for g in range(n) for t in range(m)
    ]
    return lax.ppermute(x, ALL, pairs)


def on_device(v, st, cx, cy, via, mask, blocks, owner, slot):
    layers, rows, cols = v.shape
    devices = lax.axis_size("gx") * lax.axis_size("yt")
    nb = blocks.shape[0]
    total = rows + 2 * H
    nr = total + 2 * H
    side_blocks = -(-total // W)
    place = jnp.stack(
        [
            lax.axis_index("gx") * rows,
            jnp.int32(rows * lax.axis_size("gx")),
            lax.axis_index("yt") * cols,
            jnp.int32(cols * lax.axis_size("yt")),
        ]
    ).astype(jnp.int32)

    outgoing, dest, v_top = call(
        send_kernel,
        [
            pltpu.HBM((devices * ROWS_MSG, W), F32),
            jax.ShapeDtypeStruct((nb,), jnp.int32),
            pltpu.HBM((rows + TAIL, W), F32),
        ],
        [owner.reshape(nb), slot, blocks, v],
        scratch=[
            pltpu.SMEM((devices,), jnp.int32),
            pltpu.VMEM((devices * CAP * 8, W), F32),
            pltpu.VMEM((devices, W), jnp.int32),
            pltpu.VMEM((devices * ROWS_MSG, W), F32),
            pltpu.VMEM((rows + TAIL, W), F32),
            pltpu.SemaphoreType.DMA((6,)),
        ],
        specs={0: SMEM, 1: SMEM, 3: ANY},
        out_specs=[ANY, SMEM, ANY],
        far=(3,),
    )
    sources = [v, cx, cy, st, via]
    args = sources + [mask] + sources + [mask]
    specs = {}
    last = rows // 8 - 1
    for i in range(5):
        n = sources[i].shape[0]
        specs[i] = pl.BlockSpec((n, 8, W), lambda _: (0, 0, 0))
        specs[6 + i] = pl.BlockSpec((n, 8, W), lambda _: (0, last, 0))
    specs[5] = pl.BlockSpec((8, W), lambda _: (0, 0))
    specs[11] = pl.BlockSpec((8, W), lambda _: (last, 0))
    count = 5 * layers
    first_rows, last_rows = pl.pallas_call(
        pack_x_kernel,
        grid=(1,),
        out_shape=[shape(count, 8, W)] * 2,
        in_specs=[specs[i] for i in range(12)],
        out_specs=[
            pl.BlockSpec((count, 8, W), lambda _: (0, 0, 0)),
            pl.BlockSpec((count, 8, W), lambda _: (0, 0, 0)),
        ],
        name="pack_x_kernel",
        compiler_params=pltpu.CompilerParams(vmem_limit_bytes=58 << 20),
        cost_estimate=pl.CostEstimate(flops=1, bytes_accessed=1_000_000, transcendentals=0),
    )(*args)
    lo = shift(last_rows, "gx", 1)
    hi = shift(first_rows, "gx", -1)
    lo, hi, v_top, outgoing = lax.optimization_barrier((lo, hi, v_top, outgoing))
    v_part = facing(v_top)
    tiles = [v, cx, cy, st, via, mask]
    to_left, to_right = call(
        pack_y_kernel, [shape(total, W), shape(total, W)], [*tiles, lo, hi], vmem=8
    )
    f_left = shift(to_right, "yt", 1)
    f_right = shift(to_left, "yt", -1)
    outgoing, f_left, f_right, v_part = lax.optimization_barrier(
        (outgoing, f_left, f_right, v_part)
    )
    arrived = lax.all_to_all(
        outgoing.reshape(devices, ROWS_MSG, 1, W), ALL, 0, 0, tiled=True
    ).reshape(devices * ROWS_MSG, W)

    one = shape(nr, 2 * W)
    tile = shape(rows, W)
    buffer = lambda *d: pltpu.VMEM(d, F32)
    msg_shape = shape(total + 8 * side_blocks, W)
    held = [one] * (4 * layers + 5)
    msg0_shape = shape(3 * (total + 8 * side_blocks) - 2 * rows, W)
    held += [tile, one, one, tile, shape(layers - 1, rows, W), msg0_shape]
    outs = call(
        base_kernel,
        [*held, one],
        [place, *tiles, v_part, lo, hi, f_left, f_right],
        scratch=[buffer(*h.shape) for h in held]
        + [buffer(nr, 2 * W)] * (4 * layers + 1)
        + [buffer(side_blocks * W, W)]
        + [buffer(nr, 2 * W)] * 7
        + [pltpu.SemaphoreType.DMA((9 * layers + 20,))],
        specs={0: SMEM, 1: ANY, 2: ANY, 3: ANY, 4: ANY, 5: ANY, 7: ANY},
        out_specs=[ANY] * (len(held) + 1),
        vmem=VMEM_BASE,
        cost=20_000_000,
    )
    gx, gy, inv, via_e = outs[0:4], outs[4:8], outs[8:12], outs[12:15]
    bond, d02, d03, d11, d12, z12, d20, d21, z21, sb0, vd0, msg0, v3 = outs[15:]
    part0 = facing(msg0)

    cur, cur_first, cur_last, labels = call(
        map_kernel,
        [tile, shape(8, W), shape(8, W), jax.ShapeDtypeStruct((devices * CAP,), jnp.int32)],
        [arrived],
        scratch=[
            pltpu.VMEM((devices, W), jnp.int32),
            pltpu.SMEM((devices, W), jnp.int32),
            *[buffer(rows + 8, W)] * 4,
            pltpu.SemaphoreType.DMA,
        ],
        out_specs=[pl.BlockSpec(memory_space=pltpu.VMEM)] * 3 + [SMEM],
    )
    cur_lo = shift(cur_last, "gx", 1)
    cur_hi = shift(cur_first, "gx", -1)
    top = [gx[3], gy[3], inv[3], via_e[2], bond]
    cur_left, cur_right = call(
        edges_kernel,
        [shape(8, side_blocks * W)] * 2,
        [cur, cur_lo, cur_hi],
        scratch=[buffer(side_blocks * W, W)],
    )
    labels, part0 = lax.optimization_barrier((labels, part0))
    far_one = pltpu.HBM((nr, 2 * W), F32)
    d13, z13, delta, msg1 = call(
        first_top_kernel,
        [far_one, far_one, far_one, msg_shape],
        [part0, d02, d03, v3, *top],
        scratch=[buffer(nr, 2 * W)] * 12
        + [buffer(side_blocks * W, W), buffer(W, W), buffer(*msg0_shape.shape)]
        + [pltpu.SemaphoreType.DMA((12,))],
        specs={i: ANY for i in range(9)},
        out_specs=[ANY] * 3 + [pl.BlockSpec(memory_space=pltpu.VMEM)],
        vmem=VMEM_TOP,
        far=range(9),
    )
    cur_left, cur_right, msg1 = lax.optimization_barrier((cur_left, cur_right, msg1))
    part1 = facing(msg1)
    d23, z23, msg2, weight = call(
        second_top_kernel,
        [one, one, tile, tile],
        [d12, inv[2], delta, d13, z13, part1, *top],
        scratch=[buffer(nr, W), buffer(W, W)],
        vmem=VMEM_FINAL,
    )

    cur_f_left = shift(cur_right, "yt", 1)
    cur_f_right = shift(cur_left, "yt", -1)
    v0, picked, e11, e21, ze21, d20 = call(
        effect_kernel,
        [pltpu.HBM(d, F32) for d in (
            (rows, W), (devices * CAP * 8, W), (nr, 2 * W), (nr, 2 * W), (rows, W), (rows, W))],
        [labels, cur, cur_lo, cur_hi, cur_f_left, cur_f_right,
         inv[0], gx[0], gy[0], via_e[0], inv[1], gx[1], gy[1], sb0, d20],
        scratch=[buffer(nr, 2 * W)] * 9
        + [buffer(W, W), buffer(rows + 8, W), buffer(rows, W), buffer(rows, W)]
        + [buffer(devices * CAP * 8, W), pltpu.SemaphoreType.DMA((9,))],
        specs={0: SMEM},
        out_specs=[ANY] * 6,
        vmem=VMEM_EFFECT,
    )
    picked, part1 = lax.optimization_barrier((picked, part1))
    part2 = facing(msg2)
    back = lax.all_to_all(picked, ALL, 0, 0, tiled=True)

    voltage = call(
        final_kernel,
        shape(layers, rows, W),
        [v0, vd0, d11, d12, z12, e11, d13, d20, d21, e21, d23, z21, ze21, z23, delta,
         *gx[1:], *gy[1:], *inv[1:], *via_e],
        scratch=[buffer(nr, 2 * W)] * 4,
        vmem=VMEM_FINAL,
        cost=10_000_000,
    )
    whole = pl.BlockSpec(memory_space=pltpu.VMEM)
    upper = pl.BlockSpec((1, rows, W), lambda _: (layers - 1, 0, 0))
    block_voltage, voltage = pl.pallas_call(
        last_kernel,
        grid=(1,),
        out_shape=[shape(nb, 8, W), shape(layers, rows, W)],
        in_specs=[SMEM, whole, upper, whole, whole],
        out_specs=[whole, upper],
        input_output_aliases={2: 1},
        name="last_kernel",
        compiler_params=pltpu.CompilerParams(vmem_limit_bytes=8 << 20),
    )(dest, back, voltage, part2, weight)
    return voltage, block_voltage


def solution(mesh):
    tile = P(None, "gx", "yt")
    return jax.shard_map(
        on_device,
        mesh=mesh,
        in_specs=(tile, tile, tile, tile, tile, P("gx", "yt"), P(ALL, None, None), P(ALL, None), P(ALL)),
        out_specs=(tile, P(ALL, None, None)),
        check_vma=False,
    )
```

```python
import jax
import jax.numpy as jnp
from jax import lax
from jax.experimental import pallas as pl
from jax.experimental.pallas import tpu as pltpu
from jax.sharding import PartitionSpec as P

CAP = 2
TAIL = 24
BOND = 2.0
CENTER = 1.0
HALFWIDTH = 0.97
SIGMA = CENTER / HALFWIDTH
RHO0 = 1.0 / SIGMA
RHO1 = 1.0 / (2.0 * SIGMA - RHO0)
RHO2 = 1.0 / (2.0 * SIGMA - RHO1)
RHO3 = 1.0 / (2.0 * SIGMA - RHO2)
A1, B1 = RHO1 * RHO0, 2.0 * RHO1 / HALFWIDTH
A2, B2 = RHO2 * RHO1, 2.0 * RHO2 / HALFWIDTH
A3, B3 = RHO3 * RHO2, 2.0 * RHO3 / HALFWIDTH

VMEM_BASE, VMEM_TOP, VMEM_EFFECT, VMEM_FINAL = 58, 20, 16, 58

ALL = ("gx", "yt")
F32 = jnp.float32
W = 128
H = 8
PAD = 16
Q = 4
WIDE = 88
STEP = 128
ROWS_MSG = CAP * 8 + 1


def call(kernel, out, args, scratch=(), specs=None, out_specs=None, vmem=6, cost=1_000_000, far=()):
    specs = specs or {}
    in_specs = [
        specs.get(i, pl.BlockSpec(memory_space=pltpu.VMEM)) for i in range(len(args))
    ]
    args = [
        pltpu.with_memory_space_constraint(x, pltpu.HBM) if i in far else x
        for i, x in enumerate(args)
    ]
    many = isinstance(out, (list, tuple))
    outs = list(out) if many else [out]
    o_specs = out_specs or [pl.BlockSpec(memory_space=pltpu.VMEM)] * len(outs)
    return pl.pallas_call(
        kernel,
        out_shape=outs if many else outs[0],
        in_specs=in_specs,
        out_specs=o_specs if many else o_specs[0],
        scratch_shapes=list(scratch),
        name=kernel.__name__,
        compiler_params=pltpu.CompilerParams(vmem_limit_bytes=vmem << 20),
        cost_estimate=pl.CostEstimate(flops=cost, bytes_accessed=cost, transcendentals=0),
    )(*args)


def shape(*dims):
    return jax.ShapeDtypeStruct(dims, F32)


SMEM = pl.BlockSpec(memory_space=pltpu.SMEM)
ANY = pl.BlockSpec(memory_space=pl.ANY)
HBM = pl.BlockSpec(memory_space=pltpu.HBM)


class Copies:
    def __init__(self, sems):
        self.sems, self.made = sems, []

    def start(self, *pairs):
        begun = []
        for source, target in pairs:
            copy = pltpu.make_async_copy(source, target, self.sems.at[len(self.made)])
            copy.start()
            self.made.append(copy)
            begun.append(copy)
        return begun


def wait(copies):
    for copy in copies:
        copy.wait()


def from_right(x):
    return pltpu.roll(x, x.shape[-1] - 1, axis=1)


def from_left(x):
    return pltpu.roll(x, 1, axis=1)


def lanes(rows, width=W):
    return lax.broadcasted_iota(jnp.int32, (rows, width), 1)


def each_chunk(first, rows, body, step):
    @pl.loop(0, rows // step)
    def _(k):
        body(pl.multiple_of(first + k * step, 8))


def send_kernel(
    owner_ref, slot_ref, blocks_ref, v_ref, out_hbm, dest_ref, top_hbm,
    count_ref, buf, slots, out_ref, top_ref, sems,
):
    devices = count_ref.shape[0]
    copies = Copies(sems)
    rows = v_ref.shape[1]
    top = v_ref.at[v_ref.shape[0] - 1]
    [fetch] = copies.start((top, top_ref.at[pl.ds(0, rows), :]))

    @pl.loop(0, devices, unroll=8)
    def _(o):
        count_ref[o] = 0

    buf[...] = jnp.zeros_like(buf)
    slots[...] = jnp.full(slots.shape, 64, jnp.int32)
    lane = lanes(1)

    @pl.loop(0, blocks_ref.shape[0], unroll=8)
    def _(k):
        owner = owner_ref[k]
        rank = count_ref[owner]
        count_ref[owner] = rank + 1
        dest = owner * CAP + rank
        dest_ref[k] = dest
        buf[pl.ds(pl.multiple_of(dest * 8, 8), 8), :] = blocks_ref[k]
        row = slots[pl.ds(owner, 1), :]
        slots[pl.ds(owner, 1), :] = jnp.where(lane == rank, slot_ref[k], row)

    def assemble(g):
        data = buf[pl.ds(pl.multiple_of(g * CAP * 64, 8), CAP * 64), :]
        label = slots[pl.ds(pl.multiple_of(g * 8, 8), 8), :].astype(F32)
        pieces = []
        for j in range(8):
            pieces += [data[CAP * 8 * j : CAP * 8 * (j + 1)], label[j : j + 1]]
        out_ref[pl.ds(pl.multiple_of(g * ROWS_MSG * 8, 8), ROWS_MSG * 8), :] = (
            jnp.concatenate(pieces, axis=0)
        )

    fetch.wait()
    top_ref[rows:, :] = jnp.zeros((TAIL, W), F32)
    leaving = copies.start((top_ref, top_hbm))
    groups = devices // 8 // 4
    for part in range(4):
        pl.loop(part * groups, (part + 1) * groups, unroll=2)(assemble)
        n = groups * 8 * ROWS_MSG
        a = pl.ds(part * n, n)
        leaving += copies.start((out_ref.at[a, :], out_hbm.at[a, :]))
    wait(leaving)


def pack_x_kernel(*refs):
    firsts, lasts = refs[:6], refs[6:12]
    first_out, last_out = refs[12:]
    for group, out in ((firsts, first_out), (lasts, last_out)):
        p = 0
        for ref in group[:5]:
            n = ref.shape[0]
            out[p : p + n] = ref[...]
            p += n
        out[p] = BOND * group[5][...].astype(F32)


def pack_y_kernel(v, cx, cy, st, via, mask, lo, hi, to_left, to_right):
    rows = v.shape[1]

    def pack(planes, at, n):
        lane = lanes(n)
        left = jnp.zeros((n, W), F32)
        right = jnp.zeros((n, W), F32)
        for p, x in enumerate(planes):
            turned = x if p == 0 else pltpu.roll(x, Q * p, axis=1)
            left = jnp.where(lane // Q == p, turned, left)
            right = jnp.where(lane // Q == (p - 1) % (W // Q), turned, right)
        to_left[pl.ds(at, n), :] = left
        to_right[pl.ds(at, n), :] = right

    def tile(i):
        at = pl.ds(i, STEP)
        planes = [ref[l, at, :] for ref in (v, cx, cy, st, via) for l in range(ref.shape[0])]
        planes += [BOND * mask[at, :].astype(F32)]
        pack(planes, pl.multiple_of(i + H, 8), STEP)

    each_chunk(0, rows, tile, STEP)
    count = lo.shape[0]
    pack([lo[p] for p in range(count)], 0, H)
    pack([hi[p] for p in range(count)], H + rows, H)


def rows_of(ref, l=None):
    if l is None:
        return lambda s, n: ref[pl.ds(s, n), :]
    return lambda s, n: ref[l, pl.ds(s, n), :]


def weighted(x, s, n, gx, gy):
    low = pl.multiple_of(s - 8, 8)
    near = rows_of(x)(low, n + 16)
    gnear = rows_of(gx)(low, n + 8)
    c = near[8 : 8 + n]
    g = rows_of(gy)(s, n)
    up = gnear[8 : 8 + n] * near[9 : 9 + n]
    down = (gnear * near[0 : n + 8])[7 : 7 + n]
    return up + down + g * from_right(c) + from_left(g * c)


def base_kernel(*refs):
    place, v, cx, cy, st, via, mask, vp, lo, hi, f_left, f_right = refs[:12]
    refs = list(refs[12:])
    layers, rows = v.shape[0], v.shape[1]
    total = rows + 2 * H

    def take(n):
        got = refs[:n]
        del refs[:n]
        return got

    outs = take(4 * layers + 11)
    [v3_out] = take(1)
    helds = take(4 * layers + 11)
    ev, ecx, ecy, est = take(layers), take(layers), take(layers), take(layers)
    evp, side, d00, d01, d10, z10, z11, z20, e20, sems = take(10)
    copies = Copies(sems)
    home = dict(zip(map(id, helds), outs))

    def give(*held):
        return copies.start(*[(h, home[id(h)]) for h in held])

    refs = list(helds)
    gx, gy, inv, viae = take(layers), take(layers), take(layers), take(layers - 1)
    bond, d02, d03, d11, d12, z12, d20, d21, z21, sb0, vd0, msg = take(12)
    d0 = [d00, d01, d02, d03]
    d1, z1 = [d10, d11, d12], [z10, z11, z12]
    d2, z2 = [e20, d21], [z20, z21]
    dests = [*ev, *ecx, *ecy, *est, *viae, bond]
    main, edge = slice(0, W), slice(W, 2 * W)
    sources = [ref.at[l] for ref in (v, cx, cy, st, via) for l in range(ref.shape[0])]
    arriving = copies.start(
        *[
            (source, dest.at[pl.ds(PAD, rows), pl.ds(0, W)])
            for source, dest in zip([*sources, vp.at[pl.ds(0, rows), :]], [*dests[:-1], evp])
        ]
    )

    def sides(s):
        r = pl.multiple_of(s - H, 8)
        a = f_right[pl.ds(r, WIDE), :]
        b = f_left[pl.ds(r, WIDE), :]
        even = lanes(WIDE) // Q % 2 == 0
        both = [jnp.where(even, a, b), jnp.where(even, b, a)]
        for p, dest in enumerate(dests):
            x = both[p % 2]
            dest[pl.ds(s, WIDE), edge] = x if p == 0 else pltpu.roll(x, W - Q * p, axis=1)
        evp[pl.ds(s, WIDE), edge] = jnp.zeros((WIDE, W), F32)

    each_chunk(H, total, sides, WIDE)

    def bonds(i):
        weight = BOND * mask[pl.ds(i, STEP), :].astype(F32)
        bond[pl.ds(pl.multiple_of(i + PAD, 8), STEP), main] = weight

    each_chunk(0, rows, bonds, STEP)
    for p, dest in enumerate(dests):
        dest[H : 2 * H, main] = lo[p]
        dest[PAD + rows : PAD + rows + H, main] = hi[p]
    evp[H : 2 * H, main] = jnp.zeros((H, W), F32)
    evp[PAD + rows : PAD + rows + H, main] = jnp.zeros((H, W), F32)
    wait(arriving)

    x_first, x_total, y_first, y_total = place[0], place[1], place[2], place[3]
    col = lanes(1, 2 * W)
    col = y_first + jnp.where(col < W + W // 2, col, col - 2 * W)
    nxt = lax.rem(col + 1 + y_total, y_total)
    seam = W // 2
    keep_y = jnp.where((nxt != seam) & (nxt != seam + y_total // 2), 0.5, 0.0).astype(F32)

    def conductances(s):
        row = x_first + s - PAD + lax.broadcasted_iota(jnp.int32, (WIDE, 1), 0)
        keep_x = jnp.where((row != -1) & (row != x_total - 1), 0.5, 0.0).astype(F32)
        for l in range(layers):
            c = ecx[l][pl.ds(s, WIDE + 8), :]
            gx[l][pl.ds(s, WIDE), :] = keep_x * (c[0:WIDE] + c[1 : WIDE + 1])
            c = ecy[l][pl.ds(s, WIDE), :]
            gy[l][pl.ds(s, WIDE), :] = keep_y * (c + from_right(c))

    each_chunk(H, total, conductances, WIDE)
    leaving = give(*gx, *gy, *viae, bond)
    leaving += copies.start((ev[layers - 1], v3_out))

    def start(s):
        n = WIDE
        a = pl.ds(s, n)
        for l in range(layers):
            near = gx[l][pl.ds(pl.multiple_of(s - 8, 8), n + 8), :]
            up, down, right = near[8 : 8 + n], near[7 : 7 + n], gy[l][a, :]
            off = up + down + right + from_left(right)
            nb = weighted(ev[l], s, n, gx[l], gy[l])
            if l < layers - 1:
                off = off + viae[l][a, :]
                nb = nb + viae[l][a, :] * ev[l + 1][a, :]
            else:
                off = off + bond[a, :]
                nb = nb + bond[a, :] * evp[a, :]
            if l > 0:
                off = off + viae[l - 1][a, :]
                nb = nb + viae[l - 1][a, :] * ev[l - 1][a, :]
            c = ev[l][a, :]
            inverse = 1.0 / (est[l][a, :] + off)
            inv[l][a, :] = inverse
            d0[l][a, :] = (nb - off * c) * inverse

    each_chunk(H, total, start, WIDE)
    leaving += give(*inv, d02, d03)

    def links(d, l, s, n):
        nb = weighted(d[l], s, n, gx[l], gy[l])
        if l < layers - 1:
            nb = nb + viae[l][pl.ds(s, n), :] * d[l + 1][pl.ds(s, n), :]
        if l > 0:
            nb = nb + viae[l - 1][pl.ds(s, n), :] * d[l - 1][pl.ds(s, n), :]
        return inv[l][pl.ds(s, n), :] * nb

    def upper(i):
        a, o = pl.ds(pl.multiple_of(i + PAD, 8), STEP), pl.ds(i, STEP)
        for l in range(1, layers):
            vd0[l - 1, o, :] = ev[l][a, main] + d0[l][a, main]

    each_chunk(0, rows, upper, STEP)
    leaving += give(vd0)

    def first(s):
        a = pl.ds(s, WIDE)
        r = pl.ds(pl.multiple_of(s - H, 8), WIDE)
        side[r, :] = d03[a, edge]
        msg[r, :] = d03[a, main]
        for l in range(layers - 1):
            z = links(d0, l, s, WIDE)
            z1[l][a, :] = z
            d1[l][a, :] = A1 * d0[l][a, :] + B1 * z

    each_chunk(H, total, first, WIDE)
    pack_side(side, msg, total, total)
    row = total + 8 * (side.shape[0] // W)
    for product in (False, True):
        def rim(x, product=product):
            part = ev[layers - 1][x]
            return inv[layers - 1][x] * bond[x] if product else part

        msg[row : row + H, :] = rim((slice(H, 2 * H), main))
        msg[row + H : row + 2 * H, :] = rim((slice(PAD + rows, PAD + rows + H), main))

        def lay(s, rim=rim):
            side[pl.ds(pl.multiple_of(s - H, 8), WIDE), :] = rim((pl.ds(s, WIDE), edge))

        each_chunk(H, total, lay, WIDE)
        pack_side(side, msg, row + 2 * H, total)
        row += 2 * H + 8 * (side.shape[0] // W)
    leaving += give(d11, d12, z12, msg)

    def second(s):
        a = pl.ds(s, WIDE)
        for l in range(2):
            z = z1[l][a, :] - d1[l][a, :] + links(d1, l, s, WIDE)
            z2[l][a, :] = z
            d2[l][a, :] = A2 * d1[l][a, :] + B2 * z

    each_chunk(H, total, second, WIDE)
    leaving += give(d21, z21)

    def third(s):
        a = pl.ds(s, STEP)
        o = pl.ds(pl.multiple_of(s - PAD, 8), STEP)
        nb = weighted(e20, s, STEP, gx[0], gy[0])[:, main]
        nb = inv[0][a, main] * (nb + viae[0][a, main] * d21[a, main])
        d = e20[a, main]
        z = z20[a, main] - d + nb
        d20[o, :] = d
        sb0[o, :] = ev[0][a, main] + d00[a, main] + d10[a, main] + (1.0 + A3) * d + B3 * z

    each_chunk(PAD, rows, third, STEP)
    leaving += give(d20, sb0)
    wait(leaving)


def pack_side(side, msg, row, total):
    for j in range(-(-total // W)):
        t = side[W * j : W * j + W, :].T
        msg[row + 8 * j : row + 8 * j + Q, :] = t[0:Q]
        msg[row + 8 * j + Q : row + 8 * j + 2 * Q, :] = t[W - Q : W]


def unpack_side(msg, row, total, u):
    blocks = []
    for j in range(-(-total // W)):
        u[0:Q, :] = msg[row + 8 * j : row + 8 * j + Q, :]
        u[W - Q : W, :] = msg[row + 8 * j + Q : row + 8 * j + 2 * Q, :]
        blocks.append((H + W * j, min(W, total - W * j), u[...].T))
    return blocks


def first_top_kernel(part, *refs):
    inputs, (d_hbm, z_hbm, delta_hbm, msg), held = refs[:8], refs[8:12], refs[12:20]
    low, d0, v3, gx, gy, inv, via, bond = held
    d_out, z_out, delta, ep, side, u, part_held, sems = refs[20:]
    copies = Copies(sems)
    [came] = copies.start((part, part_held))
    part = part_held
    arriving = copies.start(*zip(inputs, held))
    rows = part.shape[0] - 3 * (2 * H + 8 * (side.shape[0] // W))
    total = rows + 2 * H
    sides = 8 * (side.shape[0] // W)
    main, edge = slice(0, W), slice(W, 2 * W)
    u[...] = jnp.zeros_like(u)
    came.wait()
    row = total + sides
    own = unpack_side(part, row + 2 * H, total, u)
    others = unpack_side(part, row + 2 * H + sides + 2 * H, total, u)
    theirs = unpack_side(part, total, total, u)
    wait(arriving)
    delta[PAD : PAD + rows, main] = jnp.zeros((rows, W), F32)
    ep[PAD : PAD + rows, main] = part[H : H + rows, :]

    def halo(a, cols, v_part, weight_part, d_part):
        x = inv[a, cols] * bond[a, cols] * v_part
        delta[a, cols] = x
        d0[a, cols] = d0[a, cols] + x
        ep[a, cols] = d_part + weight_part * v3[a, cols]

    for k, first in ((0, H), (1, PAD + rows)):
        at = row + H * k
        halo(
            slice(first, first + H), main, part[at : at + H, :],
            part[at + 2 * H + sides : at + 3 * H + sides, :], part[first - H : first, :],
        )
    for (first, n, a), (_, _, b), (_, _, c) in zip(own, others, theirs):
        halo(slice(first, first + n), edge, a[:n], b[:n], c[:n])

    def body(s):
        a = pl.ds(s, WIDE)
        r = pl.ds(pl.multiple_of(s - H, 8), WIDE)
        nb = weighted(d0, s, WIDE, gx, gy) + via[a, :] * low[a, :] + bond[a, :] * ep[a, :]
        x = inv[a, :] * nb
        d = A1 * d0[a, :] + B1 * x
        z_out[a, :] = x
        d_out[a, :] = d
        side[r, :] = d[:, W:]
        msg[r, :] = d[:, :W]

    each_chunk(H, total, body, WIDE)
    leaving = copies.start((d_out, d_hbm), (z_out, z_hbm), (delta, delta_hbm))
    pack_side(side, msg, total, total)
    wait(leaving)


def second_top_kernel(low, inv_low, delta, here, z, part, gx, gy, inv, via, bond, d_out, z_out, msg, weight, ep, u):
    rows = msg.shape[0]
    total = rows + 2 * H
    u[...] = jnp.zeros_like(u)
    for first, n, x in unpack_side(part, total, total, u):
        ep[first : first + n, :] = x[:n]

    def body(s):
        a = pl.ds(s, WIDE)
        r = pl.ds(pl.multiple_of(s - H, 8), WIDE)
        other = jnp.concatenate([part[r, :], ep[a, :]], axis=1)
        under = low[a, :] + B1 * inv_low[a, :] * via[a, :] * delta[a, :]
        nb = weighted(here, s, WIDE, gx, gy) + via[a, :] * under + bond[a, :] * other
        c = here[a, :]
        x = z[a, :] - c + inv[a, :] * nb
        z_out[a, :] = x
        d_out[a, :] = A2 * c + B2 * x

    each_chunk(H, total, body, WIDE)
    msg[...] = d_out[PAD : PAD + rows, 0:W]
    weight[...] = inv[PAD : PAD + rows, 0:W] * bond[PAD : PAD + rows, 0:W]


def final_kernel(
    v0, vd0, d11, b12, z12, e11, d13, d20, b21, e21, d23, z21, ze21, z23, delta,
    gx1, gx2, gx3, gy1, gy2, gy3, inv1, inv2, inv3, via0, via1, via2,
    out, d22, z22, d21, d12,
):
    main = slice(0, W)
    rows = out.shape[1]

    def amend(s):
        a = pl.ds(s, WIDE)
        c = inv2[a, :] * via2[a, :] * delta[a, :]
        z22[a, :] = z12[a, :] + c
        c = B1 * c
        d12[a, :] = b12[a, :] + c
        d21[a, :] = b21[a, :] + e21[a, :] + B2 * inv1[a, :] * via1[a, :] * c

    each_chunk(H, rows + 2 * H, amend, WIDE)

    def middle(s):
        a = pl.ds(s, WIDE)
        this = d12[a, :]
        nb = weighted(d12, s, WIDE, gx2, gy2)
        nb = nb + via1[a, :] * (d11[a, :] + e11[a, :]) + via2[a, :] * d13[a, :]
        z = z22[a, :] - this + inv2[a, :] * nb
        z22[a, :] = z
        d22[a, :] = A2 * this + B2 * z

    each_chunk(H, rows + 2 * H, middle, WIDE)
    gx, gy, inv = [None, gx1, gx2, gx3], [None, gy1, gy2, gy3], [None, inv1, inv2, inv3]
    via = [via0, via1, via2]
    d2, z2 = [None, d21, d22, d23], [None, None, z22, z23]

    def body(i):
        s = pl.multiple_of(i + PAD, 8)
        a, o = pl.ds(s, STEP), pl.ds(i, STEP)
        out[0, o, :] = v0[o, :]
        first = [None, d11[a, main] + e11[a, main], d12[a, main], d13[a, main]]
        below = d20[o, :]
        for l in range(1, 4):
            nb = weighted(d2[l], s, STEP, gx[l], gy[l])[:, main]
            nb = nb + via[l - 1][a, main] * below
            below = d2[l][a, main]
            if l < 3:
                nb = nb + via[l][a, main] * d2[l + 1][a, main]
            z = (z21[a, main] + ze21[o, :] if l == 1 else z2[l][a, main]) - below + inv[l][a, main] * nb
            out[l, o, :] = vd0[l - 1, o, :] + first[l] + (1.0 + A3) * below + B3 * z

    each_chunk(0, rows, body, STEP)


def map_kernel(arrived, out, first, last, labels, vec, lab, a0, a1, a2, a3, sem):
    devices = vec.shape[1]
    rows = out.shape[0]
    slots = arrived[pl.ds(CAP * 8, devices, stride=ROWS_MSG), :]
    vec[...] = slots.T[0:8].astype(jnp.int32)
    copy = pltpu.make_async_copy(vec, lab, sem)
    copy.start()
    parts = (a0, a1, a2, a3)
    for acc in parts:
        acc[...] = jnp.zeros_like(acc)
    copy.wait()

    @pl.loop(0, devices // 8, unroll=4)
    def _(g):
        n = ROWS_MSG * 8
        data = arrived[pl.ds(pl.multiple_of(g * n, 8), n), :]
        for j in range(8):
            for r in range(CAP):
                slot = lab[r, g * 8 + j]
                labels[(g * 8 + j) * CAP + r] = slot
                a = pl.ds(pl.multiple_of(slot * 8, 8), 8)
                acc = parts[(j * CAP + r) % 4]
                acc[a, :] += data[j * ROWS_MSG + r * 8 : j * ROWS_MSG + r * 8 + 8]

    out[...] = (a0[0:rows, :] + a1[0:rows, :]) + (a2[0:rows, :] + a3[0:rows, :])
    first[...] = out[0:8, :]
    last[...] = out[rows - 8 : rows, :]


def edges_kernel(cur, lo, hi, to_left, to_right, ext):
    rows = cur.shape[0]
    ext[0:H, :] = lo[...]
    ext[H : H + rows, :] = cur[...]
    ext[H + rows : rows + 2 * H, :] = hi[...]
    for j in range(to_left.shape[1] // W):
        t = ext[W * j : W * j + W, :].T
        to_left[:, W * j : W * j + W] = t[0:8]
        to_right[:, W * j : W * j + W] = t[W - 8 : W]


def effect_kernel(
    labels, cur, lo, hi, f_left, f_right, *refs
):
    (inv0, gx0, gy0, via0, inv1, gx1, gy1, sb0, d20), refs = refs[:9], refs[9:]
    v0_out, picked_out, e11_out, e21_out, z21_out, d20_out = refs[:6]
    ec, e0, e1, z10, z11, e2, z20, e11, e21, u, acc, z21, d20_sum, picked, sems = refs[6:]
    copies = Copies(sems)
    rows = cur.shape[0]
    total = rows + 2 * H
    main, edge = slice(0, W), slice(W, 2 * W)
    ec[H : 2 * H, main] = lo[...]
    ec[PAD : PAD + rows, main] = cur[...]
    ec[PAD + rows : PAD + rows + H, main] = hi[...]
    u[...] = jnp.zeros_like(u)
    for j in range(f_left.shape[1] // W):
        u[0:8, :] = f_right[:, W * j : W * j + W]
        u[W - 8 : W, :] = f_left[:, W * j : W * j + W]
        n = min(W, total - W * j)
        ec[H + W * j : H + W * j + n, edge] = u[...].T[:n]

    def zeroth(s):
        a = pl.ds(s, WIDE)
        e0[a, :] = inv0[a, :] * ec[a, :]

    each_chunk(H, total, zeroth, WIDE)
    def first(s):
        a = pl.ds(s, WIDE)
        here = e0[a, :]
        z = inv0[a, :] * weighted(e0, s, WIDE, gx0, gy0)
        z10[a, :] = z
        e1[a, :] = A1 * here + B1 * z
        z = inv1[a, :] * via0[a, :] * here
        z11[a, :] = z
        e11[a, :] = B1 * z

    each_chunk(H, total, first, WIDE)
    def second(s):
        a = pl.ds(s, WIDE)
        low, high, between = e1[a, :], e11[a, :], via0[a, :]
        nb = weighted(e1, s, WIDE, gx0, gy0) + between * high
        z = z10[a, :] - low + inv0[a, :] * nb
        z20[a, :] = z
        e2[a, :] = A2 * low + B2 * z
        nb = weighted(e11, s, WIDE, gx1, gy1) + between * low
        z = z11[a, :] - high + inv1[a, :] * nb
        z11[a, :] = z
        e21[a, :] = A2 * high + B2 * z

    each_chunk(H, total, second, WIDE)
    copies.start((e11, e11_out), (e21, e21_out))
    def third(i):
        s = pl.multiple_of(i + PAD, 8)
        a, o = pl.ds(s, STEP), pl.ds(i, STEP)
        here = e2[a, main]
        nb = weighted(e2, s, STEP, gx0, gy0)[:, main] + via0[a, main] * e21[a, main]
        z = z20[a, main] - here + inv0[a, main] * nb
        whole = sb0[o, :] + e0[a, main] + e1[a, main] + (1.0 + A3) * here + B3 * z
        acc[o, :] = whole
        d20_sum[o, :] = d20[o, :] + here
        z21[o, :] = z11[a, main]

    each_chunk(0, rows, third, STEP)
    copies.start((acc.at[pl.ds(0, rows), :], v0_out), (z21, z21_out), (d20_sum, d20_out))
    acc[rows : rows + 8, :] = jnp.zeros((8, W), F32)

    def pick(k):
        picked[pl.ds(pl.multiple_of(k * 8, 8), 8), :] = acc[
            pl.ds(pl.multiple_of(labels[k] * 8, 8), 8), :
        ]

    count = labels.shape[0] // 4
    for part in range(4):
        pl.loop(part * count, (part + 1) * count, unroll=8)(pick)
        a = pl.ds(part * count * 8, count * 8)
        copies.start((picked.at[a, :], picked_out.at[a, :]))
    wait(copies.made)


def last_kernel(dest, back, field, part, weight, out, top):
    top[0] = field[0] + B3 * weight[...] * part[...]

    @pl.loop(0, out.shape[0], unroll=16)
    def _(k):
        out[k] = back[pl.ds(pl.multiple_of(dest[k] * 8, 8), 8), :]


def ring(axis, step):
    n = lax.axis_size(axis)
    return [(i, (i + step) % n) for i in range(n)]


def shift(x, axis, step):
    return lax.ppermute(x, axis, ring(axis, step))


def facing(x, step=0):
    n, m = lax.axis_size("gx"), lax.axis_size("yt")
    pairs = [
        (g * m + t, ((g + step) % n) * m + (t ^ (m // 2))) for g in range(n) for t in range(m)
    ]
    return lax.ppermute(x, ALL, pairs)


def on_device(v, st, cx, cy, via, mask, blocks, owner, slot):
    layers, rows, cols = v.shape
    devices = lax.axis_size("gx") * lax.axis_size("yt")
    nb = blocks.shape[0]
    total = rows + 2 * H
    nr = total + 2 * H
    side_blocks = -(-total // W)
    place = jnp.stack(
        [
            lax.axis_index("gx") * rows,
            jnp.int32(rows * lax.axis_size("gx")),
            lax.axis_index("yt") * cols,
            jnp.int32(cols * lax.axis_size("yt")),
        ]
    ).astype(jnp.int32)

    outgoing, dest, v_top = call(
        send_kernel,
        [
            pltpu.HBM((devices * ROWS_MSG, W), F32),
            jax.ShapeDtypeStruct((nb,), jnp.int32),
            pltpu.HBM((rows + TAIL, W), F32),
        ],
        [owner.reshape(nb), slot, blocks, v],
        scratch=[
            pltpu.SMEM((devices,), jnp.int32),
            pltpu.VMEM((devices * CAP * 8, W), F32),
            pltpu.VMEM((devices, W), jnp.int32),
            pltpu.VMEM((devices * ROWS_MSG, W), F32),
            pltpu.VMEM((rows + TAIL, W), F32),
            pltpu.SemaphoreType.DMA((6,)),
        ],
        specs={0: SMEM, 1: SMEM, 3: ANY},
        out_specs=[ANY, SMEM, ANY],
        far=(3,),
    )
    sources = [v, cx, cy, st, via]
    args = sources + [mask] + sources + [mask]
    specs = {}
    last = rows // 8 - 1
    for i in range(5):
        n = sources[i].shape[0]
        specs[i] = pl.BlockSpec((n, 8, W), lambda _: (0, 0, 0))
        specs[6 + i] = pl.BlockSpec((n, 8, W), lambda _: (0, last, 0))
    specs[5] = pl.BlockSpec((8, W), lambda _: (0, 0))
    specs[11] = pl.BlockSpec((8, W), lambda _: (last, 0))
    count = 5 * layers
    first_rows, last_rows = pl.pallas_call(
        pack_x_kernel,
        grid=(1,),
        out_shape=[shape(count, 8, W)] * 2,
        in_specs=[specs[i] for i in range(12)],
        out_specs=[
            pl.BlockSpec((count, 8, W), lambda _: (0, 0, 0)),
            pl.BlockSpec((count, 8, W), lambda _: (0, 0, 0)),
        ],
        name="pack_x_kernel",
        compiler_params=pltpu.CompilerParams(vmem_limit_bytes=58 << 20),
        cost_estimate=pl.CostEstimate(flops=1, bytes_accessed=1_000_000, transcendentals=0),
    )(*args)
    lo = shift(last_rows, "gx", 1)
    hi = shift(first_rows, "gx", -1)
    lo, hi, v_top, outgoing = lax.optimization_barrier((lo, hi, v_top, outgoing))
    v_part = facing(v_top)
    tiles = [v, cx, cy, st, via, mask]
    to_left, to_right = call(
        pack_y_kernel, [shape(total, W), shape(total, W)], [*tiles, lo, hi], vmem=8
    )
    f_left = shift(to_right, "yt", 1)
    f_right = shift(to_left, "yt", -1)
    outgoing, f_left, f_right, v_part = lax.optimization_barrier(
        (outgoing, f_left, f_right, v_part)
    )
    arrived = lax.all_to_all(
        outgoing.reshape(devices, ROWS_MSG, 1, W), ALL, 0, 0, tiled=True
    ).reshape(devices * ROWS_MSG, W)

    one = shape(nr, 2 * W)
    tile = shape(rows, W)
    buffer = lambda *d: pltpu.VMEM(d, F32)
    msg_shape = shape(total + 8 * side_blocks, W)
    held = [one] * (4 * layers + 5)
    msg0_shape = shape(3 * (total + 8 * side_blocks) - 2 * rows, W)
    held += [tile, one, one, tile, shape(layers - 1, rows, W), msg0_shape]
    outs = call(
        base_kernel,
        [*held, one],
        [place, *tiles, v_part, lo, hi, f_left, f_right],
        scratch=[buffer(*h.shape) for h in held]
        + [buffer(nr, 2 * W)] * (4 * layers + 1)
        + [buffer(side_blocks * W, W)]
        + [buffer(nr, 2 * W)] * 7
        + [pltpu.SemaphoreType.DMA((9 * layers + 20,))],
        specs={0: SMEM, 1: ANY, 2: ANY, 3: ANY, 4: ANY, 5: ANY, 7: ANY},
        out_specs=[ANY] * (len(held) + 1),
        vmem=VMEM_BASE,
        cost=20_000_000,
    )
    gx, gy, inv, via_e = outs[0:4], outs[4:8], outs[8:12], outs[12:15]
    bond, d02, d03, d11, d12, z12, d20, d21, z21, sb0, vd0, msg0, v3 = outs[15:]
    part0 = facing(msg0)

    cur, cur_first, cur_last, labels = call(
        map_kernel,
        [tile, shape(8, W), shape(8, W), jax.ShapeDtypeStruct((devices * CAP,), jnp.int32)],
        [arrived],
        scratch=[
            pltpu.VMEM((8, devices), jnp.int32),
            pltpu.SMEM((8, devices), jnp.int32),
            *[buffer(rows + 8, W)] * 4,
            pltpu.SemaphoreType.DMA,
        ],
        out_specs=[pl.BlockSpec(memory_space=pltpu.VMEM)] * 3 + [SMEM],
    )
    cur_lo = shift(cur_last, "gx", 1)
    cur_hi = shift(cur_first, "gx", -1)
    top = [gx[3], gy[3], inv[3], via_e[2], bond]
    cur_left, cur_right = call(
        edges_kernel,
        [shape(8, side_blocks * W)] * 2,
        [cur, cur_lo, cur_hi],
        scratch=[buffer(side_blocks * W, W)],
    )
    labels, part0 = lax.optimization_barrier((labels, part0))
    far_one = pltpu.HBM((nr, 2 * W), F32)
    d13, z13, delta, msg1 = call(
        first_top_kernel,
        [far_one, far_one, far_one, msg_shape],
        [part0, d02, d03, v3, *top],
        scratch=[buffer(nr, 2 * W)] * 12
        + [buffer(side_blocks * W, W), buffer(W, W), buffer(*msg0_shape.shape)]
        + [pltpu.SemaphoreType.DMA((12,))],
        specs={i: ANY for i in range(9)},
        out_specs=[ANY] * 3 + [pl.BlockSpec(memory_space=pltpu.VMEM)],
        vmem=VMEM_TOP,
        far=range(9),
    )
    cur_left, cur_right, msg1 = lax.optimization_barrier((cur_left, cur_right, msg1))
    part1 = facing(msg1)
    d23, z23, msg2, weight = call(
        second_top_kernel,
        [one, one, tile, tile],
        [d12, inv[2], delta, d13, z13, part1, *top],
        scratch=[buffer(nr, W), buffer(W, W)],
        vmem=VMEM_FINAL,
    )

    cur_f_left = shift(cur_right, "yt", 1)
    cur_f_right = shift(cur_left, "yt", -1)
    v0, picked, e11, e21, ze21, d20 = call(
        effect_kernel,
        [pltpu.HBM(d, F32) for d in (
            (rows, W), (devices * CAP * 8, W), (nr, 2 * W), (nr, 2 * W), (rows, W), (rows, W))],
        [labels, cur, cur_lo, cur_hi, cur_f_left, cur_f_right,
         inv[0], gx[0], gy[0], via_e[0], inv[1], gx[1], gy[1], sb0, d20],
        scratch=[buffer(nr, 2 * W)] * 9
        + [buffer(W, W), buffer(rows + 8, W), buffer(rows, W), buffer(rows, W)]
        + [buffer(devices * CAP * 8, W), pltpu.SemaphoreType.DMA((9,))],
        specs={0: SMEM},
        out_specs=[ANY] * 6,
        vmem=VMEM_EFFECT,
    )
    picked, part1 = lax.optimization_barrier((picked, part1))
    part2 = facing(msg2)
    back = lax.all_to_all(picked, ALL, 0, 0, tiled=True)

    voltage = call(
        final_kernel,
        shape(layers, rows, W),
        [v0, vd0, d11, d12, z12, e11, d13, d20, d21, e21, d23, z21, ze21, z23, delta,
         *gx[1:], *gy[1:], *inv[1:], *via_e],
        scratch=[buffer(nr, 2 * W)] * 4,
        vmem=VMEM_FINAL,
        cost=10_000_000,
    )
    whole = pl.BlockSpec(memory_space=pltpu.VMEM)
    upper = pl.BlockSpec((1, rows, W), lambda _: (layers - 1, 0, 0))
    block_voltage, voltage = pl.pallas_call(
        last_kernel,
        grid=(1,),
        out_shape=[shape(nb, 8, W), shape(layers, rows, W)],
        in_specs=[SMEM, whole, upper, whole, whole],
        out_specs=[whole, upper],
        input_output_aliases={2: 1},
        name="last_kernel",
        compiler_params=pltpu.CompilerParams(vmem_limit_bytes=8 << 20),
    )(dest, back, voltage, part2, weight)
    return voltage, block_voltage


def solution(mesh):
    tile = P(None, "gx", "yt")
    return jax.shard_map(
        on_device,
        mesh=mesh,
        in_specs=(tile, tile, tile, tile, tile, P("gx", "yt"), P(ALL, None, None), P(ALL, None), P(ALL)),
        out_specs=(tile, P(ALL, None, None)),
        check_vma=False,
    )
```

```python
import jax
import jax.numpy as jnp
from jax import lax
from jax.experimental import pallas as pl
from jax.experimental.pallas import tpu as pltpu
from jax.sharding import PartitionSpec as P

CAP = 2
TAIL = 24
BOND = 2.0
CENTER = 1.0
HALFWIDTH = 0.97
SIGMA = CENTER / HALFWIDTH
RHO0 = 1.0 / SIGMA
RHO1 = 1.0 / (2.0 * SIGMA - RHO0)
RHO2 = 1.0 / (2.0 * SIGMA - RHO1)
RHO3 = 1.0 / (2.0 * SIGMA - RHO2)
A1, B1 = RHO1 * RHO0, 2.0 * RHO1 / HALFWIDTH
A2, B2 = RHO2 * RHO1, 2.0 * RHO2 / HALFWIDTH
A3, B3 = RHO3 * RHO2, 2.0 * RHO3 / HALFWIDTH

VMEM_BASE, VMEM_TOP, VMEM_EFFECT, VMEM_FINAL = 58, 20, 16, 58

ALL = ("gx", "yt")
F32 = jnp.float32
W = 128
H = 8
PAD = 16
Q = 4
LONG = 176
WIDE = 88
STEP = 128
ROWS_MSG = CAP * 8 + 1


def call(kernel, out, args, scratch=(), specs=None, out_specs=None, vmem=6, cost=1_000_000, far=()):
    specs = specs or {}
    in_specs = [
        specs.get(i, pl.BlockSpec(memory_space=pltpu.VMEM)) for i in range(len(args))
    ]
    args = [
        pltpu.with_memory_space_constraint(x, pltpu.HBM) if i in far else x
        for i, x in enumerate(args)
    ]
    many = isinstance(out, (list, tuple))
    outs = list(out) if many else [out]
    o_specs = out_specs or [pl.BlockSpec(memory_space=pltpu.VMEM)] * len(outs)
    return pl.pallas_call(
        kernel,
        out_shape=outs if many else outs[0],
        in_specs=in_specs,
        out_specs=o_specs if many else o_specs[0],
        scratch_shapes=list(scratch),
        name=kernel.__name__,
        compiler_params=pltpu.CompilerParams(vmem_limit_bytes=vmem << 20),
        cost_estimate=pl.CostEstimate(flops=cost, bytes_accessed=cost, transcendentals=0),
    )(*args)


def shape(*dims):
    return jax.ShapeDtypeStruct(dims, F32)


SMEM = pl.BlockSpec(memory_space=pltpu.SMEM)
ANY = pl.BlockSpec(memory_space=pl.ANY)
HBM = pl.BlockSpec(memory_space=pltpu.HBM)


class Copies:
    def __init__(self, sems):
        self.sems, self.made = sems, []

    def start(self, *pairs):
        begun = []
        for source, target in pairs:
            copy = pltpu.make_async_copy(source, target, self.sems.at[len(self.made)])
            copy.start()
            self.made.append(copy)
            begun.append(copy)
        return begun


def wait(copies):
    for copy in copies:
        copy.wait()


def from_right(x):
    return pltpu.roll(x, x.shape[-1] - 1, axis=1)


def from_left(x):
    return pltpu.roll(x, 1, axis=1)


def lanes(rows, width=W):
    return lax.broadcasted_iota(jnp.int32, (rows, width), 1)


def each_chunk(first, rows, body, step):
    @pl.loop(0, rows // step)
    def _(k):
        body(pl.multiple_of(first + k * step, 8))


def send_kernel(
    owner_ref, slot_ref, blocks_ref, v_ref, out_hbm, dest_ref, top_hbm,
    count_ref, buf, slots, out_ref, top_ref, sems,
):
    devices = count_ref.shape[0]
    copies = Copies(sems)
    rows = v_ref.shape[1]
    top = v_ref.at[v_ref.shape[0] - 1]
    [fetch] = copies.start((top, top_ref.at[pl.ds(0, rows), :]))

    @pl.loop(0, devices, unroll=8)
    def _(o):
        count_ref[o] = 0

    buf[...] = jnp.zeros_like(buf)
    slots[...] = jnp.full(slots.shape, 64, jnp.int32)
    lane = lanes(1)

    @pl.loop(0, blocks_ref.shape[0], unroll=8)
    def _(k):
        owner = owner_ref[k]
        rank = count_ref[owner]
        count_ref[owner] = rank + 1
        dest = owner * CAP + rank
        dest_ref[k] = dest
        buf[pl.ds(pl.multiple_of(dest * 8, 8), 8), :] = blocks_ref[k]
        row = slots[pl.ds(owner, 1), :]
        slots[pl.ds(owner, 1), :] = jnp.where(lane == rank, slot_ref[k], row)

    def assemble(g):
        data = buf[pl.ds(pl.multiple_of(g * CAP * 64, 8), CAP * 64), :]
        label = slots[pl.ds(pl.multiple_of(g * 8, 8), 8), :].astype(F32)
        pieces = []
        for j in range(8):
            pieces += [data[CAP * 8 * j : CAP * 8 * (j + 1)], label[j : j + 1]]
        out_ref[pl.ds(pl.multiple_of(g * ROWS_MSG * 8, 8), ROWS_MSG * 8), :] = (
            jnp.concatenate(pieces, axis=0)
        )

    fetch.wait()
    top_ref[rows:, :] = jnp.zeros((TAIL, W), F32)
    leaving = copies.start((top_ref, top_hbm))
    groups = devices // 8 // 4
    for part in range(4):
        pl.loop(part * groups, (part + 1) * groups, unroll=2)(assemble)
        n = groups * 8 * ROWS_MSG
        a = pl.ds(part * n, n)
        leaving += copies.start((out_ref.at[a, :], out_hbm.at[a, :]))
    wait(leaving)


def pack_x_kernel(*refs):
    firsts, lasts = refs[:6], refs[6:12]
    first_out, last_out = refs[12:]
    for group, out in ((firsts, first_out), (lasts, last_out)):
        p = 0
        for ref in group[:5]:
            n = ref.shape[0]
            out[p : p + n] = ref[...]
            p += n
        out[p] = BOND * group[5][...].astype(F32)


def pack_y_kernel(v, cx, cy, st, via, mask, lo, hi, to_left, to_right):
    rows = v.shape[1]

    def pack(planes, at, n):
        lane = lanes(n)
        left = jnp.zeros((n, W), F32)
        right = jnp.zeros((n, W), F32)
        for p, x in enumerate(planes):
            turned = x if p == 0 else pltpu.roll(x, Q * p, axis=1)
            left = jnp.where(lane // Q == p, turned, left)
            right = jnp.where(lane // Q == (p - 1) % (W // Q), turned, right)
        to_left[pl.ds(at, n), :] = left
        to_right[pl.ds(at, n), :] = right

    def tile(i):
        at = pl.ds(i, STEP)
        planes = [ref[l, at, :] for ref in (v, cx, cy, st, via) for l in range(ref.shape[0])]
        planes += [BOND * mask[at, :].astype(F32)]
        pack(planes, pl.multiple_of(i + H, 8), STEP)

    each_chunk(0, rows, tile, STEP)
    count = lo.shape[0]
    pack([lo[p] for p in range(count)], 0, H)
    pack([hi[p] for p in range(count)], H + rows, H)


def rows_of(ref, l=None):
    if l is None:
        return lambda s, n: ref[pl.ds(s, n), :]
    return lambda s, n: ref[l, pl.ds(s, n), :]


def weighted(x, s, n, gx, gy):
    low = pl.multiple_of(s - 8, 8)
    near = rows_of(x)(low, n + 16)
    gnear = rows_of(gx)(low, n + 8)
    c = near[8 : 8 + n]
    g = rows_of(gy)(s, n)
    up = gnear[8 : 8 + n] * near[9 : 9 + n]
    down = (gnear * near[0 : n + 8])[7 : 7 + n]
    return up + down + g * from_right(c) + from_left(g * c)


def base_kernel(*refs):
    place, v, cx, cy, st, via, mask, vp, lo, hi, f_left, f_right = refs[:12]
    refs = list(refs[12:])
    layers, rows = v.shape[0], v.shape[1]
    total = rows + 2 * H

    def take(n):
        got = refs[:n]
        del refs[:n]
        return got

    outs = take(4 * layers + 11)
    [v3_out] = take(1)
    helds = take(4 * layers + 11)
    ev, ecx, ecy, est = take(layers), take(layers), take(layers), take(layers)
    evp, side, d00, d01, d10, z10, z11, z20, e20, sems = take(10)
    copies = Copies(sems)
    home = dict(zip(map(id, helds), outs))

    def give(*held):
        return copies.start(*[(h, home[id(h)]) for h in held])

    refs = list(helds)
    gx, gy, inv, viae = take(layers), take(layers), take(layers), take(layers - 1)
    bond, d02, d03, d11, d12, z12, d20, d21, z21, sb0, vd0, msg = take(12)
    d0 = [d00, d01, d02, d03]
    d1, z1 = [d10, d11, d12], [z10, z11, z12]
    d2, z2 = [e20, d21], [z20, z21]
    dests = [*ev, *ecx, *ecy, *est, *viae, bond]
    main, edge = slice(0, W), slice(W, 2 * W)
    sources = [ref.at[l] for ref in (v, cx, cy, st, via) for l in range(ref.shape[0])]
    arriving = copies.start(
        *[
            (source, dest.at[pl.ds(PAD, rows), pl.ds(0, W)])
            for source, dest in zip([*sources, vp.at[pl.ds(0, rows), :]], [*dests[:-1], evp])
        ]
    )

    def sides(s):
        r = pl.multiple_of(s - H, 8)
        a = f_right[pl.ds(r, WIDE), :]
        b = f_left[pl.ds(r, WIDE), :]
        even = lanes(WIDE) // Q % 2 == 0
        both = [jnp.where(even, a, b), jnp.where(even, b, a)]
        for p, dest in enumerate(dests):
            x = both[p % 2]
            dest[pl.ds(s, WIDE), edge] = x if p == 0 else pltpu.roll(x, W - Q * p, axis=1)
        evp[pl.ds(s, WIDE), edge] = jnp.zeros((WIDE, W), F32)

    each_chunk(H, total, sides, WIDE)

    def bonds(i):
        weight = BOND * mask[pl.ds(i, STEP), :].astype(F32)
        bond[pl.ds(pl.multiple_of(i + PAD, 8), STEP), main] = weight

    each_chunk(0, rows, bonds, STEP)
    for p, dest in enumerate(dests):
        dest[H : 2 * H, main] = lo[p]
        dest[PAD + rows : PAD + rows + H, main] = hi[p]
    evp[H : 2 * H, main] = jnp.zeros((H, W), F32)
    evp[PAD + rows : PAD + rows + H, main] = jnp.zeros((H, W), F32)
    wait(arriving)

    x_first, x_total, y_first, y_total = place[0], place[1], place[2], place[3]
    col = lanes(1, 2 * W)
    col = y_first + jnp.where(col < W + W // 2, col, col - 2 * W)
    nxt = lax.rem(col + 1 + y_total, y_total)
    seam = W // 2
    keep_y = jnp.where((nxt != seam) & (nxt != seam + y_total // 2), 0.5, 0.0).astype(F32)

    def conductances(s):
        row = x_first + s - PAD + lax.broadcasted_iota(jnp.int32, (WIDE, 1), 0)
        keep_x = jnp.where((row != -1) & (row != x_total - 1), 0.5, 0.0).astype(F32)
        for l in range(layers):
            c = ecx[l][pl.ds(s, WIDE + 8), :]
            gx[l][pl.ds(s, WIDE), :] = keep_x * (c[0:WIDE] + c[1 : WIDE + 1])
            c = ecy[l][pl.ds(s, WIDE), :]
            gy[l][pl.ds(s, WIDE), :] = keep_y * (c + from_right(c))

    each_chunk(H, total, conductances, WIDE)
    leaving = give(*gx, *gy, *viae, bond)
    leaving += copies.start((ev[layers - 1], v3_out))

    def start(s):
        n = WIDE
        a = pl.ds(s, n)
        for l in range(layers):
            near = gx[l][pl.ds(pl.multiple_of(s - 8, 8), n + 8), :]
            up, down, right = near[8 : 8 + n], near[7 : 7 + n], gy[l][a, :]
            off = up + down + right + from_left(right)
            nb = weighted(ev[l], s, n, gx[l], gy[l])
            if l < layers - 1:
                off = off + viae[l][a, :]
                nb = nb + viae[l][a, :] * ev[l + 1][a, :]
            else:
                off = off + bond[a, :]
                nb = nb + bond[a, :] * evp[a, :]
            if l > 0:
                off = off + viae[l - 1][a, :]
                nb = nb + viae[l - 1][a, :] * ev[l - 1][a, :]
            c = ev[l][a, :]
            inverse = 1.0 / (est[l][a, :] + off)
            inv[l][a, :] = inverse
            d0[l][a, :] = (nb - off * c) * inverse

    each_chunk(H, total, start, WIDE)
    leaving += give(*inv, d02, d03)

    def links(d, l, s, n):
        nb = weighted(d[l], s, n, gx[l], gy[l])
        if l < layers - 1:
            nb = nb + viae[l][pl.ds(s, n), :] * d[l + 1][pl.ds(s, n), :]
        if l > 0:
            nb = nb + viae[l - 1][pl.ds(s, n), :] * d[l - 1][pl.ds(s, n), :]
        return inv[l][pl.ds(s, n), :] * nb

    def upper(i):
        a, o = pl.ds(pl.multiple_of(i + PAD, 8), STEP), pl.ds(i, STEP)
        for l in range(1, layers):
            vd0[l - 1, o, :] = ev[l][a, main] + d0[l][a, main]

    each_chunk(0, rows, upper, STEP)
    leaving += give(vd0)

    def first(s):
        a = pl.ds(s, WIDE)
        r = pl.ds(pl.multiple_of(s - H, 8), WIDE)
        side[r, :] = d03[a, edge]
        msg[r, :] = d03[a, main]
        for l in range(layers - 1):
            z = links(d0, l, s, WIDE)
            z1[l][a, :] = z
            d1[l][a, :] = A1 * d0[l][a, :] + B1 * z

    each_chunk(H, total, first, WIDE)
    pack_side(side, msg, total, total)
    row = total + 8 * (side.shape[0] // W)
    for product in (False, True):
        def rim(x, product=product):
            part = ev[layers - 1][x]
            return inv[layers - 1][x] * bond[x] if product else part

        msg[row : row + H, :] = rim((slice(H, 2 * H), main))
        msg[row + H : row + 2 * H, :] = rim((slice(PAD + rows, PAD + rows + H), main))

        def lay(s, rim=rim):
            side[pl.ds(pl.multiple_of(s - H, 8), WIDE), :] = rim((pl.ds(s, WIDE), edge))

        each_chunk(H, total, lay, WIDE)
        pack_side(side, msg, row + 2 * H, total)
        row += 2 * H + 8 * (side.shape[0] // W)
    leaving += give(d11, d12, z12, msg)

    def second(s):
        a = pl.ds(s, WIDE)
        for l in range(2):
            z = z1[l][a, :] - d1[l][a, :] + links(d1, l, s, WIDE)
            z2[l][a, :] = z
            d2[l][a, :] = A2 * d1[l][a, :] + B2 * z

    each_chunk(H, total, second, WIDE)
    leaving += give(d21, z21)

    def third(s):
        a = pl.ds(s, STEP)
        o = pl.ds(pl.multiple_of(s - PAD, 8), STEP)
        nb = weighted(e20, s, STEP, gx[0], gy[0])[:, main]
        nb = inv[0][a, main] * (nb + viae[0][a, main] * d21[a, main])
        d = e20[a, main]
        z = z20[a, main] - d + nb
        d20[o, :] = d
        sb0[o, :] = ev[0][a, main] + d00[a, main] + d10[a, main] + (1.0 + A3) * d + B3 * z

    each_chunk(PAD, rows, third, STEP)
    leaving += give(d20, sb0)
    wait(leaving)


def pack_side(side, msg, row, total):
    for j in range(-(-total // W)):
        t = side[W * j : W * j + W, :].T
        msg[row + 8 * j : row + 8 * j + Q, :] = t[0:Q]
        msg[row + 8 * j + Q : row + 8 * j + 2 * Q, :] = t[W - Q : W]


def unpack_side(msg, row, total, u):
    blocks = []
    for j in range(-(-total // W)):
        u[0:Q, :] = msg[row + 8 * j : row + 8 * j + Q, :]
        u[W - Q : W, :] = msg[row + 8 * j + Q : row + 8 * j + 2 * Q, :]
        blocks.append((H + W * j, min(W, total - W * j), u[...].T))
    return blocks


def first_top_kernel(part, *refs):
    inputs, (d_hbm, z_hbm, delta_hbm, msg), held = refs[:8], refs[8:12], refs[12:20]
    low, d0, v3, gx, gy, inv, via, bond = held
    d_out, z_out, delta, ep, side, u, part_held, sems = refs[20:]
    copies = Copies(sems)
    [came] = copies.start((part, part_held))
    part = part_held
    arriving = copies.start(*zip(inputs, held))
    rows = part.shape[0] - 3 * (2 * H + 8 * (side.shape[0] // W))
    total = rows + 2 * H
    sides = 8 * (side.shape[0] // W)
    main, edge = slice(0, W), slice(W, 2 * W)
    u[...] = jnp.zeros_like(u)
    came.wait()
    row = total + sides
    own = unpack_side(part, row + 2 * H, total, u)
    others = unpack_side(part, row + 2 * H + sides + 2 * H, total, u)
    theirs = unpack_side(part, total, total, u)
    wait(arriving)
    delta[PAD : PAD + rows, main] = jnp.zeros((rows, W), F32)
    ep[PAD : PAD + rows, main] = part[H : H + rows, :]

    def halo(a, cols, v_part, weight_part, d_part):
        x = inv[a, cols] * bond[a, cols] * v_part
        delta[a, cols] = x
        d0[a, cols] = d0[a, cols] + x
        ep[a, cols] = d_part + weight_part * v3[a, cols]

    for k, first in ((0, H), (1, PAD + rows)):
        at = row + H * k
        halo(
            slice(first, first + H), main, part[at : at + H, :],
            part[at + 2 * H + sides : at + 3 * H + sides, :], part[first - H : first, :],
        )
    for (first, n, a), (_, _, b), (_, _, c) in zip(own, others, theirs):
        halo(slice(first, first + n), edge, a[:n], b[:n], c[:n])

    def body(s):
        a = pl.ds(s, LONG)
        r = pl.ds(pl.multiple_of(s - H, 8), LONG)
        nb = weighted(d0, s, LONG, gx, gy) + via[a, :] * low[a, :] + bond[a, :] * ep[a, :]
        x = inv[a, :] * nb
        d = A1 * d0[a, :] + B1 * x
        z_out[a, :] = x
        d_out[a, :] = d
        side[r, :] = d[:, W:]
        msg[r, :] = d[:, :W]

    each_chunk(H, total, body, LONG)
    leaving = copies.start((d_out, d_hbm), (z_out, z_hbm), (delta, delta_hbm))
    pack_side(side, msg, total, total)
    wait(leaving)


def second_top_kernel(low, inv_low, delta, here, z, part, gx, gy, inv, via, bond, d_out, z_out, msg, weight, ep, u):
    rows = msg.shape[0]
    total = rows + 2 * H
    u[...] = jnp.zeros_like(u)
    for first, n, x in unpack_side(part, total, total, u):
        ep[first : first + n, :] = x[:n]

    def body(s):
        a = pl.ds(s, WIDE)
        r = pl.ds(pl.multiple_of(s - H, 8), WIDE)
        other = jnp.concatenate([part[r, :], ep[a, :]], axis=1)
        under = low[a, :] + B1 * inv_low[a, :] * via[a, :] * delta[a, :]
        nb = weighted(here, s, WIDE, gx, gy) + via[a, :] * under + bond[a, :] * other
        c = here[a, :]
        x = z[a, :] - c + inv[a, :] * nb
        z_out[a, :] = x
        d_out[a, :] = A2 * c + B2 * x

    each_chunk(H, total, body, WIDE)
    msg[...] = d_out[PAD : PAD + rows, 0:W]
    weight[...] = inv[PAD : PAD + rows, 0:W] * bond[PAD : PAD + rows, 0:W]


def final_kernel(
    v0, vd0, d11, b12, z12, e11, d13, d20, b21, e21, d23, z21, ze21, z23, delta,
    gx1, gx2, gx3, gy1, gy2, gy3, inv1, inv2, inv3, via0, via1, via2,
    out, d22, z22, d21, d12,
):
    main = slice(0, W)
    rows = out.shape[1]

    def amend(s):
        a = pl.ds(s, WIDE)
        c = inv2[a, :] * via2[a, :] * delta[a, :]
        z22[a, :] = z12[a, :] + c
        c = B1 * c
        d12[a, :] = b12[a, :] + c
        d21[a, :] = b21[a, :] + e21[a, :] + B2 * inv1[a, :] * via1[a, :] * c

    each_chunk(H, rows + 2 * H, amend, WIDE)

    def middle(s):
        a = pl.ds(s, WIDE)
        this = d12[a, :]
        nb = weighted(d12, s, WIDE, gx2, gy2)
        nb = nb + via1[a, :] * (d11[a, :] + e11[a, :]) + via2[a, :] * d13[a, :]
        z = z22[a, :] - this + inv2[a, :] * nb
        z22[a, :] = z
        d22[a, :] = A2 * this + B2 * z

    each_chunk(H, rows + 2 * H, middle, WIDE)
    gx, gy, inv = [None, gx1, gx2, gx3], [None, gy1, gy2, gy3], [None, inv1, inv2, inv3]
    via = [via0, via1, via2]
    d2, z2 = [None, d21, d22, d23], [None, None, z22, z23]

    def body(i):
        s = pl.multiple_of(i + PAD, 8)
        a, o = pl.ds(s, STEP), pl.ds(i, STEP)
        out[0, o, :] = v0[o, :]
        first = [None, d11[a, main] + e11[a, main], d12[a, main], d13[a, main]]
        below = d20[o, :]
        for l in range(1, 4):
            nb = weighted(d2[l], s, STEP, gx[l], gy[l])[:, main]
            nb = nb + via[l - 1][a, main] * below
            below = d2[l][a, main]
            if l < 3:
                nb = nb + via[l][a, main] * d2[l + 1][a, main]
            z = (z21[a, main] + ze21[o, :] if l == 1 else z2[l][a, main]) - below + inv[l][a, main] * nb
            out[l, o, :] = vd0[l - 1, o, :] + first[l] + (1.0 + A3) * below + B3 * z

    each_chunk(0, rows, body, STEP)


def map_kernel(arrived, out, first, last, labels, vec, lab, a0, a1, a2, a3, sem):
    devices = vec.shape[1]
    rows = out.shape[0]
    slots = arrived[pl.ds(CAP * 8, devices, stride=ROWS_MSG), :]
    vec[...] = slots.T[0:8].astype(jnp.int32)
    copy = pltpu.make_async_copy(vec, lab, sem)
    copy.start()
    parts = (a0, a1, a2, a3)
    for acc in parts:
        acc[...] = jnp.zeros_like(acc)
    copy.wait()

    @pl.loop(0, devices // 8, unroll=4)
    def _(g):
        n = ROWS_MSG * 8
        data = arrived[pl.ds(pl.multiple_of(g * n, 8), n), :]
        for j in range(8):
            for r in range(CAP):
                slot = lab[r, g * 8 + j]
                labels[(g * 8 + j) * CAP + r] = slot
                a = pl.ds(pl.multiple_of(slot * 8, 8), 8)
                acc = parts[(j * CAP + r) % 4]
                acc[a, :] += data[j * ROWS_MSG + r * 8 : j * ROWS_MSG + r * 8 + 8]

    out[...] = (a0[0:rows, :] + a1[0:rows, :]) + (a2[0:rows, :] + a3[0:rows, :])
    first[...] = out[0:8, :]
    last[...] = out[rows - 8 : rows, :]


def edges_kernel(cur, lo, hi, to_left, to_right, ext):
    rows = cur.shape[0]
    ext[0:H, :] = lo[...]
    ext[H : H + rows, :] = cur[...]
    ext[H + rows : rows + 2 * H, :] = hi[...]
    for j in range(to_left.shape[1] // W):
        t = ext[W * j : W * j + W, :].T
        to_left[:, W * j : W * j + W] = t[0:8]
        to_right[:, W * j : W * j + W] = t[W - 8 : W]


def effect_kernel(
    labels, cur, lo, hi, f_left, f_right, *refs
):
    (inv0, gx0, gy0, via0, inv1, gx1, gy1, sb0, d20), refs = refs[:9], refs[9:]
    v0_out, picked_out, e11_out, e21_out, z21_out, d20_out = refs[:6]
    ec, e0, e1, z10, z11, e2, z20, e11, e21, u, acc, z21, d20_sum, picked, sems = refs[6:]
    copies = Copies(sems)
    rows = cur.shape[0]
    total = rows + 2 * H
    main, edge = slice(0, W), slice(W, 2 * W)
    ec[H : 2 * H, main] = lo[...]
    ec[PAD : PAD + rows, main] = cur[...]
    ec[PAD + rows : PAD + rows + H, main] = hi[...]
    u[...] = jnp.zeros_like(u)
    for j in range(f_left.shape[1] // W):
        u[0:8, :] = f_right[:, W * j : W * j + W]
        u[W - 8 : W, :] = f_left[:, W * j : W * j + W]
        n = min(W, total - W * j)
        ec[H + W * j : H + W * j + n, edge] = u[...].T[:n]

    def zeroth(s):
        a = pl.ds(s, LONG)
        e0[a, :] = inv0[a, :] * ec[a, :]

    each_chunk(H, total, zeroth, LONG)
    def first(s):
        a = pl.ds(s, LONG)
        here = e0[a, :]
        z = inv0[a, :] * weighted(e0, s, LONG, gx0, gy0)
        z10[a, :] = z
        e1[a, :] = A1 * here + B1 * z
        z = inv1[a, :] * via0[a, :] * here
        z11[a, :] = z
        e11[a, :] = B1 * z

    each_chunk(H, total, first, LONG)
    def second(s):
        a = pl.ds(s, LONG)
        low, high, between = e1[a, :], e11[a, :], via0[a, :]
        nb = weighted(e1, s, LONG, gx0, gy0) + between * high
        z = z10[a, :] - low + inv0[a, :] * nb
        z20[a, :] = z
        e2[a, :] = A2 * low + B2 * z
        nb = weighted(e11, s, LONG, gx1, gy1) + between * low
        z = z11[a, :] - high + inv1[a, :] * nb
        z11[a, :] = z
        e21[a, :] = A2 * high + B2 * z

    each_chunk(H, total, second, LONG)
    copies.start((e11, e11_out), (e21, e21_out))
    def third(i):
        s = pl.multiple_of(i + PAD, 8)
        a, o = pl.ds(s, STEP), pl.ds(i, STEP)
        here = e2[a, main]
        nb = weighted(e2, s, STEP, gx0, gy0)[:, main] + via0[a, main] * e21[a, main]
        z = z20[a, main] - here + inv0[a, main] * nb
        whole = sb0[o, :] + e0[a, main] + e1[a, main] + (1.0 + A3) * here + B3 * z
        acc[o, :] = whole
        d20_sum[o, :] = d20[o, :] + here
        z21[o, :] = z11[a, main]

    each_chunk(0, rows, third, STEP)
    copies.start((acc.at[pl.ds(0, rows), :], v0_out), (z21, z21_out), (d20_sum, d20_out))
    acc[rows : rows + 8, :] = jnp.zeros((8, W), F32)

    def pick(k):
        picked[pl.ds(pl.multiple_of(k * 8, 8), 8), :] = acc[
            pl.ds(pl.multiple_of(labels[k] * 8, 8), 8), :
        ]

    count = labels.shape[0] // 4
    for part in range(4):
        pl.loop(part * count, (part + 1) * count, unroll=8)(pick)
        a = pl.ds(part * count * 8, count * 8)
        copies.start((picked.at[a, :], picked_out.at[a, :]))
    wait(copies.made)


def last_kernel(dest, back, field, part, weight, out, top):
    top[0] = field[0] + B3 * weight[...] * part[...]

    @pl.loop(0, out.shape[0], unroll=16)
    def _(k):
        out[k] = back[pl.ds(pl.multiple_of(dest[k] * 8, 8), 8), :]


def ring(axis, step):
    n = lax.axis_size(axis)
    return [(i, (i + step) % n) for i in range(n)]


def shift(x, axis, step):
    return lax.ppermute(x, axis, ring(axis, step))


def facing(x, step=0):
    n, m = lax.axis_size("gx"), lax.axis_size("yt")
    pairs = [
        (g * m + t, ((g + step) % n) * m + (t ^ (m // 2))) for g in range(n) for t in range(m)
    ]
    return lax.ppermute(x, ALL, pairs)


def on_device(v, st, cx, cy, via, mask, blocks, owner, slot):
    layers, rows, cols = v.shape
    devices = lax.axis_size("gx") * lax.axis_size("yt")
    nb = blocks.shape[0]
    total = rows + 2 * H
    nr = total + 2 * H
    side_blocks = -(-total // W)
    place = jnp.stack(
        [
            lax.axis_index("gx") * rows,
            jnp.int32(rows * lax.axis_size("gx")),
            lax.axis_index("yt") * cols,
            jnp.int32(cols * lax.axis_size("yt")),
        ]
    ).astype(jnp.int32)

    outgoing, dest, v_top = call(
        send_kernel,
        [
            pltpu.HBM((devices * ROWS_MSG, W), F32),
            jax.ShapeDtypeStruct((nb,), jnp.int32),
            pltpu.HBM((rows + TAIL, W), F32),
        ],
        [owner.reshape(nb), slot, blocks, v],
        scratch=[
            pltpu.SMEM((devices,), jnp.int32),
            pltpu.VMEM((devices * CAP * 8, W), F32),
            pltpu.VMEM((devices, W), jnp.int32),
            pltpu.VMEM((devices * ROWS_MSG, W), F32),
            pltpu.VMEM((rows + TAIL, W), F32),
            pltpu.SemaphoreType.DMA((6,)),
        ],
        specs={0: SMEM, 1: SMEM, 3: ANY},
        out_specs=[ANY, SMEM, ANY],
        far=(3,),
    )
    sources = [v, cx, cy, st, via]
    args = sources + [mask] + sources + [mask]
    specs = {}
    last = rows // 8 - 1
    for i in range(5):
        n = sources[i].shape[0]
        specs[i] = pl.BlockSpec((n, 8, W), lambda _: (0, 0, 0))
        specs[6 + i] = pl.BlockSpec((n, 8, W), lambda _: (0, last, 0))
    specs[5] = pl.BlockSpec((8, W), lambda _: (0, 0))
    specs[11] = pl.BlockSpec((8, W), lambda _: (last, 0))
    count = 5 * layers
    first_rows, last_rows = pl.pallas_call(
        pack_x_kernel,
        grid=(1,),
        out_shape=[shape(count, 8, W)] * 2,
        in_specs=[specs[i] for i in range(12)],
        out_specs=[
            pl.BlockSpec((count, 8, W), lambda _: (0, 0, 0)),
            pl.BlockSpec((count, 8, W), lambda _: (0, 0, 0)),
        ],
        name="pack_x_kernel",
        compiler_params=pltpu.CompilerParams(vmem_limit_bytes=58 << 20),
        cost_estimate=pl.CostEstimate(flops=1, bytes_accessed=1_000_000, transcendentals=0),
    )(*args)
    lo = shift(last_rows, "gx", 1)
    hi = shift(first_rows, "gx", -1)
    lo, hi, v_top, outgoing = lax.optimization_barrier((lo, hi, v_top, outgoing))
    v_part = facing(v_top)
    tiles = [v, cx, cy, st, via, mask]
    to_left, to_right = call(
        pack_y_kernel, [shape(total, W), shape(total, W)], [*tiles, lo, hi], vmem=8
    )
    f_left = shift(to_right, "yt", 1)
    f_right = shift(to_left, "yt", -1)
    outgoing, f_left, f_right, v_part = lax.optimization_barrier(
        (outgoing, f_left, f_right, v_part)
    )
    arrived = lax.all_to_all(
        outgoing.reshape(devices, ROWS_MSG, 1, W), ALL, 0, 0, tiled=True
    ).reshape(devices * ROWS_MSG, W)

    one = shape(nr, 2 * W)
    tile = shape(rows, W)
    buffer = lambda *d: pltpu.VMEM(d, F32)
    msg_shape = shape(total + 8 * side_blocks, W)
    held = [one] * (4 * layers + 5)
    msg0_shape = shape(3 * (total + 8 * side_blocks) - 2 * rows, W)
    held += [tile, one, one, tile, shape(layers - 1, rows, W), msg0_shape]
    outs = call(
        base_kernel,
        [*held, one],
        [place, *tiles, v_part, lo, hi, f_left, f_right],
        scratch=[buffer(*h.shape) for h in held]
        + [buffer(nr, 2 * W)] * (4 * layers + 1)
        + [buffer(side_blocks * W, W)]
        + [buffer(nr, 2 * W)] * 7
        + [pltpu.SemaphoreType.DMA((9 * layers + 20,))],
        specs={0: SMEM, 1: ANY, 2: ANY, 3: ANY, 4: ANY, 5: ANY, 7: ANY},
        out_specs=[ANY] * (len(held) + 1),
        vmem=VMEM_BASE,
        cost=20_000_000,
    )
    gx, gy, inv, via_e = outs[0:4], outs[4:8], outs[8:12], outs[12:15]
    bond, d02, d03, d11, d12, z12, d20, d21, z21, sb0, vd0, msg0, v3 = outs[15:]
    part0 = facing(msg0)

    cur, cur_first, cur_last, labels = call(
        map_kernel,
        [tile, shape(8, W), shape(8, W), jax.ShapeDtypeStruct((devices * CAP,), jnp.int32)],
        [arrived],
        scratch=[
            pltpu.VMEM((8, devices), jnp.int32),
            pltpu.SMEM((8, devices), jnp.int32),
            *[buffer(rows + 8, W)] * 4,
            pltpu.SemaphoreType.DMA,
        ],
        out_specs=[pl.BlockSpec(memory_space=pltpu.VMEM)] * 3 + [SMEM],
    )
    cur_lo = shift(cur_last, "gx", 1)
    cur_hi = shift(cur_first, "gx", -1)
    top = [gx[3], gy[3], inv[3], via_e[2], bond]
    cur_left, cur_right = call(
        edges_kernel,
        [shape(8, side_blocks * W)] * 2,
        [cur, cur_lo, cur_hi],
        scratch=[buffer(side_blocks * W, W)],
    )
    labels, part0 = lax.optimization_barrier((labels, part0))
    far_one = pltpu.HBM((nr, 2 * W), F32)
    d13, z13, delta, msg1 = call(
        first_top_kernel,
        [far_one, far_one, far_one, msg_shape],
        [part0, d02, d03, v3, *top],
        scratch=[buffer(nr, 2 * W)] * 12
        + [buffer(side_blocks * W, W), buffer(W, W), buffer(*msg0_shape.shape)]
        + [pltpu.SemaphoreType.DMA((12,))],
        specs={i: ANY for i in range(9)},
        out_specs=[ANY] * 3 + [pl.BlockSpec(memory_space=pltpu.VMEM)],
        vmem=VMEM_TOP,
        far=range(9),
    )
    cur_left, cur_right, msg1 = lax.optimization_barrier((cur_left, cur_right, msg1))
    part1 = facing(msg1)
    d23, z23, msg2, weight = call(
        second_top_kernel,
        [one, one, tile, tile],
        [d12, inv[2], delta, d13, z13, part1, *top],
        scratch=[buffer(nr, W), buffer(W, W)],
        vmem=VMEM_FINAL,
    )

    cur_f_left = shift(cur_right, "yt", 1)
    cur_f_right = shift(cur_left, "yt", -1)
    v0, picked, e11, e21, ze21, d20 = call(
        effect_kernel,
        [pltpu.HBM(d, F32) for d in (
            (rows, W), (devices * CAP * 8, W), (nr, 2 * W), (nr, 2 * W), (rows, W), (rows, W))],
        [labels, cur, cur_lo, cur_hi, cur_f_left, cur_f_right,
         inv[0], gx[0], gy[0], via_e[0], inv[1], gx[1], gy[1], sb0, d20],
        scratch=[buffer(nr, 2 * W)] * 9
        + [buffer(W, W), buffer(rows + 8, W), buffer(rows, W), buffer(rows, W)]
        + [buffer(devices * CAP * 8, W), pltpu.SemaphoreType.DMA((9,))],
        specs={0: SMEM},
        out_specs=[ANY] * 6,
        vmem=VMEM_EFFECT,
    )
    picked, part1 = lax.optimization_barrier((picked, part1))
    part2 = facing(msg2)
    back = lax.all_to_all(picked, ALL, 0, 0, tiled=True)

    voltage = call(
        final_kernel,
        shape(layers, rows, W),
        [v0, vd0, d11, d12, z12, e11, d13, d20, d21, e21, d23, z21, ze21, z23, delta,
         *gx[1:], *gy[1:], *inv[1:], *via_e],
        scratch=[buffer(nr, 2 * W)] * 4,
        vmem=VMEM_FINAL,
        cost=10_000_000,
    )
    whole = pl.BlockSpec(memory_space=pltpu.VMEM)
    upper = pl.BlockSpec((1, rows, W), lambda _: (layers - 1, 0, 0))
    block_voltage, voltage = pl.pallas_call(
        last_kernel,
        grid=(1,),
        out_shape=[shape(nb, 8, W), shape(layers, rows, W)],
        in_specs=[SMEM, whole, upper, whole, whole],
        out_specs=[whole, upper],
        input_output_aliases={2: 1},
        name="last_kernel",
        compiler_params=pltpu.CompilerParams(vmem_limit_bytes=8 << 20),
    )(dest, back, voltage, part2, weight)
    return voltage, block_voltage


def solution(mesh):
    tile = P(None, "gx", "yt")
    return jax.shard_map(
        on_device,
        mesh=mesh,
        in_specs=(tile, tile, tile, tile, tile, P("gx", "yt"), P(ALL, None, None), P(ALL, None), P(ALL)),
        out_specs=(tile, P(ALL, None, None)),
        check_vma=False,
    )
```
